32 devices in a mesh: blk: 8 (over z, core), head: 4 (over y, x).
Axes of the slice: x: 2, y: 2, z: 4, core: 2. Of those that a mesh axis runs over, the one named last changes fastest.
Arguments:
- inputs: bfloat16 [4096, 1024], P(('blk', 'head')), may hold values from -6 to 6
- token_place: int32 [4096], replicated, may hold values from 0 to 4095, as said below
- lengths: int32 [4], replicated, may hold values from 256 to 2048, as said below
- w_norm1: float32 [1024], replicated, may hold values from 0.1 to 1.9
- w_query: bfloat16 [1024, 1024], P('blk', 'head'), may hold values from -0.1875 to 0.1875
- key_weight: bfloat16 [1024, 512], P('blk', 'head'), may hold values from -0.1875 to 0.1875
- value_weight: bfloat16 [1024, 512], P('blk', 'head'), may hold values from -0.1875 to 0.1875
- w_out: bfloat16 [1024, 1024], P('head', 'blk'), may hold values from -0.75 to 0.75
- w_norm2: float32 [1024], replicated, may hold values from 0.1 to 1.9
- router: bfloat16 [1024, 32], replicated, may hold values from -0.09375 to 0.09375
- routes: int32 [4096, 8], P(('blk', 'head')), may hold values from 0 to 31, all different within a row
- slot_order: int32 [4096, 8], P(('blk', 'head')), may hold values from 0 to 1023, as said below
- w_gate: bfloat16 [32, 1024, 512], P('head', 'blk'), may hold values from -0.1875 to 0.1875
- w_up: bfloat16 [32, 1024, 512], P('head', 'blk'), may hold values from -0.1875 to 0.1875
- w_down: bfloat16 [32, 512, 1024], P('head', None, 'blk'), may hold values from -1 to 1
- grad_out: bfloat16 [4096, 1024], P(('blk', 'head')), may hold values from -6 to 6
Outputs:
- output: bfloat16 [4096, 1024], P(('blk', 'head'))
- grad_inputs: float32 [4096, 1024], P(('blk', 'head'))
- grad_norm1: float32 [1024], replicated
- grad_query: float32 [1024, 1024], P('blk', 'head')
- grad_key: float32 [1024, 512], P('blk', 'head')
- grad_value: float32 [1024, 512], P('blk', 'head')
- grad_w_out: float32 [1024, 1024], P('head', 'blk')
- grad_norm2: float32 [1024], replicated
- grad_router: float32 [1024, 32], replicated
- grad_gate: float32 [32, 1024, 512], P('head', 'blk')
- grad_up: float32 [32, 1024, 512], P('head', 'blk')
- grad_down: float32 [32, 512, 1024], P('head', None, 'blk')
The draws below stay inside these ranges and needn't reach their ends.
Inputs may be any that keep to these rules, and one draw needn't show every extreme that they name: `token_place`: A permutation. With the stream cut into blocks of 256 places, the p-th aligned group of 512 rows holds, in some order, blocks p and 15 - p. `lengths`: the sequences fill the 4096 places in order; the first or the last has 2048 places, the others 4096/16 or more, one of them exactly that. `routes`: each row names 8 different experts. `slot_order`: each aligned block of 128 rows holds every number of 0 to 1023 once.
All inputs are finite; a program needn't handle non-finite values.
Results may differ from the reference program's by a relative error of at most 0.025.
Values may be sent and summed in bfloat16 or wider, within the bound.
A program may use at most 192 MiB of HBM per device.

```python
import math
import jax
import jax.numpy as jnp
from jax import lax

MODEL_WIDTH = 1024
QUERY_HEADS = 16
KEY_VALUE_HEADS = 8
HEAD_SIZE = 64
E = 32
TOPK = 8
F = 512
TOK_DEV = 128
GROUP = 512
STREAM_TOKENS = 4096
CAP = 40


def draw_token_place(key, part):
    key = jax.random.fold_in(key, 11)
    block_list = STREAM_TOKENS // GROUP
    half = GROUP // 2
    owner = jnp.arange(block_list, dtype=jnp.int32)[:, None]
    column = jnp.arange(GROUP, dtype=jnp.int32)[None, :]
    base = jnp.where(column < half, owner * half + column, (2 * block_list - 1 - owner) * half + column - half)

    def shuffle(single):
        return jax.random.permutation(single, GROUP)
    orders = jax.vmap(shuffle)(jax.random.split(key, block_list)).astype(jnp.int32)
    return jnp.take_along_axis(base, orders, axis=1).reshape(STREAM_TOKENS).astype(jnp.int32)


def draw_lengths(key, part):
    key = jax.random.fold_in(key, 12)
    parts_keys = jax.random.split(key, 3)
    least = STREAM_TOKENS // 16
    spare = STREAM_TOKENS // 2 - 3 * least
    cut = jax.random.randint(parts_keys[0], (), 0, spare + 1, dtype=jnp.int32)
    shorts = least + jnp.stack([jnp.zeros((), jnp.int32), cut, spare - cut]).astype(jnp.int32)
    shorts = shorts[jax.random.permutation(parts_keys[1], 3)]
    longest = jnp.full((1,), STREAM_TOKENS // 2, jnp.int32)
    front = jax.random.randint(parts_keys[2], (), 0, 2, dtype=jnp.int32)
    return jnp.where(front == 0, jnp.concatenate([longest, shorts]), jnp.concatenate([shorts, longest])).astype(jnp.int32)


def draw_slot_order(key, part):
    key = jax.random.fold_in(key, 13)
    block_list = STREAM_TOKENS // TOK_DEV

    def shuffle(single):
        return jax.random.permutation(single, TOK_DEV * TOPK)
    orders = jax.vmap(shuffle)(jax.random.split(key, block_list))
    return orders.reshape(STREAM_TOKENS, TOPK).astype(jnp.int32)


def block_levels(own_key, dims, cuts, smallest, top_value):
    level = 1.0
    for dim, blocks in cuts:
        steps = jax.random.uniform(jax.random.fold_in(jax.random.fold_in(own_key, 6), dim), (blocks,), jnp.float32, smallest / len(cuts), top_value / len(cuts))
        level = level * jnp.repeat(jnp.exp(steps), dims[dim] // blocks).reshape((-1,) + (1,) * (len(dims) - 1 - dim))
    return level


def different_ones(key, rows, amount, top, lift):
    sequence = jax.random.permutation(jax.random.fold_in(key, 1), amount)
    favour = sequence
    for power in range(3):
        favour = favour * favour // amount
    favour = favour * lift // amount
    tickets = jax.random.randint(jax.random.fold_in(key, 2), (rows, amount), 0, 4096) + favour
    sure = jax.random.permutation(jax.random.fold_in(key, 3), rows)[jnp.arange(amount) % rows]
    tickets = jnp.where(jnp.arange(rows)[:, None] == sure[None, :], 1 << 14, tickets)
    priority = tickets * amount + jnp.arange(amount)
    return lax.top_k(priority.astype(jnp.int32), top)[1].astype(jnp.int32)


def centred(rng, extent, deviation, most, cuts=(), kind=jnp.bfloat16):
    level = block_levels(rng, extent, cuts, -0.22, 0.18) if cuts else 1.0
    array = jax.random.normal(rng, extent, jnp.float32) * deviation * level
    return jnp.minimum(jnp.maximum(array, -most), most).astype(kind)


def setup_inputs(seed: int = 0) -> dict:
    seeds = jax.random.split(jax.random.key(seed), 17)
    inputs = centred(seeds[0], (STREAM_TOKENS, MODEL_WIDTH), 1.0, 6.0, ((0, 32),))
    token_place = draw_token_place(jax.random.fold_in(seeds[16], 71), 0)
    lengths = draw_lengths(jax.random.fold_in(seeds[16], 71), 0)
    w_norm1 = jnp.clip(1.0 + 0.18 * jax.random.normal(seeds[3], (MODEL_WIDTH,), jnp.float32), 0.1, 1.9)
    w_query = centred(seeds[4], (MODEL_WIDTH, QUERY_HEADS * HEAD_SIZE), MODEL_WIDTH ** -0.5, 0.1875, ((0, 8), (1, 4)))
    key_weight = centred(seeds[5], (MODEL_WIDTH, KEY_VALUE_HEADS * HEAD_SIZE), MODEL_WIDTH ** -0.5, 0.1875, ((0, 8), (1, 4)))
    value_weight = centred(seeds[6], (MODEL_WIDTH, KEY_VALUE_HEADS * HEAD_SIZE), MODEL_WIDTH ** -0.5, 0.1875, ((0, 8), (1, 4)))
    w_out = centred(seeds[7], (QUERY_HEADS * HEAD_SIZE, MODEL_WIDTH), (QUERY_HEADS * HEAD_SIZE // 16) ** -0.5, 0.75, ((0, 4), (1, 8)))
    w_norm2 = jnp.clip(1.0 + 0.18 * jax.random.normal(seeds[8], (MODEL_WIDTH,), jnp.float32), 0.1, 1.9)
    router = centred(seeds[9], (MODEL_WIDTH, E), (4 * MODEL_WIDTH) ** -0.5, 0.09375)
    routes = different_ones(seeds[10], STREAM_TOKENS, E, TOPK, 2048)
    slot_order = draw_slot_order(jax.random.fold_in(seeds[16], 71), 0)
    w_gate = centred(seeds[12], (E, MODEL_WIDTH, F), MODEL_WIDTH ** -0.5, 0.1875, ((0, 4), (1, 8)))
    w_up = centred(seeds[13], (E, MODEL_WIDTH, F), MODEL_WIDTH ** -0.5, 0.1875, ((0, 4), (1, 8)))
    w_down = centred(seeds[14], (E, F, MODEL_WIDTH), (F // 16) ** -0.5, 1.0, ((0, 4), (2, 8)))
    grad_out = centred(seeds[15], (STREAM_TOKENS, MODEL_WIDTH), 1.0, 6.0, ((0, 32),))
    return {"inputs": inputs, "token_place": token_place, "lengths": lengths, "w_norm1": w_norm1, "w_query": w_query, "key_weight": key_weight, "value_weight": value_weight, "w_out": w_out, "w_norm2": w_norm2, "router": router, "routes": routes, "slot_order": slot_order, "w_gate": w_gate, "w_up": w_up, "w_down": w_down, "grad_out": grad_out}


eps = 1e-06
rope_base = 10000.0
query_row_block = 128
highest = lax.Precision.HIGHEST

@jax.custom_vjp
def lower_bound(v):
    return lax.optimization_barrier(v.astype(jnp.bfloat16)).astype(jnp.float32)

@jax.custom_vjp
def lower_bound_back(v):
    return v

def low_keep(v):
    return (lower_bound(v), None)

def low_pass(kept, grad):
    return (grad,)

def back_keep(v):
    return (v, None)

def back_low(kept, grad):
    return (lower_bound(grad),)
lower_bound.defvjp(low_keep, low_pass)
lower_bound_back.defvjp(back_keep, back_low)

def seq_begin(token_position, lengths):
    starts = (jnp.cumsum(lengths) - lengths).astype(jnp.int32)
    inside = token_position[:, None] >= starts[None, 1:]
    return lax.optimization_barrier(jnp.sum(jnp.where(inside, lengths[None, :-1], 0), axis=1)).astype(jnp.int32)

def rotation(token_position, begin_index, width):
    half = width // 2
    freq = jnp.exp(jnp.arange(half, dtype=jnp.float32) * (-2.0 * math.log(rope_base) / width))
    angle = (token_position - begin_index).astype(jnp.float32)[:, None] * freq[None, :]
    return (jnp.cos(angle)[:, None, :], jnp.sin(angle)[:, None, :])

def turn_index(values, cosine_table, sine_table):
    half = values.shape[-1] // 2
    leading = values[..., :half]
    trailing = values[..., half:]
    return jnp.concatenate([leading * cosine_table - trailing * sine_table, trailing * cosine_table + leading * sine_table], axis=-1)

def rms_norm(values, gain):
    factor = lax.rsqrt(lax.optimization_barrier(jnp.mean(values * values, axis=-1, keepdims=True)) + eps)
    return values * factor * gain

def slot_numbers(routes, slot_order):
    flat_expert = routes.reshape(-1).astype(jnp.int32)
    rank = slot_order.reshape(-1).astype(jnp.int32)
    count = flat_expert.shape[0]
    by_rank = jnp.zeros((count,), jnp.int32).at[rank].set(jnp.arange(count, dtype=jnp.int32))
    expert_sorted = flat_expert[by_rank]
    onehot = (expert_sorted[:, None] == jnp.arange(E, dtype=jnp.int32)[None, :]).astype(jnp.int32)
    before = (jnp.cumsum(onehot, axis=0) - onehot).astype(jnp.int32)
    slot_sorted = lax.optimization_barrier(jnp.sum(before * onehot, axis=1)).astype(jnp.int32)
    slot = slot_sorted[rank].reshape(routes.shape)
    return (slot, slot < CAP)

def attention_output(rotated_query, rotated_key, value_rows, token_position, begin_index):
    head_groups = QUERY_HEADS // KEY_VALUE_HEADS
    scale = 1.0 / math.sqrt(HEAD_SIZE)
    block_list = STREAM_TOKENS // query_row_block
    query_block_list = rotated_query.reshape(block_list, query_row_block, KEY_VALUE_HEADS, head_groups, HEAD_SIZE)

    def one_block(pieces):
        query_block, place_block, begin_block = pieces
        scores = jnp.einsum('qhgd,khd->hgqk', query_block, rotated_key, precision=highest) * scale
        allowed = (token_position[None, :] <= place_block[:, None]) & (token_position[None, :] >= begin_block[:, None])
        scores = lower_bound_back(jnp.where(allowed, scores, -1e+30))
        shifted = jnp.exp(scores - lax.optimization_barrier(jnp.max(scores, axis=-1, keepdims=True)))
        probs = lower_bound(shifted / lax.optimization_barrier(jnp.sum(shifted, axis=-1, keepdims=True)))
        result = jnp.einsum('hgqk,khd->qhgd', probs, value_rows, precision=highest)
        return result.reshape(query_row_block, QUERY_HEADS * HEAD_SIZE)
    result = lax.map(jax.checkpoint(one_block), (query_block_list, token_position.reshape(block_list, query_row_block), begin_index.reshape(block_list, query_row_block)))
    return result.reshape(STREAM_TOKENS, QUERY_HEADS * HEAD_SIZE)

def expert_block(normed, routes, slot_order, router, w_gate, w_up, w_down):
    logits = jnp.dot(normed, router, precision=highest)
    chosen = jnp.take_along_axis(logits, routes, axis=1)
    shifted = jnp.exp(chosen - lax.optimization_barrier(jnp.max(chosen, axis=-1, keepdims=True)))
    gates = shifted / lax.optimization_barrier(jnp.sum(shifted, axis=-1, keepdims=True))
    slot, kept = slot_numbers(routes, slot_order)
    target = jnp.where(kept, routes * CAP + slot, E * CAP).reshape(-1).astype(jnp.int32)
    pairs = jnp.repeat(normed, TOPK, axis=0)
    buffer = jnp.zeros((E * CAP, MODEL_WIDTH), normed.dtype).at[target].add(pairs, mode='drop')
    buffer = lower_bound_back(buffer).reshape(E, CAP, MODEL_WIDTH)
    gate_pre = lower_bound_back(jnp.einsum('ecd,edf->ecf', buffer, w_gate, precision=highest))
    up_pre = lower_bound_back(jnp.einsum('ecd,edf->ecf', buffer, w_up, precision=highest))
    activated = lower_bound(gate_pre * jax.nn.sigmoid(gate_pre) * up_pre)
    expert_out = lower_bound(lower_bound_back(jnp.einsum('ecf,efd->ecd', activated, w_down, precision=highest)))
    picked = jnp.take(expert_out.reshape(E * CAP, MODEL_WIDTH), target, axis=0, mode='fill', fill_value=0.0)
    picked = picked.reshape(-1, TOPK, MODEL_WIDTH)
    return lax.optimization_barrier(jnp.sum(gates[..., None] * picked, axis=1))

def layer(inputs, w_norm1, w_query, key_weight, value_weight, w_out, w_norm2, router, w_gate, w_up, w_down, token_position, begin_index, routes, slot_order):
    normed = lower_bound(rms_norm(inputs, w_norm1))
    query = lower_bound_back(jnp.dot(normed, w_query, precision=highest))
    key = lower_bound_back(jnp.dot(normed, key_weight, precision=highest))
    value_rows = lower_bound(lower_bound_back(jnp.dot(normed, value_weight, precision=highest)))
    cosine_table, sine_table = rotation(token_position, begin_index, HEAD_SIZE)
    rotated_query = lower_bound(turn_index(query.reshape(STREAM_TOKENS, QUERY_HEADS, HEAD_SIZE), cosine_table, sine_table))
    rotated_key = lower_bound(turn_index(key.reshape(STREAM_TOKENS, KEY_VALUE_HEADS, HEAD_SIZE), cosine_table, sine_table))
    attended_rows = lower_bound(lower_bound_back(attention_output(rotated_query, rotated_key, value_rows.reshape(STREAM_TOKENS, KEY_VALUE_HEADS, HEAD_SIZE), token_position, begin_index)))
    middle = inputs + lower_bound_back(jnp.dot(attended_rows, w_out, precision=highest))
    normed_two = lower_bound(rms_norm(middle, w_norm2))
    block_list = STREAM_TOKENS // TOK_DEV

    def per_device(pieces):
        return expert_block(pieces[0], pieces[1], pieces[2], router, w_gate, w_up, w_down)
    mixed = lax.map(jax.checkpoint(per_device), (normed_two.reshape(block_list, TOK_DEV, MODEL_WIDTH), routes.reshape(block_list, TOK_DEV, TOPK), slot_order.reshape(block_list, TOK_DEV, TOPK)))
    return middle + mixed.reshape(STREAM_TOKENS, MODEL_WIDTH)

def reference(inputs, token_place, lengths, w_norm1, w_query, key_weight, value_weight, w_out, w_norm2, router, routes, slot_order, w_gate, w_up, w_down, grad_out):
    begin_index = seq_begin(token_place, lengths)

    def forward(inputs32, norm_one, query_w, key_w, value_w, out_w, norm_two, router_w, gate_w, up_w, down_w):
        return layer(inputs32, norm_one, query_w, key_w, value_w, out_w, norm_two, router_w, gate_w, up_w, down_w, token_place, begin_index, routes, slot_order)
    floats = (inputs.astype(jnp.float32), w_norm1.astype(jnp.float32), w_query.astype(jnp.float32), key_weight.astype(jnp.float32), value_weight.astype(jnp.float32), w_out.astype(jnp.float32), w_norm2.astype(jnp.float32), router.astype(jnp.float32), w_gate.astype(jnp.float32), w_up.astype(jnp.float32), w_down.astype(jnp.float32))
    result, pullback = jax.vjp(forward, *floats)
    grads = pullback(grad_out.astype(jnp.float32))
    return (result.astype(jnp.bfloat16), grads[0], grads[1], grads[2], grads[3], grads[4], grads[5], grads[6], grads[7], grads[8], grads[9], grads[10])
```

```python
import functools
import math

import jax
import jax.numpy as jnp
from jax import lax
from jax.experimental import pallas as pl
from jax.experimental.pallas import tpu as pltpu
from jax.sharding import PartitionSpec as P

MODEL_WIDTH = 1024
HEAD_SIZE = 64
E = 32
TOPK = 8
CAP = 40
MESH = pl.DeviceIdType.MESH
VMEM = pl.BlockSpec(memory_space=pltpu.VMEM)
ANY = pl.BlockSpec(memory_space=pl.ANY)
BF = jnp.bfloat16
F32 = jnp.float32

eps = 1e-06
rope_base = 10000.0


def nn(a, b, **kw):
    return lax.dot_general(a, b, (((1,), (0,)), ((), ())), preferred_element_type=F32, **kw)


def nt(a, b, **kw):
    return lax.dot_general(a, b, (((1,), (1,)), ((), ())), preferred_element_type=F32, **kw)


def tn(a, b, **kw):
    return lax.dot_general(a, b, (((0,), (0,)), ((), ())), preferred_element_type=F32, **kw)


def remote(src, dst, send, recv, device):
    return pltpu.make_async_remote_copy(
        src_ref=src,
        dst_ref=dst,
        send_sem=send,
        recv_sem=recv,
        device_id=device,
        device_id_type=MESH,
    )


class Place:
    def __init__(self, nb, nh):
        self.nb, self.nh, self.nz = nb, nh, nb // 2
        self.b, self.h = lax.axis_index("blk"), lax.axis_index("head")
        self.z, self.core = self.b // 2, lax.rem(self.b, 2)
        self.sibling = 2 * self.z + 1 - self.core

    def in_blk(self, b):
        return (b, self.h)

    def in_head(self, h):
        return (self.b, h)

    def head_peer(self, k):
        return lax.rem(self.h + k, self.nh)

    def blk_peer(self, k):
        return lax.rem(self.b + k, self.nb)

    def meet(self):
        barrier = pltpu.get_barrier_semaphore()
        for k in range(1, self.nh):
            pl.semaphore_signal(
                barrier, inc=1, device_id=self.in_head(self.head_peer(k)), device_id_type=MESH
            )
        for k in range(1, self.nb):
            pl.semaphore_signal(
                barrier, inc=1, device_id=self.in_blk(self.blk_peer(k)), device_id_type=MESH
            )
        pl.semaphore_wait(barrier, self.nh + self.nb - 2)


class Relay:
    def __init__(self, at, buf, send, recv):
        self.at, self.buf, self.send, self.recv = at, buf, send, recv

    def copy(self, s, way, device):
        return remote(
            self.buf.at[s], self.buf.at[s], self.send.at[way, s], self.recv.at[s], device
        )

    def right(self, s):
        return self.copy(s, 0, self.at.in_blk(jnp.minimum(self.at.b + 2, self.at.nb - 2 + self.at.core)))

    def left(self, s):
        return self.copy(s, 1, self.at.in_blk(jnp.maximum(self.at.b - 2, self.at.core)))

    def across(self, s):
        return self.copy(s, 2, self.at.in_blk(self.at.sibling))

    def begin(self):
        at = self.at
        pl.when(at.z + 1 < at.nz)(lambda: self.right(at.b).start())
        pl.when(at.z > 0)(lambda: self.left(at.b).start())
        self.across(at.b).start()

    def hop(self, i):
        at = self.at

        @pl.when(at.z >= i)
        def _():
            s = at.b - 2 * i
            self.across(s).wait_recv()
            pl.when(at.z + 1 < at.nz)(lambda: self.right(s).start())
            self.across(s).start()

        @pl.when(at.z + i < at.nz)
        def _():
            s = at.b + 2 * i
            self.across(s).wait_recv()
            pl.when(at.z > 0)(lambda: self.left(s).start())
            self.across(s).start()

    def take_sibling(self, z):
        self.across(2 * z + 1 - self.at.core).wait_recv()

    def finish(self):
        at = self.at
        for i in range(at.nz):

            @pl.when(at.z >= i)
            def _():
                s = at.b - 2 * i
                pl.when(at.z + 1 < at.nz)(lambda: self.right(s).wait_send())
                self.across(s).wait_send()

            if i == 0:
                pl.when(at.z > 0)(lambda: self.left(at.b).wait_send())
            else:

                @pl.when(at.z + i < at.nz)
                def _():
                    s = at.b + 2 * i
                    pl.when(at.z > 0)(lambda: self.left(s).wait_send())
                    self.across(s).wait_send()

    def all(self):
        self.begin()
        for i in range(1, self.at.nz):
            self.hop(i)
        for z in range(self.at.nz):
            self.take_sibling(z)


def sorted_place(at, half, shape, axis):
    s = lax.broadcasted_iota(jnp.int32, shape, axis)
    return jnp.where(
        s < half, at.b * half + s, (2 * at.nb - 1 - at.b) * half + s - half
    )


def block_base(at, b, second, half):
    return jnp.where(second == 0, b * half, (2 * at.nb - 1 - b) * half)


def turn_rows(values, cos, sin):
    half = HEAD_SIZE // 2
    pieces = []
    for first in range(0, values.shape[0], HEAD_SIZE):
        lead = values[first : first + half]
        trail = values[first + half : first + HEAD_SIZE]
        pieces.append(lead * cos - trail * sin)
        pieces.append(trail * cos + lead * sin)
    return jnp.concatenate(pieces, axis=0)


def front_kernel(
    nb,
    nh,
    hl,
    kl,
    inputs,
    w_norm1,
    w_norm2,
    w_own,
    place_row,
    place_col,
    cos,
    sin,
    begin,
    xg,
    wg,
    qn,
    kv,
    lse,
    attn_t,
    ao,
    middle,
    n2,
    qt,
    perm,
    top,
    total,
    out_send,
    out_recv,
    x_sems,
    w_send,
    w_recv,
    kv_send,
    kv_recv,
    o_sems,
):
    at = Place(nb, nh)
    rows = inputs.shape[0]
    group = rows * nh
    half = group // 2
    qw, kw = hl * HEAD_SIZE, kl * HEAD_SIZE
    width = qw + 2 * kw

    hidden = inputs[...].astype(F32)
    unit = hidden * lax.rsqrt(jnp.mean(hidden * hidden, axis=-1, keepdims=True) + eps)
    xg[at.h] = (unit * w_norm1[...]).astype(BF)
    wg[at.b] = w_own[...]
    at.meet()
    x_copies = [
        remote(xg.at[at.h], xg.at[at.h], x_sems.at[0, k], x_sems.at[1, k], at.in_head(at.head_peer(k)))
        for k in range(1, nh)
    ]
    for c in x_copies:
        c.start()
    weights = Relay(at, wg, w_send, w_recv)
    weights.begin()
    perm[...] = jnp.where(
        place_row[...] == sorted_place(at, half, (group, group), 0), 1.0, 0.0
    ).astype(BF)
    for i in range(1, nb // 2):
        weights.hop(i)
    for z in range(nb // 2):
        weights.take_sibling(z)
    for c in x_copies:
        c.wait_recv()
    x = xg[...].reshape(group, MODEL_WIDTH)
    w = wg[...].reshape(MODEL_WIDTH, width + qw)
    qkv_t = nn(x, w[:, :width]).T
    qkv_t = jnp.concatenate(
        [turn_rows(qkv_t[: qw + kw], cos[...], sin[...]), qkv_t[qw + kw :]], axis=0
    ).astype(BF)
    order = perm[...]
    kv_rows = nt(order, qkv_t[qw:]).astype(BF)
    kv[at.b, 0] = kv_rows[:half]
    kv[at.b, 1] = kv_rows[half:]

    def kv_copy(p, second, way, device):
        return remote(
            kv.at[p, second], kv.at[p, second], kv_send.at[way, p], kv_recv.at[p], device
        )

    right = at.in_blk(jnp.minimum(at.b + 2, nb - 2 + at.core))
    left = at.in_blk(jnp.maximum(at.b - 2, at.core))
    across = at.in_blk(at.sibling)
    pl.when(at.z + 1 < at.nz)(lambda: kv_copy(at.b, 0, 0, right).start())
    pl.when(at.z > 0)(lambda: kv_copy(at.b, 1, 0, left).start())
    kv_copy(at.b, at.core, 1, across).start()
    q_rows = nt(order, qkv_t[:qw]).astype(BF)
    qn[...] = q_rows
    q_cols = (nt(qkv_t[:qw], order) * (1.0 / math.sqrt(HEAD_SIZE))).astype(BF)
    qt[0] = q_cols[:, :half]
    qt[1] = q_cols[:, half:]
    top[...] = jnp.full(top.shape, -1e30, F32)
    total[...] = jnp.zeros(total.shape, F32)
    attn_t[...] = jnp.zeros(attn_t.shape, F32)

    def attend(p, second):
        old_top, old_total = top[second], total[second]
        tops, totals = [], []
        block = kv[p, second]
        key_place = block_base(at, p, second, half) + lax.broadcasted_iota(
            jnp.int32, (half, half), 0
        )
        own_place = block_base(at, at.b, second, half) + lax.broadcasted_iota(
            jnp.int32, (half, half), 1
        )
        allowed = (key_place <= own_place) & (key_place >= begin[second])
        for a in range(hl):
            g = a // (hl // kl)
            rows_a = slice(a * HEAD_SIZE, (a + 1) * HEAD_SIZE)
            scores = nn(block[:, g * HEAD_SIZE : (g + 1) * HEAD_SIZE], qt[second, rows_a])
            scores = jnp.where(allowed, scores, -1e30)
            old = old_top[a : a + 1]
            new = jnp.maximum(old, jnp.max(scores, axis=0, keepdims=True))
            probs = jnp.exp(scores - new)
            fade = jnp.exp(old - new)
            totals.append(old_total[a : a + 1] * fade + jnp.sum(probs, axis=0, keepdims=True))
            tops.append(new)
            attn_t[second, rows_a] = attn_t[second, rows_a] * fade + tn(
                block[:, kw + g * HEAD_SIZE : kw + (g + 1) * HEAD_SIZE], probs.astype(BF)
            )
        top[second, :hl] = jnp.concatenate(tops, axis=0)
        total[second, :hl] = jnp.concatenate(totals, axis=0)

    def visit(step, unused):
        i = step // 4
        second = lax.rem(step, 2)
        same = lax.rem(step // 2, 2) == 0
        z = jnp.where(second == 0, at.z - i, at.z + i)
        p = 2 * z + jnp.where(same, at.core, 1 - at.core)
        exists = (z >= 0) & (z < nb // 2) & ((i > 0) | same | (at.core != second))

        @pl.when(exists)
        def _():
            @pl.when(p != at.b)
            def _():
                kv_copy(p, second, 1, across).wait_recv()

            @pl.when((i > 0) & same)
            def _():
                @pl.when((second == 0) & (at.z + 1 < at.nz))
                def _():
                    kv_copy(p, second, 0, right).start()

                @pl.when((second == 1) & (at.z > 0))
                def _():
                    kv_copy(p, second, 0, left).start()

                kv_copy(p, second, 1, across).start()

            attend(p, second)

        return 0

    lax.fori_loop(0, 4 * (nb // 2), visit, 0)
    for second in range(2):
        sums = total[second]
        for a in range(hl):
            rows_a = slice(a * HEAD_SIZE, (a + 1) * HEAD_SIZE)
            attn_t[second, rows_a] = attn_t[second, rows_a] / sums[a : a + 1]
    lse[...] = top[...] + jnp.log(total[...])
    back = jnp.where(place_col[...] == sorted_place(at, half, (group, group), 1), 1.0, 0.0).astype(BF)
    attn_rows = (
        nt(back[:, :half], attn_t[0].astype(BF)) + nt(back[:, half:], attn_t[1].astype(BF))
    ).astype(BF)
    ao[...] = attn_rows
    o_copies = []
    for k in range(nh):
        peer = at.head_peer(k)
        chunk = nt(ao[pl.ds(peer * rows, rows)], w[:, width:])
        if k == 0:
            middle[...] = hidden + chunk
            continue
        out_send[peer] = chunk.astype(BF)
        c = remote(
            out_send.at[peer], out_recv.at[at.h], o_sems.at[0, k], o_sems.at[1, k], at.in_head(peer)
        )
        c.start()
        o_copies.append(c)
    for k in range(1, nh):
        o_copies[k - 1].wait_recv()
        middle[...] += out_recv[lax.rem(at.h + nh - k, nh)].astype(F32)
    mid = middle[...]
    n2[...] = (
        mid * lax.rsqrt(jnp.mean(mid * mid, axis=-1, keepdims=True) + eps) * w_norm2[...]
    ).astype(BF)
    weights.finish()
    for c in x_copies + o_copies:
        c.wait_send()

    def drain(step, unused):
        i = step // 2
        second = lax.rem(step, 2)
        z = jnp.where(second == 0, at.z - i, at.z + i)
        p = 2 * z + at.core

        @pl.when((z >= 0) & (z < nb // 2))
        def _():
            @pl.when((second == 0) & (at.z + 1 < at.nz))
            def _():
                kv_copy(p, second, 0, right).wait_send()

            @pl.when((second == 1) & (at.z > 0))
            def _():
                kv_copy(p, second, 0, left).wait_send()

            @pl.when((i > 0) | (second == at.core))
            def _():
                kv_copy(p, second, 1, across).wait_send()

        return 0

    lax.fori_loop(0, nb, drain, 0)


def front(nb, nh, hl, kl, inputs, w_norm1, w_norm2, w_own, place_row, place_col, cos, sin, begin):
    rows = inputs.shape[0]
    group, half = rows * nh, rows * nh // 2
    dl, wide = w_own.shape
    qw, kw = hl * HEAD_SIZE, kl * HEAD_SIZE
    shape = jax.ShapeDtypeStruct
    return pl.pallas_call(
        functools.partial(front_kernel, nb, nh, hl, kl),
        out_shape=(
            shape((nh, rows, MODEL_WIDTH), BF),
            shape((nb, dl, wide), BF),
            shape((group, qw), BF),
            shape((nb, 2, half, 2 * kw), BF),
            shape((2, max(hl, 8), half), F32),
            shape((2, qw, half), F32),
            shape((group, qw), BF),
            shape((rows, MODEL_WIDTH), F32),
            shape((rows, MODEL_WIDTH), BF),
        ),
        in_specs=[VMEM] * 9,
        out_specs=[VMEM] * 9,
        scratch_shapes=[
            pltpu.VMEM((2, qw, half), BF),
            pltpu.VMEM((group, group), BF),
            pltpu.VMEM((2, max(hl, 8), half), F32),
            pltpu.VMEM((2, max(hl, 8), half), F32),
            pltpu.VMEM((nh, rows, MODEL_WIDTH), BF),
            pltpu.VMEM((nh, rows, MODEL_WIDTH), BF),
            pltpu.SemaphoreType.DMA((2, nh)),
            pltpu.SemaphoreType.DMA((3, nb)),
            pltpu.SemaphoreType.DMA((nb,)),
            pltpu.SemaphoreType.DMA((2, nb)),
            pltpu.SemaphoreType.DMA((nb,)),
            pltpu.SemaphoreType.DMA((2, nh)),
        ],
        compiler_params=pltpu.CompilerParams(collective_id=1, vmem_limit_bytes=48 * 2**20),
        name="front",
    )(inputs, w_norm1, w_norm2, w_own, place_row, place_col, cos, sin, begin)


def seq_begin(token_position, lengths):
    starts = jnp.cumsum(lengths) - lengths
    inside = token_position[:, None] >= starts[None, 1:]
    return jnp.sum(jnp.where(inside, lengths[None, :-1], 0), axis=1)


def rotation_rows(token_position, begin_index):
    half = HEAD_SIZE // 2
    freq = jnp.exp(
        jnp.arange(half, dtype=F32) * (-2.0 * math.log(rope_base) / HEAD_SIZE)
    )
    angle = freq[:, None] * (token_position - begin_index).astype(F32)[None, :]
    return jnp.cos(angle), jnp.sin(angle)


def head_inputs(nb, nh, rows, token_place, lengths, w_query, key_weight, value_weight, w_out):
    group, half = rows * nh, rows * nh // 2
    b = lax.axis_index("blk")
    own = lax.dynamic_slice_in_dim(token_place, b * group, group)
    s = jnp.arange(group, dtype=jnp.int32)
    in_order = jnp.where(s < half, b * half + s, (2 * nb - 1 - b) * half + s - half)
    begin_s = seq_begin(in_order, lengths)
    cos_o, sin_o = rotation_rows(own, seq_begin(own, lengths))
    cos_s, sin_s = rotation_rows(in_order, begin_s)
    w_own = jnp.concatenate([w_query, key_weight, value_weight, w_out.T], axis=1)
    return own, begin_s.reshape(2, 1, half), cos_o, sin_o, cos_s, sin_s, w_own


def seq_rotation(token_position, begin_index, width):
    half = width // 2
    freq = jnp.exp(jnp.arange(half, dtype=jnp.float32) * (-2.0 * math.log(rope_base) / width))
    angle = (token_position - begin_index).astype(jnp.float32)[:, None] * freq[None, :]
    return (jnp.cos(angle)[:, None, :], jnp.sin(angle)[:, None, :])


def turn_index(values, cosine_table, sine_table):
    half = values.shape[-1] // 2
    leading = values[..., :half]
    trailing = values[..., half:]
    return jnp.concatenate(
        [
            leading * cosine_table - trailing * sine_table,
            trailing * cosine_table + leading * sine_table,
        ],
        axis=-1,
    )


def slot_numbers(routes, slot_order):
    flat_expert = routes.reshape(-1)
    rank = slot_order.reshape(-1)
    count = flat_expert.shape[0]
    by_rank = jnp.zeros((count,), jnp.int32).at[rank].set(jnp.arange(count, dtype=jnp.int32))
    expert_sorted = flat_expert[by_rank]
    onehot = (expert_sorted[:, None] == jnp.arange(E, dtype=jnp.int32)[None, :]).astype(jnp.int32)
    before = jnp.cumsum(onehot, axis=0) - onehot
    slot_sorted = jnp.sum(before * onehot, axis=1)
    slot = slot_sorted[rank].reshape(routes.shape)
    return (slot, slot < CAP)


def along_rows(left, right):
    return lax.dot_general(
        left, right, (((0,), (0,)), ((), ())), preferred_element_type=jnp.float32
    )


def against(left, right):
    return lax.dot_general(
        left, right, (((1,), (1,)), ((), ())), preferred_element_type=jnp.float32
    )


def fetch_attention(w_query, key_weight, value_weight, w_out):
    return (
        lax.all_gather(w_query, "blk", axis=0, tiled=True),
        lax.all_gather(key_weight, "blk", axis=0, tiled=True),
        lax.all_gather(value_weight, "blk", axis=0, tiled=True),
        lax.all_gather(w_out, "blk", axis=1, tiled=True),
    )


def fetch_experts(w_gate, w_up, w_down):
    return (
        lax.all_gather(w_gate, "blk", axis=1, tiled=True),
        lax.all_gather(w_up, "blk", axis=1, tiled=True),
        lax.all_gather(w_down, "blk", axis=2, tiled=True),
    )


def fetch_keys(rotated_key, value_rows):
    return (
        lax.all_gather(rotated_key, "blk", axis=0, tiled=True),
        lax.all_gather(value_rows, "blk", axis=0, tiled=True),
    )


def on_device(
    inputs,
    token_place,
    lengths,
    w_norm1,
    w_query,
    key_weight,
    value_weight,
    w_out,
    w_norm2,
    router,
    routes,
    slot_order,
    w_gate,
    w_up,
    w_down,
    grad_out,
):
    rows = inputs.shape[0]
    blk_count = lax.axis_size("blk")
    head_count = lax.axis_size("head")
    group_rows = rows * head_count
    heads_local = w_query.shape[1] // HEAD_SIZE
    kv_local = key_weight.shape[1] // HEAD_SIZE
    head_groups = heads_local // kv_local
    experts_local = E // head_count
    scale = 1.0 / math.sqrt(HEAD_SIZE)
    query_all, key_all, value_all, out_all = fetch_attention(
        w_query, key_weight, value_weight, w_out
    )
    gate_all, up_all, down_all = fetch_experts(w_gate, w_up, w_down)
    hidden = inputs.astype(jnp.float32)
    scale_one = lax.rsqrt(jnp.mean(hidden * hidden, axis=-1, keepdims=True) + eps)
    unit_one = hidden * scale_one
    normed = (unit_one * w_norm1).astype(jnp.bfloat16)
    gathered = lax.all_gather(normed, "head", axis=0, tiled=True)
    begin_index = seq_begin(token_place, lengths)
    first_row = lax.axis_index("blk") * group_rows
    own_place = lax.dynamic_slice_in_dim(token_place, first_row, group_rows)
    own_begin = lax.dynamic_slice_in_dim(begin_index, first_row, group_rows)
    cosine_table, sine_table = seq_rotation(own_place, own_begin, HEAD_SIZE)
    query = jnp.dot(gathered, query_all, preferred_element_type=jnp.float32)
    key = jnp.dot(gathered, key_all, preferred_element_type=jnp.float32)
    value_rows = jnp.dot(gathered, value_all, preferred_element_type=jnp.float32).astype(
        jnp.bfloat16
    )
    rotated_query = turn_index(
        query.reshape(group_rows, heads_local, HEAD_SIZE), cosine_table, sine_table
    ).astype(jnp.bfloat16)
    rotated_key = (
        turn_index(key.reshape(group_rows, kv_local, HEAD_SIZE), cosine_table, sine_table)
        .astype(jnp.bfloat16)
        .reshape(group_rows, kv_local * HEAD_SIZE)
    )
    keys_all, values_all = fetch_keys(rotated_key, value_rows)
    query_heads = rotated_query.reshape(group_rows, kv_local, head_groups, HEAD_SIZE)
    steps = jnp.arange(blk_count, dtype=jnp.int32)

    def block_scores(key_source, value_source, index):
        start = index * group_rows
        key_block = lax.dynamic_slice_in_dim(key_source, start, group_rows).reshape(
            group_rows, kv_local, HEAD_SIZE
        )
        value_block = lax.dynamic_slice_in_dim(value_source, start, group_rows).reshape(
            group_rows, kv_local, HEAD_SIZE
        )
        key_place = lax.dynamic_slice_in_dim(token_place, start, group_rows)
        scores = (
            jnp.einsum("qhgd,khd->hgqk", query_heads, key_block, preferred_element_type=jnp.float32)
            * scale
        )
        allowed = (key_place[None, :] <= own_place[:, None]) & (
            key_place[None, :] >= own_begin[:, None]
        )
        return (scores, allowed, key_block, value_block)

    def stats_step(carry, index):
        top, total = carry
        scores, allowed, unused_keys, unused_values = block_scores(keys_all, values_all, index)
        masked = jnp.where(allowed, scores, -1e30)
        new_top = jnp.maximum(top, jnp.max(masked, axis=-1))
        total = total * jnp.exp(top - new_top) + jnp.sum(
            jnp.where(allowed, jnp.exp(masked - new_top[..., None]), 0.0), axis=-1
        )
        return ((new_top, total), None)

    start_top = jnp.full((kv_local, head_groups, group_rows), -1e30, jnp.float32)
    start_total = jnp.zeros((kv_local, head_groups, group_rows), jnp.float32)
    (top, total), unused = lax.scan(stats_step, (start_top, start_total), steps)
    log_total = top + jnp.log(total)

    def out_step(acc, index):
        scores, allowed, unused_keys, value_block = block_scores(keys_all, values_all, index)
        probs = jnp.where(allowed, jnp.exp(scores - log_total[..., None]), 0.0).astype(jnp.bfloat16)
        acc = acc + jnp.einsum(
            "hgqk,khd->qhgd", probs, value_block, preferred_element_type=jnp.float32
        )
        return (acc, None)

    attended32, unused = lax.scan(
        out_step, jnp.zeros((group_rows, kv_local, head_groups, HEAD_SIZE), jnp.float32), steps
    )
    attended_rows = attended32.reshape(group_rows, heads_local * HEAD_SIZE).astype(jnp.bfloat16)
    own, begin_s, cos_o, sin_o, cos_s, sin_s, w_own = head_inputs(
        blk_count, head_count, rows, token_place, lengths, w_query, key_weight, value_weight, w_out
    )
    middle = front(
        blk_count, head_count, heads_local, kv_local, inputs, w_norm1.reshape(1, -1), w_norm2.reshape(1, -1),
        w_own, own.reshape(1, -1), own.reshape(-1, 1), cos_o, sin_o, begin_s,
    )[7]
    scale_two = lax.rsqrt(jnp.mean(middle * middle, axis=-1, keepdims=True) + eps)
    unit_two = middle * scale_two
    normed_two = (unit_two * w_norm2).astype(jnp.bfloat16)
    logits = jnp.dot(normed_two, router, preferred_element_type=jnp.float32)
    chosen = jnp.take_along_axis(logits, routes, axis=1)
    shifted = jnp.exp(chosen - jnp.max(chosen, axis=-1, keepdims=True))
    gates = shifted / jnp.sum(shifted, axis=-1, keepdims=True)
    slot, kept = slot_numbers(routes, slot_order)
    target = routes * CAP + slot
    slot_ids = jnp.arange(E * CAP, dtype=jnp.int32)
    match = (target[None, :, :] == slot_ids[:, None, None]) & kept[None, :, :]
    dispatch = jnp.any(match, axis=-1).astype(jnp.bfloat16)
    buffer = jnp.dot(dispatch, normed_two, preferred_element_type=jnp.float32).astype(jnp.bfloat16)
    arrived = lax.all_to_all(
        buffer.reshape(head_count, experts_local, CAP, MODEL_WIDTH),
        "head",
        split_axis=0,
        concat_axis=0,
        tiled=True,
    )
    gate_pre = jnp.einsum("secd,edf->secf", arrived, gate_all, preferred_element_type=jnp.float32)
    up_pre = jnp.einsum("secd,edf->secf", arrived, up_all, preferred_element_type=jnp.float32)
    sigma = jax.nn.sigmoid(gate_pre)
    swish = gate_pre * sigma
    activated = (swish * up_pre).astype(jnp.bfloat16)
    expert_out = jnp.einsum(
        "secf,efd->secd", activated, down_all, preferred_element_type=jnp.float32
    ).astype(jnp.bfloat16)
    returned = lax.all_to_all(expert_out, "head", split_axis=0, concat_axis=0, tiled=True).reshape(
        E * CAP, MODEL_WIDTH
    )
    picked = returned[jnp.where(kept, target, 0)].astype(jnp.float32)
    mixed = jnp.sum(jnp.where(kept, gates, 0.0)[..., None] * picked, axis=1)
    output = (middle + mixed).astype(jnp.bfloat16)
    query_all, key_all, value_all, out_all = fetch_attention(
        w_query, key_weight, value_weight, w_out
    )
    gate_all, up_all, down_all = fetch_experts(w_gate, w_up, w_down)
    keys_all, values_all = fetch_keys(rotated_key, value_rows)
    upstream = grad_out.astype(jnp.float32)
    d_gates = jnp.where(kept, jnp.sum(picked * upstream[:, None, :], axis=-1), 0.0)
    token_ids = jnp.broadcast_to(jnp.arange(rows, dtype=jnp.int32)[:, None], (rows, TOPK))
    slot_token = jnp.sum(jnp.where(match, token_ids[None], 0), axis=(1, 2))
    slot_gate = jnp.sum(jnp.where(match, gates[None], 0.0), axis=(1, 2))
    d_slots = (slot_gate[:, None] * upstream[slot_token]).astype(jnp.bfloat16)
    d_returned = lax.all_to_all(
        d_slots.reshape(head_count, experts_local, CAP, MODEL_WIDTH),
        "head",
        split_axis=0,
        concat_axis=0,
        tiled=True,
    )
    d_activated = jnp.einsum(
        "secd,efd->secf", d_returned, down_all, preferred_element_type=jnp.float32
    )
    d_gate_pre = (d_activated * up_pre * sigma * (1.0 + gate_pre * (1.0 - sigma))).astype(
        jnp.bfloat16
    )
    d_up_pre = (d_activated * swish).astype(jnp.bfloat16)
    d_arrived = jnp.einsum(
        "secf,edf->secd", d_gate_pre, gate_all, preferred_element_type=jnp.float32
    )
    d_arrived = (
        d_arrived
        + jnp.einsum("secf,edf->secd", d_up_pre, up_all, preferred_element_type=jnp.float32)
    ).astype(jnp.bfloat16)
    d_buffer = lax.all_to_all(d_arrived, "head", split_axis=0, concat_axis=0, tiled=True).reshape(
        E * CAP, MODEL_WIDTH
    )
    d_normed_two = along_rows(dispatch, d_buffer)
    weighted = jnp.sum(gates * d_gates, axis=-1, keepdims=True)
    d_chosen = gates * (d_gates - weighted)
    route_hits = routes[..., None] == jnp.arange(E, dtype=jnp.int32)[None, None, :]
    d_logits = jnp.sum(jnp.where(route_hits, d_chosen[..., None], 0.0), axis=1)
    router_wide = router.astype(jnp.float32)
    d_normed_two = d_normed_two + lax.dot_general(
        d_logits, router_wide, (((1,), (1,)), ((), ())), precision=lax.Precision.HIGHEST
    )
    grad_router = lax.dot_general(
        normed_two.astype(jnp.float32),
        d_logits,
        (((0,), (0,)), ((), ())),
        precision=lax.Precision.HIGHEST,
    )
    weighted_two = d_normed_two * w_norm2
    grad_norm2 = jnp.sum(d_normed_two * unit_two, axis=0)
    d_middle = upstream + scale_two * (
        weighted_two - unit_two * jnp.mean(unit_two * weighted_two, axis=-1, keepdims=True)
    )
    d_branch = lax.all_gather(d_middle.astype(jnp.bfloat16), "head", axis=0, tiled=True)
    grad_out_w = along_rows(attended_rows, d_branch)
    d_attended = against(d_branch, out_all).astype(jnp.bfloat16)
    d_heads = d_attended.reshape(group_rows, kv_local, head_groups, HEAD_SIZE)
    delta = jnp.transpose(jnp.sum(d_heads.astype(jnp.float32) * attended32, axis=-1), (1, 2, 0))

    def back_step(acc, index):
        scores, allowed, key_block, value_block = block_scores(keys_all, values_all, index)
        probs = jnp.where(allowed, jnp.exp(scores - log_total[..., None]), 0.0)
        d_probs = jnp.einsum(
            "qhgd,khd->hgqk", d_heads, value_block, preferred_element_type=jnp.float32
        )
        d_scores = (probs * (d_probs - delta[..., None])).astype(jnp.bfloat16)
        acc = acc + jnp.einsum(
            "hgqk,khd->qhgd", d_scores, key_block, preferred_element_type=jnp.float32
        )
        d_keys = (
            jnp.einsum("hgqk,qhgd->khd", d_scores, query_heads, preferred_element_type=jnp.float32)
            * scale
        )
        d_values = jnp.einsum(
            "hgqk,qhgd->khd",
            probs.astype(jnp.bfloat16),
            d_heads,
            preferred_element_type=jnp.float32,
        )
        return (
            acc,
            (
                d_keys.reshape(group_rows, kv_local * HEAD_SIZE),
                d_values.reshape(group_rows, kv_local * HEAD_SIZE),
            ),
        )

    d_query_acc, (key_pieces, value_pieces) = lax.scan(
        back_step, jnp.zeros((group_rows, kv_local, head_groups, HEAD_SIZE), jnp.float32), steps
    )
    d_key_rot, d_value_sum = (
        lax.psum_scatter(
            key_pieces.reshape(blk_count * group_rows, kv_local * HEAD_SIZE).astype(jnp.bfloat16),
            "blk",
            scatter_dimension=0,
            tiled=True,
        ).astype(jnp.float32),
        lax.psum_scatter(
            value_pieces.reshape(blk_count * group_rows, kv_local * HEAD_SIZE).astype(jnp.bfloat16),
            "blk",
            scatter_dimension=0,
            tiled=True,
        ).astype(jnp.float32),
    )
    d_query = (
        turn_index(
            d_query_acc.reshape(group_rows, heads_local, HEAD_SIZE) * scale,
            cosine_table,
            -sine_table,
        )
        .reshape(group_rows, heads_local * HEAD_SIZE)
        .astype(jnp.bfloat16)
    )
    d_key = (
        turn_index(d_key_rot.reshape(group_rows, kv_local, HEAD_SIZE), cosine_table, -sine_table)
        .reshape(group_rows, kv_local * HEAD_SIZE)
        .astype(jnp.bfloat16)
    )
    d_value = d_value_sum.astype(jnp.bfloat16)
    grad_query_w = along_rows(gathered, d_query)
    grad_key_w = along_rows(gathered, d_key)
    grad_value_w = along_rows(gathered, d_value)
    total = against(d_query, query_all)
    total = total + against(d_key, key_all)
    d_normed = lax.psum_scatter(
        (total + against(d_value, value_all)).astype(jnp.bfloat16),
        "head",
        scatter_dimension=0,
        tiled=True,
    ).astype(jnp.float32)
    weighted_one = d_normed * w_norm1
    grad_norm1 = jnp.sum(d_normed * unit_one, axis=0)
    grad_inputs = d_middle + scale_one * (
        weighted_one - unit_one * jnp.mean(unit_one * weighted_one, axis=-1, keepdims=True)
    )
    grad_gate = jnp.einsum(
        "secd,secf->edf", arrived, d_gate_pre, preferred_element_type=jnp.float32
    )
    grad_up = jnp.einsum("secd,secf->edf", arrived, d_up_pre, preferred_element_type=jnp.float32)
    grad_down = jnp.einsum(
        "secf,secd->efd", activated, d_returned, preferred_element_type=jnp.float32
    )
    sharded = (
        lax.psum_scatter(
            grad_query_w.astype(jnp.bfloat16), "blk", scatter_dimension=0, tiled=True
        ).astype(jnp.float32),
        lax.psum_scatter(
            grad_key_w.astype(jnp.bfloat16), "blk", scatter_dimension=0, tiled=True
        ).astype(jnp.float32),
        lax.psum_scatter(
            grad_value_w.astype(jnp.bfloat16), "blk", scatter_dimension=0, tiled=True
        ).astype(jnp.float32),
        lax.psum_scatter(
            grad_out_w.astype(jnp.bfloat16), "blk", scatter_dimension=1, tiled=True
        ).astype(jnp.float32),
        lax.psum_scatter(
            grad_gate.astype(jnp.bfloat16), "blk", scatter_dimension=1, tiled=True
        ).astype(jnp.float32),
        lax.psum_scatter(
            grad_up.astype(jnp.bfloat16), "blk", scatter_dimension=1, tiled=True
        ).astype(jnp.float32),
        lax.psum_scatter(
            grad_down.astype(jnp.bfloat16), "blk", scatter_dimension=2, tiled=True
        ).astype(jnp.float32),
    )
    small = lax.psum((grad_norm1, grad_norm2, grad_router), ("blk", "head"))
    return (
        output,
        grad_inputs,
        small[0],
        sharded[0],
        sharded[1],
        sharded[2],
        sharded[3],
        small[1],
        small[2],
        sharded[4],
        sharded[5],
        sharded[6],
    )


def solution(mesh):
    return jax.shard_map(
        on_device,
        mesh=mesh,
        in_specs=(
            P(("blk", "head"), None),
            P(),
            P(),
            P(),
            P("blk", "head"),
            P("blk", "head"),
            P("blk", "head"),
            P("head", "blk"),
            P(),
            P(),
            P(("blk", "head"), None),
            P(("blk", "head"), None),
            P("head", "blk", None),
            P("head", "blk", None),
            P("head", None, "blk"),
            P(("blk", "head"), None),
        ),
        out_specs=(
            P(("blk", "head"), None),
            P(("blk", "head"), None),
            P(),
            P("blk", "head"),
            P("blk", "head"),
            P("blk", "head"),
            P("head", "blk"),
            P(),
            P(),
            P("head", "blk", None),
            P("head", "blk", None),
            P("head", None, "blk"),
        ),
        check_vma=False,
    )
```

```python
import functools
import math

import jax
import jax.numpy as jnp
from jax import lax
from jax.experimental import pallas as pl
from jax.experimental.pallas import tpu as pltpu
from jax.sharding import PartitionSpec as P

MODEL_WIDTH = 1024
HEAD_SIZE = 64
E = 32
TOPK = 8
CAP = 40
MESH = pl.DeviceIdType.MESH
VMEM = pl.BlockSpec(memory_space=pltpu.VMEM)
ANY = pl.BlockSpec(memory_space=pl.ANY)
BF = jnp.bfloat16
F32 = jnp.float32

eps = 1e-06
rope_base = 10000.0


def nn(a, b, **kw):
    return lax.dot_general(a, b, (((1,), (0,)), ((), ())), preferred_element_type=F32, **kw)


def nt(a, b, **kw):
    return lax.dot_general(a, b, (((1,), (1,)), ((), ())), preferred_element_type=F32, **kw)


def tn(a, b, **kw):
    return lax.dot_general(a, b, (((0,), (0,)), ((), ())), preferred_element_type=F32, **kw)


def remote(src, dst, send, recv, device):
    return pltpu.make_async_remote_copy(
        src_ref=src,
        dst_ref=dst,
        send_sem=send,
        recv_sem=recv,
        device_id=device,
        device_id_type=MESH,
    )


class Place:
    def __init__(self, nb, nh):
        self.nb, self.nh, self.nz = nb, nh, nb // 2
        self.b, self.h = lax.axis_index("blk"), lax.axis_index("head")
        self.z, self.core = self.b // 2, lax.rem(self.b, 2)
        self.sibling = 2 * self.z + 1 - self.core

    def in_blk(self, b):
        return (b, self.h)

    def in_head(self, h):
        return (self.b, h)

    def head_peer(self, k):
        return lax.rem(self.h + k, self.nh)

    def blk_peer(self, k):
        return lax.rem(self.b + k, self.nb)

    def meet(self):
        barrier = pltpu.get_barrier_semaphore()
        for k in range(1, self.nh):
            pl.semaphore_signal(
                barrier, inc=1, device_id=self.in_head(self.head_peer(k)), device_id_type=MESH
            )
        for k in range(1, self.nb):
            pl.semaphore_signal(
                barrier, inc=1, device_id=self.in_blk(self.blk_peer(k)), device_id_type=MESH
            )
        pl.semaphore_wait(barrier, self.nh + self.nb - 2)


class Relay:
    def __init__(self, at, buf, send, recv):
        self.at, self.buf, self.send, self.recv = at, buf, send, recv

    def copy(self, s, way, device):
        return remote(
            self.buf.at[s], self.buf.at[s], self.send.at[way, s], self.recv.at[s], device
        )

    def right(self, s):
        return self.copy(s, 0, self.at.in_blk(jnp.minimum(self.at.b + 2, self.at.nb - 2 + self.at.core)))

    def left(self, s):
        return self.copy(s, 1, self.at.in_blk(jnp.maximum(self.at.b - 2, self.at.core)))

    def across(self, s):
        return self.copy(s, 2, self.at.in_blk(self.at.sibling))

    def begin(self):
        at = self.at
        pl.when(at.z + 1 < at.nz)(lambda: self.right(at.b).start())
        pl.when(at.z > 0)(lambda: self.left(at.b).start())
        self.across(at.b).start()

    def hop(self, i):
        at = self.at

        @pl.when(at.z >= i)
        def _():
            s = at.b - 2 * i
            self.across(s).wait_recv()
            pl.when(at.z + 1 < at.nz)(lambda: self.right(s).start())
            self.across(s).start()

        @pl.when(at.z + i < at.nz)
        def _():
            s = at.b + 2 * i
            self.across(s).wait_recv()
            pl.when(at.z > 0)(lambda: self.left(s).start())
            self.across(s).start()

    def take_sibling(self, z):
        self.across(2 * z + 1 - self.at.core).wait_recv()

    def finish(self):
        at = self.at
        for i in range(at.nz):

            @pl.when(at.z >= i)
            def _():
                s = at.b - 2 * i
                pl.when(at.z + 1 < at.nz)(lambda: self.right(s).wait_send())
                self.across(s).wait_send()

            if i == 0:
                pl.when(at.z > 0)(lambda: self.left(at.b).wait_send())
            else:

                @pl.when(at.z + i < at.nz)
                def _():
                    s = at.b + 2 * i
                    pl.when(at.z > 0)(lambda: self.left(s).wait_send())
                    self.across(s).wait_send()

    def all(self):
        self.begin()
        for i in range(1, self.at.nz):
            self.hop(i)
        for z in range(self.at.nz):
            self.take_sibling(z)


def sorted_place(at, half, shape, axis):
    s = lax.broadcasted_iota(jnp.int32, shape, axis)
    return jnp.where(
        s < half, at.b * half + s, (2 * at.nb - 1 - at.b) * half + s - half
    )


def block_base(at, b, second, half):
    return jnp.where(second == 0, b * half, (2 * at.nb - 1 - b) * half)


def turn_rows(values, cos, sin):
    half = HEAD_SIZE // 2
    pieces = []
    for first in range(0, values.shape[0], HEAD_SIZE):
        lead = values[first : first + half]
        trail = values[first + half : first + HEAD_SIZE]
        pieces.append(lead * cos - trail * sin)
        pieces.append(trail * cos + lead * sin)
    return jnp.concatenate(pieces, axis=0)


def front_kernel(
    nb,
    nh,
    hl,
    kl,
    inputs,
    w_norm1,
    w_norm2,
    w_own,
    place_row,
    place_col,
    cos,
    sin,
    begin,
    xg,
    wg,
    qt,
    kv,
    lse,
    attn_t,
    ao_t,
    middle,
    n2,
    ao,
    perm,
    top,
    total,
    out_send,
    out_recv,
    x_sems,
    w_send,
    w_recv,
    kv_send,
    kv_recv,
    o_sems,
):
    at = Place(nb, nh)
    rows = inputs.shape[0]
    group = rows * nh
    half = group // 2
    qw, kw = hl * HEAD_SIZE, kl * HEAD_SIZE
    width = qw + 2 * kw

    hidden = inputs[...].astype(F32)
    unit = hidden * lax.rsqrt(jnp.mean(hidden * hidden, axis=-1, keepdims=True) + eps)
    xg[at.h] = (unit * w_norm1[...]).astype(BF)
    wg[at.b] = w_own[...]
    at.meet()
    x_copies = [
        remote(xg.at[at.h], xg.at[at.h], x_sems.at[0, k], x_sems.at[1, k], at.in_head(at.head_peer(k)))
        for k in range(1, nh)
    ]
    for c in x_copies:
        c.start()
    weights = Relay(at, wg, w_send, w_recv)
    weights.begin()
    perm[...] = jnp.where(
        place_row[...] == sorted_place(at, half, (group, group), 0), 1.0, 0.0
    ).astype(BF)
    for i in range(1, nb // 2):
        weights.hop(i)
    for z in range(nb // 2):
        weights.take_sibling(z)
    for c in x_copies:
        c.wait_recv()
    x = xg[...].reshape(group, MODEL_WIDTH)
    w = wg[...].reshape(MODEL_WIDTH, width + qw)
    qkv_t = nn(x, w[:, :width]).T
    qkv_t = jnp.concatenate(
        [turn_rows(qkv_t[: qw + kw], cos[...], sin[...]), qkv_t[qw + kw :]], axis=0
    ).astype(BF)
    order = perm[...]
    kv_rows = nt(order, qkv_t[qw:]).astype(BF)
    kv[at.b, 0] = kv_rows[:half]
    kv[at.b, 1] = kv_rows[half:]

    def kv_copy(p, second, way, device):
        return remote(
            kv.at[p, second], kv.at[p, second], kv_send.at[way, p], kv_recv.at[p], device
        )

    right = at.in_blk(jnp.minimum(at.b + 2, nb - 2 + at.core))
    left = at.in_blk(jnp.maximum(at.b - 2, at.core))
    across = at.in_blk(at.sibling)
    pl.when(at.z + 1 < at.nz)(lambda: kv_copy(at.b, 0, 0, right).start())
    pl.when(at.z > 0)(lambda: kv_copy(at.b, 1, 0, left).start())
    kv_copy(at.b, at.core, 1, across).start()
    q_cols = (nt(qkv_t[:qw], order) * (1.0 / math.sqrt(HEAD_SIZE))).astype(BF)
    qt[0] = q_cols[:, :half]
    qt[1] = q_cols[:, half:]
    top[...] = jnp.full(top.shape, -1e30, F32)
    total[...] = jnp.zeros(total.shape, F32)
    attn_t[...] = jnp.zeros(attn_t.shape, F32)

    def attend(p, second):
        old_top, old_total = top[second], total[second]
        tops, totals = [], []
        block = kv[p, second]
        key_place = block_base(at, p, second, half) + lax.broadcasted_iota(
            jnp.int32, (half, half), 0
        )
        own_place = block_base(at, at.b, second, half) + lax.broadcasted_iota(
            jnp.int32, (half, half), 1
        )
        allowed = (key_place <= own_place) & (key_place >= begin[second])
        for a in range(hl):
            g = a // (hl // kl)
            rows_a = slice(a * HEAD_SIZE, (a + 1) * HEAD_SIZE)
            scores = nn(block[:, g * HEAD_SIZE : (g + 1) * HEAD_SIZE], qt[second, rows_a])
            scores = jnp.where(allowed, scores, -1e30)
            old = old_top[a : a + 1]
            new = jnp.maximum(old, jnp.max(scores, axis=0, keepdims=True))
            probs = jnp.exp(scores - new)
            fade = jnp.exp(old - new)
            totals.append(old_total[a : a + 1] * fade + jnp.sum(probs, axis=0, keepdims=True))
            tops.append(new)
            attn_t[second, rows_a] = attn_t[second, rows_a] * fade + tn(
                block[:, kw + g * HEAD_SIZE : kw + (g + 1) * HEAD_SIZE], probs.astype(BF)
            )
        top[second, :hl] = jnp.concatenate(tops, axis=0)
        total[second, :hl] = jnp.concatenate(totals, axis=0)

    def visit(step, unused):
        i = step // 4
        second = lax.rem(step, 2)
        same = lax.rem(step // 2, 2) == 0
        z = jnp.where(second == 0, at.z - i, at.z + i)
        p = 2 * z + jnp.where(same, at.core, 1 - at.core)
        exists = (z >= 0) & (z < nb // 2) & ((i > 0) | same | (at.core != second))

        @pl.when(exists)
        def _():
            @pl.when(p != at.b)
            def _():
                kv_copy(p, second, 1, across).wait_recv()

            @pl.when((i > 0) & same)
            def _():
                @pl.when((second == 0) & (at.z + 1 < at.nz))
                def _():
                    kv_copy(p, second, 0, right).start()

                @pl.when((second == 1) & (at.z > 0))
                def _():
                    kv_copy(p, second, 0, left).start()

                kv_copy(p, second, 1, across).start()

            attend(p, second)

        return 0

    lax.fori_loop(0, 4 * (nb // 2), visit, 0)
    for second in range(2):
        sums = total[second]
        for a in range(hl):
            rows_a = slice(a * HEAD_SIZE, (a + 1) * HEAD_SIZE)
            attn_t[second, rows_a] = attn_t[second, rows_a] / sums[a : a + 1]
    lse[...] = top[...] + jnp.log(total[...])
    back = jnp.where(place_col[...] == sorted_place(at, half, (group, group), 1), 1.0, 0.0).astype(BF)
    attn_rows = (
        nt(back[:, :half], attn_t[0].astype(BF)) + nt(back[:, half:], attn_t[1].astype(BF))
    ).astype(BF)
    ao[...] = attn_rows
    ao_t[...] = (
        nn(attn_t[0].astype(BF), perm[:half]) + nn(attn_t[1].astype(BF), perm[half:])
    ).astype(BF)
    o_copies = []
    for k in range(nh):
        peer = at.head_peer(k)
        chunk = nt(ao[pl.ds(peer * rows, rows)], w[:, width:])
        if k == 0:
            middle[...] = hidden + chunk
            continue
        out_send[peer] = chunk.astype(BF)
        c = remote(
            out_send.at[peer], out_recv.at[at.h], o_sems.at[0, k], o_sems.at[1, k], at.in_head(peer)
        )
        c.start()
        o_copies.append(c)
    for k in range(1, nh):
        o_copies[k - 1].wait_recv()
        middle[...] += out_recv[lax.rem(at.h + nh - k, nh)].astype(F32)
    mid = middle[...]
    n2[...] = (
        mid * lax.rsqrt(jnp.mean(mid * mid, axis=-1, keepdims=True) + eps) * w_norm2[...]
    ).astype(BF)
    weights.finish()
    for c in x_copies + o_copies:
        c.wait_send()

    def drain(step, unused):
        i = step // 2
        second = lax.rem(step, 2)
        z = jnp.where(second == 0, at.z - i, at.z + i)
        p = 2 * z + at.core

        @pl.when((z >= 0) & (z < nb // 2))
        def _():
            @pl.when((second == 0) & (at.z + 1 < at.nz))
            def _():
                kv_copy(p, second, 0, right).wait_send()

            @pl.when((second == 1) & (at.z > 0))
            def _():
                kv_copy(p, second, 0, left).wait_send()

            @pl.when((i > 0) | (second == at.core))
            def _():
                kv_copy(p, second, 1, across).wait_send()

        return 0

    lax.fori_loop(0, nb, drain, 0)


def front(nb, nh, hl, kl, inputs, w_norm1, w_norm2, w_own, place_row, place_col, cos, sin, begin):
    rows = inputs.shape[0]
    group, half = rows * nh, rows * nh // 2
    dl, wide = w_own.shape
    qw, kw = hl * HEAD_SIZE, kl * HEAD_SIZE
    shape = jax.ShapeDtypeStruct
    return pl.pallas_call(
        functools.partial(front_kernel, nb, nh, hl, kl),
        out_shape=(
            shape((nh, rows, MODEL_WIDTH), BF),
            shape((nb, dl, wide), BF),
            shape((2, qw, half), BF),
            shape((nb, 2, half, 2 * kw), BF),
            shape((2, max(hl, 8), half), F32),
            shape((2, qw, half), F32),
            shape((qw, group), BF),
            shape((rows, MODEL_WIDTH), F32),
            shape((rows, MODEL_WIDTH), BF),
        ),
        in_specs=[VMEM] * 9,
        out_specs=[VMEM] * 9,
        scratch_shapes=[
            pltpu.VMEM((group, qw), BF),
            pltpu.VMEM((group, group), BF),
            pltpu.VMEM((2, max(hl, 8), half), F32),
            pltpu.VMEM((2, max(hl, 8), half), F32),
            pltpu.VMEM((nh, rows, MODEL_WIDTH), BF),
            pltpu.VMEM((nh, rows, MODEL_WIDTH), BF),
            pltpu.SemaphoreType.DMA((2, nh)),
            pltpu.SemaphoreType.DMA((3, nb)),
            pltpu.SemaphoreType.DMA((nb,)),
            pltpu.SemaphoreType.DMA((2, nb)),
            pltpu.SemaphoreType.DMA((nb,)),
            pltpu.SemaphoreType.DMA((2, nh)),
        ],
        compiler_params=pltpu.CompilerParams(collective_id=1, vmem_limit_bytes=48 * 2**20),
        name="front",
    )(inputs, w_norm1, w_norm2, w_own, place_row, place_col, cos, sin, begin)


def seq_begin(token_position, lengths):
    starts = jnp.cumsum(lengths) - lengths
    inside = token_position[:, None] >= starts[None, 1:]
    return jnp.sum(jnp.where(inside, lengths[None, :-1], 0), axis=1)


def rotation_rows(token_position, begin_index):
    half = HEAD_SIZE // 2
    freq = jnp.exp(
        jnp.arange(half, dtype=F32) * (-2.0 * math.log(rope_base) / HEAD_SIZE)
    )
    angle = freq[:, None] * (token_position - begin_index).astype(F32)[None, :]
    return jnp.cos(angle), jnp.sin(angle)


def head_inputs(nb, nh, rows, token_place, lengths, w_query, key_weight, value_weight, w_out):
    group, half = rows * nh, rows * nh // 2
    b = lax.axis_index("blk")
    own = lax.dynamic_slice_in_dim(token_place, b * group, group)
    s = jnp.arange(group, dtype=jnp.int32)
    in_order = jnp.where(s < half, b * half + s, (2 * nb - 1 - b) * half + s - half)
    begin_s = seq_begin(in_order, lengths)
    cos_o, sin_o = rotation_rows(own, seq_begin(own, lengths))
    cos_s, sin_s = rotation_rows(in_order, begin_s)
    w_own = jnp.concatenate([w_query, key_weight, value_weight, w_out.T], axis=1)
    return own, begin_s.reshape(2, 1, half), cos_o, sin_o, cos_s, sin_s, w_own


class Scatter:
    def __init__(self, at, sib_out, sib_in, z_out, z_in, sems):
        self.at, self.sib_out, self.sib_in, self.z_out, self.z_in = at, sib_out, sib_in, z_out, z_in
        self.sems = sems

    def across(self, z):
        return remote(
            self.sib_out.at[z],
            self.sib_in.at[z],
            self.sems.at[0, z],
            self.sems.at[1, z],
            self.at.in_blk(self.at.sibling),
        )

    def along(self, z):
        return remote(
            self.z_out.at[z],
            self.z_in.at[self.at.z],
            self.sems.at[2, z],
            self.sems.at[3, self.at.z],
            self.at.in_blk(2 * z + self.at.core),
        )

    def give_sibling(self, z, value):
        self.sib_out[z] = value.astype(BF)
        self.across(z).start()

    def from_sibling(self, z):
        self.across(z).wait_recv()
        return self.sib_in[z].astype(F32)

    def give(self, z, value):
        self.z_out[z] = value.astype(BF)
        self.along(z).start()

    def taken(self, z):
        remote(
            self.z_out.at[z],
            self.z_in.at[z],
            self.sems.at[2, z],
            self.sems.at[3, z],
            self.at.in_blk(2 * z + self.at.core),
        ).wait_recv()
        return self.z_in[z].astype(F32)

    def finish(self):
        at = self.at
        for z in range(at.nz):
            self.across(z).wait_send()
            pl.when(at.z != z)(lambda: self.along(z).wait_send())


class Total:
    def __init__(self, at, part, by_head, by_blk, whole, sems):
        self.at, self.part, self.by_head, self.by_blk, self.whole = at, part, by_head, by_blk, whole
        self.sems = sems

    def copy(self, stage, k):
        at = self.at
        peer = at.blk_peer(k) if stage == 1 else at.head_peer(k)
        device = at.in_blk(peer) if stage == 1 else at.in_head(peer)
        if stage == 0:
            src, dst = self.part.at[peer], self.by_head.at[at.h]
        elif stage == 1:
            src, dst = self.by_blk.at[at.b], self.by_blk.at[at.b]
        else:
            src, dst = self.whole.at[at.h], self.whole.at[at.h]
        return remote(src, dst, self.sems.at[0, stage, k], self.sems.at[1, stage, k], device)

    def peers(self, stage):
        return range(1, self.at.nb if stage == 1 else self.at.nh)

    def begin(self, stage):
        at = self.at
        if stage == 0:
            self.by_head[at.h] = self.part[at.h]
        elif stage == 1:
            self.by_blk[at.b] = sum_slots(self.by_head, at.nh)
        else:
            self.whole[at.h] = sum_slots(self.by_blk, at.nb)
        for k in self.peers(stage):
            self.copy(stage, k).start()

    def end(self, stage):
        for k in self.peers(stage):
            self.copy(stage, k).wait_recv()

    def finish(self):
        for stage in range(3):
            for k in self.peers(stage):
                self.copy(stage, k).wait_send()


def sum_slots(ref, n):
    total = ref[0]
    for s in range(1, n):
        total = total + ref[s]
    return total


def back_kernel(
    nb,
    nh,
    hl,
    kl,
    inputs,
    w_norm1,
    d_middle,
    wg,
    xg,
    ao_t,
    qt,
    kv,
    lse,
    attn_t,
    place_row,
    place_col,
    cos,
    sin,
    begin,
    small,
    grad_in,
    grad_w,
    grad_n1,
    small_sum,
    dbg,
    perm,
    d_rows_ref,
    do_t,
    delta,
    dq_t,
    own_kv,
    kv_bufs,
    w_part,
    w_bufs,
    out_send,
    out_recv,
    n1_head,
    n1_blk,
    s_head,
    s_blk,
    d_sems,
    kv_sems,
    w_sems,
    o_sems,
    n_sems,
    s_sems,
):
    at = Place(nb, nh)
    nz = at.nz
    rows = inputs.shape[0]
    group = rows * nh
    half = group // 2
    qw, kw = hl * HEAD_SIZE, kl * HEAD_SIZE
    width = qw + 2 * kw
    dl = MODEL_WIDTH // nb
    scale = 1.0 / math.sqrt(HEAD_SIZE)

    dbg[at.h] = d_middle[...].astype(BF)
    at.meet()
    d_copies = [
        remote(dbg.at[at.h], dbg.at[at.h], d_sems.at[0, k], d_sems.at[1, k], at.in_head(at.head_peer(k)))
        for k in range(1, nh)
    ]
    for c in d_copies:
        c.start()
    totals = Total(at, small, s_head, s_blk, small_sum, s_sems)
    totals.begin(0)
    perm[...] = jnp.where(
        place_row[...] == sorted_place(at, half, (group, group), 0), 1.0, 0.0
    ).astype(BF)
    dq_t[...] = jnp.zeros(dq_t.shape, F32)
    for c in d_copies:
        c.wait_recv()
    totals.end(0)
    totals.begin(1)
    d_branch = dbg[...].reshape(group, MODEL_WIDTH)
    w = wg[...].reshape(MODEL_WIDTH, width + qw)
    d_attn_t = nn(d_branch, w[:, width:]).T.astype(BF)
    d_sorted = nt(d_attn_t, perm[...])
    for second in range(2):
        piece = d_sorted[:, second * half : (second + 1) * half]
        do_t[second] = piece.astype(BF)
        product = piece * attn_t[second]
        delta[second, :hl] = jnp.concatenate(
            [
                jnp.sum(product[a * HEAD_SIZE : (a + 1) * HEAD_SIZE], axis=0, keepdims=True)
                for a in range(hl)
            ],
            axis=0,
        )

    def step_back(p, second):
        block = kv[p, second]
        lse_all, delta_all = lse[second], delta[second]
        key_place = block_base(at, p, second, half) + lax.broadcasted_iota(
            jnp.int32, (half, half), 0
        )
        own_place = block_base(at, at.b, second, half) + lax.broadcasted_iota(
            jnp.int32, (half, half), 1
        )
        allowed = (key_place <= own_place) & (key_place >= begin[second])
        d_keys, d_values = [None] * kl, [None] * kl
        for a in range(hl):
            g = a // (hl // kl)
            rows_a = slice(a * HEAD_SIZE, (a + 1) * HEAD_SIZE)
            key = block[:, g * HEAD_SIZE : (g + 1) * HEAD_SIZE]
            value = block[:, kw + g * HEAD_SIZE : kw + (g + 1) * HEAD_SIZE]
            scores = jnp.where(allowed, nn(key, qt[second, rows_a]), -1e30)
            probs = jnp.exp(scores - lse_all[a : a + 1])
            d_probs = nn(value, do_t[second, rows_a])
            d_scores = (probs * (d_probs - delta_all[a : a + 1])).astype(BF)
            d_key = nt(qt[second, rows_a], d_scores)
            d_value = nt(do_t[second, rows_a], probs.astype(BF))
            d_keys[g] = d_key if d_keys[g] is None else d_keys[g] + d_key
            d_values[g] = d_value if d_values[g] is None else d_values[g] + d_value
            dq_t[second, rows_a] += tn(key, d_scores)
        return jnp.concatenate(d_keys + d_values, axis=0)

    scatter = Scatter(at, *(kv_bufs.at[j] for j in range(4)), kv_sems)

    def visit(step, unused):
        i = nz - 1 - step // 4
        second = lax.rem(step // 2, 2)
        same = lax.rem(step, 2) == 1
        z = jnp.where(second == 0, at.z - i, at.z + i)
        p = 2 * z + jnp.where(same, at.core, 1 - at.core)
        exists = (z >= 0) & (z < nz) & ((i > 0) | same | (at.core != second))

        @pl.when(exists)
        def _():
            part = step_back(p, second)

            @pl.when(jnp.logical_not(same))
            def _():
                scatter.give_sibling(z, part)

            @pl.when(same & (i > 0))
            def _():
                scatter.give(z, part + scatter.from_sibling(z))

            @pl.when(same & (i == 0))
            def _():
                own_kv[second] = part

        return 0

    lax.fori_loop(0, 4 * nz, visit, 0)
    totals.end(1)
    totals.begin(2)
    wide = 256

    def weight_part(first, left):
        for c in range(MODEL_WIDTH // wide):
            source = xg if first == 0 else dbg
            piece = nn(left, source[:, :, c * wide : (c + 1) * wide].reshape(group, wide))
            for j in range(wide // dl):
                w_part[c * (wide // dl) + j, first : first + left.shape[0]] = piece[
                    :, j * dl : (j + 1) * dl
                ]

    weight_part(width, ao_t[...])
    own_kv[at.core] += scatter.from_sibling(at.z)
    for z in range(nz):

        @pl.when(at.z != z)
        def _():
            own_kv[jnp.where(at.z < z, 0, 1)] += scatter.taken(z)

    d_sorted_t = []
    for second in range(2):
        cols = slice(second * half, (second + 1) * half)
        both = own_kv[second]
        turned = jnp.concatenate([dq_t[second] * scale, both[:kw]], axis=0)
        turned = turn_rows(turned, cos[:, cols], -sin[:, cols])
        d_sorted_t.append(jnp.concatenate([turned, both[kw:]], axis=0).astype(BF))
    back = jnp.where(place_col[...] == sorted_place(at, half, (group, group), 1), 1.0, 0.0).astype(BF)
    d_rows = (
        nt(back[:, :half], d_sorted_t[0]) + nt(back[:, half:], d_sorted_t[1])
    ).astype(BF)
    d_rows_ref[...] = d_rows.reshape(nh, rows, width)
    d_cols = (nn(d_sorted_t[0], perm[:half]) + nn(d_sorted_t[1], perm[half:])).astype(BF)
    o_copies = []
    for k in range(1, nh):
        peer = at.head_peer(k)
        out_send[peer] = nt(d_rows_ref[peer], w[:, :width]).astype(BF)
        c = remote(
            out_send.at[peer], out_recv.at[at.h], o_sems.at[0, k], o_sems.at[1, k], at.in_head(peer)
        )
        c.start()
        o_copies.append(c)
    own_normed = nt(d_rows_ref[at.h], w[:, :width])
    weight_part(0, d_cols)
    w_scatter = Scatter(at, *(w_bufs.at[j] for j in range(4)), w_sems)

    def w_sib(step, unused):
        z = lax.rem(at.z + 1 + step, nz)
        w_scatter.give_sibling(z, w_part[2 * z + 1 - at.core])
        return 0

    lax.fori_loop(0, nz, w_sib, 0)

    def w_along(step, unused):
        z = lax.rem(at.z + 1 + step, nz)
        w_scatter.give(z, w_part[2 * z + at.core] + w_scatter.from_sibling(z))
        return 0

    lax.fori_loop(0, nz - 1, w_along, 0)
    for k in range(1, nh):
        o_copies[k - 1].wait_recv()
        own_normed = own_normed + out_recv[lax.rem(at.h + nh - k, nh)].astype(F32)
    hidden = inputs[...].astype(F32)
    factor = lax.rsqrt(jnp.mean(hidden * hidden, axis=-1, keepdims=True) + eps)
    unit = hidden * factor
    n1_head[at.h] = jnp.sum(own_normed * unit, axis=0, keepdims=True)
    n1_copies = [
        remote(n1_head.at[at.h], n1_head.at[at.h], n_sems.at[0, k], n_sems.at[1, k], at.in_head(at.head_peer(k)))
        for k in range(1, nh)
    ]
    for c in n1_copies:
        c.start()
    weighted = own_normed * w_norm1[...]
    grad_in[...] = d_middle[...] + factor * (
        weighted - unit * jnp.mean(unit * weighted, axis=-1, keepdims=True)
    )
    for c in n1_copies:
        c.wait_recv()
    n1_blk[at.b] = sum_slots(n1_head, nh)
    n1_blk_copies = [
        remote(n1_blk.at[at.b], n1_blk.at[at.b], n_sems.at[0, nh + k], n_sems.at[1, nh + k], at.in_blk(at.blk_peer(k)))
        for k in range(1, nb)
    ]
    for c in n1_blk_copies:
        c.start()
    total_w = w_part[at.b] + w_scatter.from_sibling(at.z)
    grad_w[...] = total_w
    for z in range(nz):

        @pl.when(at.z != z)
        def _():
            grad_w[...] += w_scatter.taken(z)

    for c in n1_blk_copies:
        c.wait_recv()
    grad_n1[...] = sum_slots(n1_blk, nb)
    totals.end(2)
    totals.finish()
    scatter.finish()
    w_scatter.finish()
    for c in d_copies + o_copies + n1_copies + n1_blk_copies:
        c.wait_send()


def back(nb, nh, hl, kl, *operands):
    inputs, kv, small = operands[0], operands[7], operands[15]
    rows = inputs.shape[0]
    group, half = rows * nh, rows * nh // 2
    nz, dl = nb // 2, MODEL_WIDTH // nb
    qw, kw = hl * HEAD_SIZE, kl * HEAD_SIZE
    width = qw + 2 * kw
    shape = jax.ShapeDtypeStruct
    chunk = small.shape[1:]
    return pl.pallas_call(
        functools.partial(back_kernel, nb, nh, hl, kl),
        out_shape=(
            shape((rows, MODEL_WIDTH), F32),
            shape((width + qw, dl), F32),
            shape((1, MODEL_WIDTH), F32),
            shape((nh,) + chunk, F32),
        ),
        in_specs=[VMEM] * 16,
        out_specs=[VMEM] * 4,
        scratch_shapes=[
            pltpu.VMEM((nh, rows, MODEL_WIDTH), BF),
            pltpu.VMEM((group, group), BF),
            pltpu.VMEM((nh, rows, width), BF),
            pltpu.VMEM((2, qw, half), BF),
            pltpu.VMEM((2, max(hl, 8), half), F32),
            pltpu.VMEM((2, qw, half), F32),
            pltpu.VMEM((2, 2 * kw, half), F32),
            pltpu.VMEM((4, nz, 2 * kw, half), BF),
            pltpu.VMEM((nb, width + qw, dl), F32),
            pltpu.VMEM((4, nz, width + qw, dl), BF),
            pltpu.VMEM((nh, rows, MODEL_WIDTH), BF),
            pltpu.VMEM((nh, rows, MODEL_WIDTH), BF),
            pltpu.VMEM((nh, 1, MODEL_WIDTH), F32),
            pltpu.VMEM((nb, 1, MODEL_WIDTH), F32),
            pltpu.VMEM((nh,) + chunk, F32),
            pltpu.VMEM((nb,) + chunk, F32),
            pltpu.SemaphoreType.DMA((2, nh)),
            pltpu.SemaphoreType.DMA((4, nz)),
            pltpu.SemaphoreType.DMA((4, nz)),
            pltpu.SemaphoreType.DMA((2, nh)),
            pltpu.SemaphoreType.DMA((2, nh + nb)),
            pltpu.SemaphoreType.DMA((2, 3, max(nh, nb))),
        ],
        compiler_params=pltpu.CompilerParams(collective_id=2, vmem_limit_bytes=56 * 2**20),
        name="back",
    )(*operands)


def slot_numbers(routes, slot_order):
    flat_expert = routes.reshape(-1)
    rank = slot_order.reshape(-1)
    count = flat_expert.shape[0]
    by_rank = jnp.zeros((count,), jnp.int32).at[rank].set(jnp.arange(count, dtype=jnp.int32))
    expert_sorted = flat_expert[by_rank]
    onehot = (expert_sorted[:, None] == jnp.arange(E, dtype=jnp.int32)[None, :]).astype(jnp.int32)
    before = jnp.cumsum(onehot, axis=0) - onehot
    slot_sorted = jnp.sum(before * onehot, axis=1)
    slot = slot_sorted[rank].reshape(routes.shape)
    return (slot, slot < CAP)


def along_rows(left, right):
    return lax.dot_general(
        left, right, (((0,), (0,)), ((), ())), preferred_element_type=jnp.float32
    )


def against(left, right):
    return lax.dot_general(
        left, right, (((1,), (1,)), ((), ())), preferred_element_type=jnp.float32
    )


def fetch_experts(w_gate, w_up, w_down):
    return (
        lax.all_gather(w_gate, "blk", axis=1, tiled=True),
        lax.all_gather(w_up, "blk", axis=1, tiled=True),
        lax.all_gather(w_down, "blk", axis=2, tiled=True),
    )


def on_device(
    inputs,
    token_place,
    lengths,
    w_norm1,
    w_query,
    key_weight,
    value_weight,
    w_out,
    w_norm2,
    router,
    routes,
    slot_order,
    w_gate,
    w_up,
    w_down,
    grad_out,
):
    rows = inputs.shape[0]
    blk_count = lax.axis_size("blk")
    head_count = lax.axis_size("head")
    group_rows = rows * head_count
    heads_local = w_query.shape[1] // HEAD_SIZE
    kv_local = key_weight.shape[1] // HEAD_SIZE
    head_groups = heads_local // kv_local
    experts_local = E // head_count
    scale = 1.0 / math.sqrt(HEAD_SIZE)
    gate_all, up_all, down_all = fetch_experts(w_gate, w_up, w_down)
    own, begin_s, cos_o, sin_o, cos_s, sin_s, w_own = head_inputs(
        blk_count, head_count, rows, token_place, lengths, w_query, key_weight, value_weight, w_out
    )
    gain_one = w_norm1.reshape(1, -1)
    place_row, place_col = own.reshape(1, -1), own.reshape(-1, 1)
    sizes = (blk_count, head_count, heads_local, kv_local)
    gathered, weights, turned_q, kv, lse, attn_t, ao_t, middle, normed_two = front(
        *sizes, inputs, gain_one, w_norm2.reshape(1, -1), w_own, place_row, place_col, cos_o, sin_o, begin_s
    )
    scale_two = lax.rsqrt(jnp.mean(middle * middle, axis=-1, keepdims=True) + eps)
    unit_two = middle * scale_two
    logits = jnp.dot(normed_two, router, preferred_element_type=jnp.float32)
    chosen = jnp.take_along_axis(logits, routes, axis=1)
    shifted = jnp.exp(chosen - jnp.max(chosen, axis=-1, keepdims=True))
    gates = shifted / jnp.sum(shifted, axis=-1, keepdims=True)
    slot, kept = slot_numbers(routes, slot_order)
    target = routes * CAP + slot
    slot_ids = jnp.arange(E * CAP, dtype=jnp.int32)
    match = (target[None, :, :] == slot_ids[:, None, None]) & kept[None, :, :]
    dispatch = jnp.any(match, axis=-1).astype(jnp.bfloat16)
    buffer = jnp.dot(dispatch, normed_two, preferred_element_type=jnp.float32).astype(jnp.bfloat16)
    arrived = lax.all_to_all(
        buffer.reshape(head_count, experts_local, CAP, MODEL_WIDTH),
        "head",
        split_axis=0,
        concat_axis=0,
        tiled=True,
    )
    gate_pre = jnp.einsum("secd,edf->secf", arrived, gate_all, preferred_element_type=jnp.float32)
    up_pre = jnp.einsum("secd,edf->secf", arrived, up_all, preferred_element_type=jnp.float32)
    sigma = jax.nn.sigmoid(gate_pre)
    swish = gate_pre * sigma
    activated = (swish * up_pre).astype(jnp.bfloat16)
    expert_out = jnp.einsum(
        "secf,efd->secd", activated, down_all, preferred_element_type=jnp.float32
    ).astype(jnp.bfloat16)
    returned = lax.all_to_all(expert_out, "head", split_axis=0, concat_axis=0, tiled=True).reshape(
        E * CAP, MODEL_WIDTH
    )
    picked = returned[jnp.where(kept, target, 0)].astype(jnp.float32)
    mixed = jnp.sum(jnp.where(kept, gates, 0.0)[..., None] * picked, axis=1)
    output = (middle + mixed).astype(jnp.bfloat16)
    upstream = grad_out.astype(jnp.float32)
    d_gates = jnp.where(kept, jnp.sum(picked * upstream[:, None, :], axis=-1), 0.0)
    token_ids = jnp.broadcast_to(jnp.arange(rows, dtype=jnp.int32)[:, None], (rows, TOPK))
    slot_token = jnp.sum(jnp.where(match, token_ids[None], 0), axis=(1, 2))
    slot_gate = jnp.sum(jnp.where(match, gates[None], 0.0), axis=(1, 2))
    d_slots = (slot_gate[:, None] * upstream[slot_token]).astype(jnp.bfloat16)
    d_returned = lax.all_to_all(
        d_slots.reshape(head_count, experts_local, CAP, MODEL_WIDTH),
        "head",
        split_axis=0,
        concat_axis=0,
        tiled=True,
    )
    d_activated = jnp.einsum(
        "secd,efd->secf", d_returned, down_all, preferred_element_type=jnp.float32
    )
    d_gate_pre = (d_activated * up_pre * sigma * (1.0 + gate_pre * (1.0 - sigma))).astype(
        jnp.bfloat16
    )
    d_up_pre = (d_activated * swish).astype(jnp.bfloat16)
    d_arrived = jnp.einsum(
        "secf,edf->secd", d_gate_pre, gate_all, preferred_element_type=jnp.float32
    )
    d_arrived = (
        d_arrived
        + jnp.einsum("secf,edf->secd", d_up_pre, up_all, preferred_element_type=jnp.float32)
    ).astype(jnp.bfloat16)
    d_buffer = lax.all_to_all(d_arrived, "head", split_axis=0, concat_axis=0, tiled=True).reshape(
        E * CAP, MODEL_WIDTH
    )
    d_normed_two = along_rows(dispatch, d_buffer)
    weighted = jnp.sum(gates * d_gates, axis=-1, keepdims=True)
    d_chosen = gates * (d_gates - weighted)
    route_hits = routes[..., None] == jnp.arange(E, dtype=jnp.int32)[None, None, :]
    d_logits = jnp.sum(jnp.where(route_hits, d_chosen[..., None], 0.0), axis=1)
    router_wide = router.astype(jnp.float32)
    d_normed_two = d_normed_two + lax.dot_general(
        d_logits, router_wide, (((1,), (1,)), ((), ())), precision=lax.Precision.HIGHEST
    )
    grad_router = lax.dot_general(
        normed_two.astype(jnp.float32),
        d_logits,
        (((0,), (0,)), ((), ())),
        precision=lax.Precision.HIGHEST,
    )
    weighted_two = d_normed_two * w_norm2
    grad_norm2 = jnp.sum(d_normed_two * unit_two, axis=0)
    d_middle = upstream + scale_two * (
        weighted_two - unit_two * jnp.mean(unit_two * weighted_two, axis=-1, keepdims=True)
    )
    small = jnp.concatenate(
        [grad_router.T, grad_norm2[None], jnp.zeros((7, MODEL_WIDTH), F32)], axis=0
    )
    small = small.reshape(40, head_count, -1).transpose(1, 0, 2)
    grad_inputs, grad_w, grad_norm1, small = back(
        *sizes, inputs, gain_one, d_middle, weights, gathered, ao_t, turned_q, kv, lse, attn_t,
        place_row, place_col, cos_s, sin_s, begin_s, small
    )
    small = small.transpose(1, 0, 2).reshape(40, MODEL_WIDTH)
    qw, kw = heads_local * HEAD_SIZE, kv_local * HEAD_SIZE
    grad_gate = jnp.einsum(
        "secd,secf->edf", arrived, d_gate_pre, preferred_element_type=jnp.float32
    )
    grad_up = jnp.einsum("secd,secf->edf", arrived, d_up_pre, preferred_element_type=jnp.float32)
    grad_down = jnp.einsum(
        "secf,secd->efd", activated, d_returned, preferred_element_type=jnp.float32
    )
    sharded = (
        lax.psum_scatter(
            grad_gate.astype(jnp.bfloat16), "blk", scatter_dimension=1, tiled=True
        ).astype(jnp.float32),
        lax.psum_scatter(
            grad_up.astype(jnp.bfloat16), "blk", scatter_dimension=1, tiled=True
        ).astype(jnp.float32),
        lax.psum_scatter(
            grad_down.astype(jnp.bfloat16), "blk", scatter_dimension=2, tiled=True
        ).astype(jnp.float32),
    )
    return (
        output,
        grad_inputs,
        grad_norm1.reshape(-1),
        grad_w[:qw].T,
        grad_w[qw : qw + kw].T,
        grad_w[qw + kw : qw + 2 * kw].T,
        grad_w[qw + 2 * kw :],
        small[32],
        small[:32].T,
        sharded[0],
        sharded[1],
        sharded[2],
    )


def solution(mesh):
    return jax.shard_map(
        on_device,
        mesh=mesh,
        in_specs=(
            P(("blk", "head"), None),
            P(),
            P(),
            P(),
            P("blk", "head"),
            P("blk", "head"),
            P("blk", "head"),
            P("head", "blk"),
            P(),
            P(),
            P(("blk", "head"), None),
            P(("blk", "head"), None),
            P("head", "blk", None),
            P("head", "blk", None),
            P("head", None, "blk"),
            P(("blk", "head"), None),
        ),
        out_specs=(
            P(("blk", "head"), None),
            P(("blk", "head"), None),
            P(),
            P("blk", "head"),
            P("blk", "head"),
            P("blk", "head"),
            P("head", "blk"),
            P(),
            P(),
            P("head", "blk", None),
            P("head", "blk", None),
            P("head", None, "blk"),
        ),
        check_vma=False,
    )
```

```python
import functools
import math

import jax
import jax.numpy as jnp
from jax import lax
from jax.experimental import pallas as pl
from jax.experimental.pallas import tpu as pltpu
from jax.sharding import PartitionSpec as P

MODEL_WIDTH = 1024
HEAD_SIZE = 64
E = 32
TOPK = 8
CAP = 40
MESH = pl.DeviceIdType.MESH
VMEM = pl.BlockSpec(memory_space=pltpu.VMEM)
ANY = pl.BlockSpec(memory_space=pl.ANY)
BF = jnp.bfloat16
F32 = jnp.float32

eps = 1e-06
rope_base = 10000.0


def nn(a, b, **kw):
    return lax.dot_general(a, b, (((1,), (0,)), ((), ())), preferred_element_type=F32, **kw)


def nt(a, b, **kw):
    return lax.dot_general(a, b, (((1,), (1,)), ((), ())), preferred_element_type=F32, **kw)


def tn(a, b, **kw):
    return lax.dot_general(a, b, (((0,), (0,)), ((), ())), preferred_element_type=F32, **kw)


def remote(src, dst, send, recv, device):
    return pltpu.make_async_remote_copy(
        src_ref=src,
        dst_ref=dst,
        send_sem=send,
        recv_sem=recv,
        device_id=device,
        device_id_type=MESH,
    )


class Place:
    def __init__(self, nb, nh):
        self.nb, self.nh, self.nz = nb, nh, nb // 2
        self.b, self.h = lax.axis_index("blk"), lax.axis_index("head")
        self.z, self.core = self.b // 2, lax.rem(self.b, 2)
        self.sibling = 2 * self.z + 1 - self.core

    def in_blk(self, b):
        return (b, self.h)

    def in_head(self, h):
        return (self.b, h)

    def head_peer(self, k):
        return lax.rem(self.h + k, self.nh)

    def blk_peer(self, k):
        return lax.rem(self.b + k, self.nb)

    def meet(self):
        barrier = pltpu.get_barrier_semaphore()
        for k in range(1, self.nh):
            pl.semaphore_signal(
                barrier, inc=1, device_id=self.in_head(self.head_peer(k)), device_id_type=MESH
            )
        for k in range(1, self.nb):
            pl.semaphore_signal(
                barrier, inc=1, device_id=self.in_blk(self.blk_peer(k)), device_id_type=MESH
            )
        pl.semaphore_wait(barrier, self.nh + self.nb - 2)


class Relay:
    def __init__(self, at, buf, send, recv):
        self.at, self.buf, self.send, self.recv = at, buf, send, recv

    def copy(self, s, way, device):
        return remote(
            self.buf.at[s], self.buf.at[s], self.send.at[way, s], self.recv.at[s], device
        )

    def right(self, s):
        return self.copy(s, 0, self.at.in_blk(jnp.minimum(self.at.b + 2, self.at.nb - 2 + self.at.core)))

    def left(self, s):
        return self.copy(s, 1, self.at.in_blk(jnp.maximum(self.at.b - 2, self.at.core)))

    def across(self, s):
        return self.copy(s, 2, self.at.in_blk(self.at.sibling))

    def begin(self):
        at = self.at
        pl.when(at.z + 1 < at.nz)(lambda: self.right(at.b).start())
        pl.when(at.z > 0)(lambda: self.left(at.b).start())
        self.across(at.b).start()

    def hop(self, i):
        at = self.at

        @pl.when(at.z >= i)
        def _():
            s = at.b - 2 * i
            self.across(s).wait_recv()
            pl.when(at.z + 1 < at.nz)(lambda: self.right(s).start())
            self.across(s).start()

        @pl.when(at.z + i < at.nz)
        def _():
            s = at.b + 2 * i
            self.across(s).wait_recv()
            pl.when(at.z > 0)(lambda: self.left(s).start())
            self.across(s).start()

    def take_sibling(self, z):
        self.across(2 * z + 1 - self.at.core).wait_recv()

    def finish(self):
        at = self.at
        for i in range(at.nz):

            @pl.when(at.z >= i)
            def _():
                s = at.b - 2 * i
                pl.when(at.z + 1 < at.nz)(lambda: self.right(s).wait_send())
                self.across(s).wait_send()

            if i == 0:
                pl.when(at.z > 0)(lambda: self.left(at.b).wait_send())
            else:

                @pl.when(at.z + i < at.nz)
                def _():
                    s = at.b + 2 * i
                    pl.when(at.z > 0)(lambda: self.left(s).wait_send())
                    self.across(s).wait_send()

    def all(self):
        self.begin()
        for i in range(1, self.at.nz):
            self.hop(i)
        for z in range(self.at.nz):
            self.take_sibling(z)


def sorted_place(at, half, shape, axis):
    s = lax.broadcasted_iota(jnp.int32, shape, axis)
    return jnp.where(
        s < half, at.b * half + s, (2 * at.nb - 1 - at.b) * half + s - half
    )


def block_base(at, b, second, half):
    return jnp.where(second == 0, b * half, (2 * at.nb - 1 - b) * half)


def turn_rows(values, cos, sin):
    half = HEAD_SIZE // 2
    pieces = []
    for first in range(0, values.shape[0], HEAD_SIZE):
        lead = values[first : first + half]
        trail = values[first + half : first + HEAD_SIZE]
        pieces.append(lead * cos - trail * sin)
        pieces.append(trail * cos + lead * sin)
    return jnp.concatenate(pieces, axis=0)


def pick_targets(slots, pair_rows):
    lane = lax.broadcasted_iota(jnp.int32, slots.shape, 1)
    kept = (slots >= 0) & (slots < CAP)
    return jnp.where(kept, slots + jnp.where(lane >= pair_rows // 2, CAP, 0), -1)


def hits(target_row, pair_rows):
    return lax.broadcasted_iota(jnp.int32, (2 * CAP, pair_rows), 0) == target_row


def diagonal():
    shape = (2 * CAP, 2 * CAP)
    return lax.broadcasted_iota(jnp.int32, shape, 0) == lax.broadcasted_iota(jnp.int32, shape, 1)


def to_row(column):
    return jnp.sum(jnp.where(diagonal(), column, 0.0), axis=0, keepdims=True)


def to_column(row):
    return jnp.sum(jnp.where(diagonal(), row, 0.0), axis=1, keepdims=True)


def split_product(dot, left, right):
    high = left.astype(BF)
    low = (left - high.astype(F32)).astype(BF)
    return dot(high, right) + dot(low, right)


def front_kernel(
    nb,
    nh,
    hl,
    kl,
    repeat,
    inputs,
    w_norm1,
    w_norm2,
    w_own,
    place_row,
    place_col,
    cos,
    sin,
    begin,
    grad_out,
    table,
    router_t,
    xg,
    wg,
    qt,
    kv,
    lse,
    attn_t,
    ao_t,
    middle,
    n2,
    slots,
    own_gates,
    in_gate,
    in_rows,
    in_g,
    ao,
    perm,
    top,
    total,
    out_send,
    out_recv,
    x_sems,
    w_send,
    w_recv,
    kv_send,
    kv_recv,
    o_sems,
    slot_all,
    g_all,
    n2_all,
    gates,
    out_rows,
    out_g,
    out_gate,
    s_send,
    s_recv,
    g_send,
    g_recv,
    n_send,
    n_recv,
    row_sems,
    g_sems,
    gate_sems,
    local_sems,
):
    at = Place(nb, nh)
    rows = inputs.shape[0]
    group = rows * nh
    half = group // 2
    qw, kw = hl * HEAD_SIZE, kl * HEAD_SIZE
    width = qw + 2 * kw

    hidden = inputs[...].astype(F32)
    unit = hidden * lax.rsqrt(jnp.mean(hidden * hidden, axis=-1, keepdims=True) + eps)
    xg[at.h] = (unit * w_norm1[...]).astype(BF)
    wg[at.b] = w_own[...]
    slot_all[at.b] = table[...]
    g_all[at.b] = grad_out[...]
    at.meet()
    x_copies = [
        remote(xg.at[at.h], xg.at[at.h], x_sems.at[0, k], x_sems.at[1, k], at.in_head(at.head_peer(k)))
        for k in range(1, nh)
    ]
    for c in x_copies:
        c.start()
    weights = Relay(at, wg, w_send, w_recv)
    weights.begin()
    slot_relay = Relay(at, slot_all, s_send, s_recv)
    slot_relay.begin()
    g_relay = Relay(at, g_all, g_send, g_recv)
    g_relay.begin()
    pair = 2 * rows
    own_expert = (at.b // repeat) * nh

    def go(buf_out, buf_in, sems, z, k):
        peer = at.head_peer(k)
        return remote(
            buf_out.at[z, peer],
            buf_in.at[z, at.h],
            sems.at[0, z, k],
            sems.at[1, z, k],
            at.in_head(peer),
        )

    def keep(buf_out, buf_in, j, z):
        return pltpu.make_async_copy(buf_out.at[z, at.h], buf_in.at[z, at.h], local_sems.at[j, z])

    def outward(relay, body, first, last):
        def step(t, unused):
            d, side = t // 2, lax.rem(t, 2)
            z = jnp.where(side == 0, at.z - d, at.z + d)
            pl.when((side == 0) & (d > 0))(lambda: relay.hop(d))

            @pl.when((z >= 0) & (z < at.nz) & ((d > 0) | (side == 0)))
            def _():
                relay.take_sibling(z)
                body(z)

            return 0

        lax.fori_loop(2 * first, 2 * last, step, 0)

    def send_g(z):
        x = g_all[pl.ds(2 * z, 2)].reshape(pair, MODEL_WIDTH)
        for k in list(range(1, nh)) + [0]:
            peer = at.head_peer(k)
            hit = hits(pick_targets(slots[z, pl.ds(own_expert + peer, 1)], pair), pair)
            out_g[z, peer] = nn(jnp.where(hit, 1.0, 0.0).astype(BF), x).astype(BF)
            if k == 0:
                keep(out_g, in_g, 0, z).start()
            else:
                go(out_g, in_g, g_sems, z, k).start()

    def send_rows(z):
        x = n2_all[pl.ds(2 * z, 2)].reshape(pair, MODEL_WIDTH)
        routed = slots[z] >= 0
        logits = jnp.where(routed, nt(router_t[...], x), -1e30)
        shifted = jnp.exp(logits - jnp.max(logits, axis=0, keepdims=True))
        shifted = jnp.where(routed, shifted, 0.0)
        gates[z] = shifted / jnp.sum(shifted, axis=0, keepdims=True)
        for k in list(range(1, nh)) + [0]:
            peer = at.head_peer(k)
            hit = hits(pick_targets(slots[z, pl.ds(own_expert + peer, 1)], pair), pair)
            gate_row = gates[z, pl.ds(own_expert + peer, 1)]
            gate = to_row(jnp.sum(jnp.where(hit, gate_row, 0.0), axis=1, keepdims=True))
            out_rows[z, peer] = nn(jnp.where(hit, 1.0, 0.0).astype(BF), x).astype(BF)
            if k == 0:
                keep(out_rows, in_rows, 1, z).start()
                in_gate[z, at.h] = gate
            else:
                go(out_rows, in_rows, row_sems, z, k).start()
                out_gate[z, peer] = gate
                go(out_gate, in_gate, gate_sems, z, k).start()

    perm[...] = jnp.where(
        place_row[...] == sorted_place(at, half, (group, group), 0), 1.0, 0.0
    ).astype(BF)
    for i in range(1, nb // 2):
        slot_relay.hop(i)
        weights.hop(i)
    for z in range(nb // 2):
        slot_relay.take_sibling(z)
    for z in range(nb // 2):
        slots[z] = jnp.concatenate([slot_all[2 * z], slot_all[2 * z + 1]], axis=1)
    outward(g_relay, send_g, 0, 1)
    for z in range(nb // 2):
        weights.take_sibling(z)
    for c in x_copies:
        c.wait_recv()
    x = xg[...].reshape(group, MODEL_WIDTH)
    w = wg[...].reshape(MODEL_WIDTH, width + qw)
    qkv_t = nn(x, w[:, :width]).T
    qkv_t = jnp.concatenate(
        [turn_rows(qkv_t[: qw + kw], cos[...], sin[...]), qkv_t[qw + kw :]], axis=0
    ).astype(BF)
    order = perm[...]
    kv_rows = nt(order, qkv_t[qw:]).astype(BF)
    kv[at.b, 0] = kv_rows[:half]
    kv[at.b, 1] = kv_rows[half:]

    def kv_copy(p, second, way, device):
        return remote(
            kv.at[p, second], kv.at[p, second], kv_send.at[way, p], kv_recv.at[p], device
        )

    right = at.in_blk(jnp.minimum(at.b + 2, nb - 2 + at.core))
    left = at.in_blk(jnp.maximum(at.b - 2, at.core))
    across = at.in_blk(at.sibling)
    pl.when(at.z + 1 < at.nz)(lambda: kv_copy(at.b, 0, 0, right).start())
    pl.when(at.z > 0)(lambda: kv_copy(at.b, 1, 0, left).start())
    kv_copy(at.b, at.core, 1, across).start()
    q_cols = (nt(qkv_t[:qw], order) * (1.0 / math.sqrt(HEAD_SIZE))).astype(BF)
    qt[0] = q_cols[:, :half]
    qt[1] = q_cols[:, half:]
    outward(g_relay, send_g, 1, 2)
    top[...] = jnp.full(top.shape, -1e30, F32)
    total[...] = jnp.zeros(total.shape, F32)
    attn_t[...] = jnp.zeros(attn_t.shape, F32)

    def attend(p, second):
        old_top, old_total = top[second], total[second]
        tops, totals = [], []
        block = kv[p, second]
        key_place = block_base(at, p, second, half) + lax.broadcasted_iota(
            jnp.int32, (half, half), 0
        )
        own_place = block_base(at, at.b, second, half) + lax.broadcasted_iota(
            jnp.int32, (half, half), 1
        )
        allowed = (key_place <= own_place) & (key_place >= begin[second])
        for a in range(hl):
            g = a // (hl // kl)
            rows_a = slice(a * HEAD_SIZE, (a + 1) * HEAD_SIZE)
            scores = nn(block[:, g * HEAD_SIZE : (g + 1) * HEAD_SIZE], qt[second, rows_a])
            scores = jnp.where(allowed, scores, -1e30)
            old = old_top[a : a + 1]
            new = jnp.maximum(old, jnp.max(scores, axis=0, keepdims=True))
            probs = jnp.exp(scores - new)
            fade = jnp.exp(old - new)
            totals.append(old_total[a : a + 1] * fade + jnp.sum(probs, axis=0, keepdims=True))
            tops.append(new)
            attn_t[second, rows_a] = attn_t[second, rows_a] * fade + tn(
                block[:, kw + g * HEAD_SIZE : kw + (g + 1) * HEAD_SIZE], probs.astype(BF)
            )
        top[second, :hl] = jnp.concatenate(tops, axis=0)
        total[second, :hl] = jnp.concatenate(totals, axis=0)

    def visit(step, unused):
        i = step // 4
        second = lax.rem(step, 2)
        same = lax.rem(step // 2, 2) == 0
        z = jnp.where(second == 0, at.z - i, at.z + i)
        p = 2 * z + jnp.where(same, at.core, 1 - at.core)
        exists = (z >= 0) & (z < nb // 2) & ((i > 0) | same | (at.core != second))

        @pl.when(exists)
        def _():
            @pl.when(p != at.b)
            def _():
                kv_copy(p, second, 1, across).wait_recv()

            @pl.when((i > 0) & same)
            def _():
                @pl.when((second == 0) & (at.z + 1 < at.nz))
                def _():
                    kv_copy(p, second, 0, right).start()

                @pl.when((second == 1) & (at.z > 0))
                def _():
                    kv_copy(p, second, 0, left).start()

                kv_copy(p, second, 1, across).start()

            attend(p, second)

        return 0

    lax.fori_loop(0, 4 * (nb // 2), visit, 0)
    for second in range(2):
        sums = total[second]
        for a in range(hl):
            rows_a = slice(a * HEAD_SIZE, (a + 1) * HEAD_SIZE)
            attn_t[second, rows_a] = attn_t[second, rows_a] / sums[a : a + 1]
    lse[...] = top[...] + jnp.log(total[...])
    back = jnp.where(place_col[...] == sorted_place(at, half, (group, group), 1), 1.0, 0.0).astype(BF)
    attn_rows = (
        nt(back[:, :half], attn_t[0].astype(BF)) + nt(back[:, half:], attn_t[1].astype(BF))
    ).astype(BF)
    ao[...] = attn_rows
    ao_t[...] = (
        nn(attn_t[0].astype(BF), perm[:half]) + nn(attn_t[1].astype(BF), perm[half:])
    ).astype(BF)
    o_copies = []
    for k in range(nh):
        peer = at.head_peer(k)
        chunk = nt(ao[pl.ds(peer * rows, rows)], w[:, width:])
        if k == 0:
            middle[...] = hidden + chunk
            continue
        out_send[peer] = chunk.astype(BF)
        c = remote(
            out_send.at[peer], out_recv.at[at.h], o_sems.at[0, k], o_sems.at[1, k], at.in_head(peer)
        )
        c.start()
        o_copies.append(c)
    outward(g_relay, send_g, 2, at.nz)
    for k in range(1, nh):
        o_copies[k - 1].wait_recv()
        middle[...] += out_recv[lax.rem(at.h + nh - k, nh)].astype(F32)
    mid = middle[...]
    n2[...] = (
        mid * lax.rsqrt(jnp.mean(mid * mid, axis=-1, keepdims=True) + eps) * w_norm2[...]
    ).astype(BF)
    n2_all[at.b] = n2[...]
    n_relay = Relay(at, n2_all, n_send, n_recv)
    n_relay.begin()
    outward(n_relay, send_rows, 0, at.nz)
    own_gates[...] = jnp.where(at.core == 0, gates[at.z, :, :rows], gates[at.z, :, rows:])
    for relay in (weights, slot_relay, g_relay, n_relay):
        relay.finish()
    for c in x_copies + o_copies:
        c.wait_send()

    def drain(step, unused):
        i = step // 2
        second = lax.rem(step, 2)
        z = jnp.where(second == 0, at.z - i, at.z + i)
        p = 2 * z + at.core

        @pl.when((z >= 0) & (z < nb // 2))
        def _():
            @pl.when((second == 0) & (at.z + 1 < at.nz))
            def _():
                kv_copy(p, second, 0, right).wait_send()

            @pl.when((second == 1) & (at.z > 0))
            def _():
                kv_copy(p, second, 0, left).wait_send()

            @pl.when((i > 0) | (second == at.core))
            def _():
                kv_copy(p, second, 1, across).wait_send()

        return 0

    lax.fori_loop(0, nb, drain, 0)

    def end(z, unused):
        for k in range(1, nh):
            for move in (
                go(out_g, in_g, g_sems, z, k),
                go(out_rows, in_rows, row_sems, z, k),
                go(out_gate, in_gate, gate_sems, z, k),
            ):
                move.wait_recv()
                move.wait_send()
        keep(out_g, in_g, 0, z).wait()
        keep(out_rows, in_rows, 1, z).wait()
        return 0

    lax.fori_loop(0, at.nz, end, 0)


def front(nb, nh, hl, kl, repeat, *operands):
    inputs, w_own = operands[0], operands[3]
    rows = inputs.shape[0]
    group, half = rows * nh, rows * nh // 2
    nz = nb // 2
    dl, wide = w_own.shape
    qw, kw = hl * HEAD_SIZE, kl * HEAD_SIZE
    shape = jax.ShapeDtypeStruct
    dma = pltpu.SemaphoreType.DMA
    chunk = (nz, nh, 2 * CAP, MODEL_WIDTH)
    line = (nz, nh, 1, 2 * CAP)
    relay_sems = [dma((3, nb)), dma((nb,))]
    return pl.pallas_call(
        functools.partial(front_kernel, nb, nh, hl, kl, repeat),
        out_shape=(
            shape((nh, rows, MODEL_WIDTH), BF),
            shape((nb, dl, wide), BF),
            shape((2, qw, half), BF),
            shape((nb, 2, half, 2 * kw), BF),
            shape((2, max(hl, 8), half), F32),
            shape((2, qw, half), F32),
            shape((qw, group), BF),
            shape((rows, MODEL_WIDTH), F32),
            shape((rows, MODEL_WIDTH), BF),
            shape((nz, E, 2 * rows), jnp.int32),
            shape((E, rows), F32),
            shape(line, F32),
            shape(chunk, BF),
            shape(chunk, BF),
        ),
        in_specs=[VMEM] * 12,
        out_specs=[VMEM] * 12 + [ANY] * 2,
        scratch_shapes=[
            pltpu.VMEM((group, qw), BF),
            pltpu.VMEM((group, group), BF),
            pltpu.VMEM((2, max(hl, 8), half), F32),
            pltpu.VMEM((2, max(hl, 8), half), F32),
            pltpu.VMEM((nh, rows, MODEL_WIDTH), BF),
            pltpu.VMEM((nh, rows, MODEL_WIDTH), BF),
            dma((2, nh)),
            dma((3, nb)),
            dma((nb,)),
            dma((2, nb)),
            dma((nb,)),
            dma((2, nh)),
            pltpu.VMEM((nb, E, rows), jnp.int32),
            pltpu.VMEM((nb, rows, MODEL_WIDTH), BF),
            pltpu.VMEM((nb, rows, MODEL_WIDTH), BF),
            pltpu.VMEM((nz, E, 2 * rows), F32),
            pltpu.VMEM(chunk, BF),
            pltpu.VMEM(chunk, BF),
            pltpu.VMEM(line, F32),
            *relay_sems,
            *relay_sems,
            *relay_sems,
            dma((2, nz, nh)),
            dma((2, nz, nh)),
            dma((2, nz, nh)),
            dma((2, nz)),
        ],
        compiler_params=pltpu.CompilerParams(collective_id=1, vmem_limit_bytes=60 * 2**20),
        name="front",
    )(*operands)


def seq_begin(token_position, lengths):
    starts = jnp.cumsum(lengths) - lengths
    inside = token_position[:, None] >= starts[None, 1:]
    return jnp.sum(jnp.where(inside, lengths[None, :-1], 0), axis=1)


def rotation_rows(token_position, begin_index):
    half = HEAD_SIZE // 2
    freq = jnp.exp(
        jnp.arange(half, dtype=F32) * (-2.0 * math.log(rope_base) / HEAD_SIZE)
    )
    angle = freq[:, None] * (token_position - begin_index).astype(F32)[None, :]
    return jnp.cos(angle), jnp.sin(angle)


def head_inputs(nb, nh, rows, token_place, lengths, w_query, key_weight, value_weight, w_out):
    group, half = rows * nh, rows * nh // 2
    b = lax.axis_index("blk")
    own = lax.dynamic_slice_in_dim(token_place, b * group, group)
    s = jnp.arange(group, dtype=jnp.int32)
    in_order = jnp.where(s < half, b * half + s, (2 * nb - 1 - b) * half + s - half)
    begin_s = seq_begin(in_order, lengths)
    cos_o, sin_o = rotation_rows(own, seq_begin(own, lengths))
    cos_s, sin_s = rotation_rows(in_order, begin_s)
    w_own = jnp.concatenate([w_query, key_weight, value_weight, w_out.T], axis=1)
    return own, begin_s.reshape(2, 1, half), cos_o, sin_o, cos_s, sin_s, w_own


def slot_table(nb, nh, repeat, routes, slot_order):
    local = E // nh
    mine = (routes % local) * nh + routes // local
    match = mine.T[:, None, :] == jnp.arange(E, dtype=jnp.int32)[None, :, None]
    order = jnp.min(jnp.where(match, slot_order.T[:, None, :], 1 << 20), axis=0)
    before = jnp.sum((order[:, :, None] < order[:, None, :]).astype(jnp.int32), axis=1)
    return jnp.where(order < (1 << 20), before, -1)


def experts_kernel(nz, nh, x_ref, g_ref, gate_ref, w, d_rows, scaled, d_gate_row, grads, sums):
    step = pl.program_id(0)
    fr = w.shape[-1]
    nb, dl = grads.shape[0], grads.shape[2]

    @pl.when(step == 0)
    def _():
        sums[...] = jnp.zeros(sums.shape, F32)

    x = x_ref[0].reshape(nh * 2 * CAP, MODEL_WIDTH)
    gate = jnp.concatenate([to_column(gate_ref[0, h]) for h in range(nh)], axis=0)
    w_gate = w[:, 0].reshape(MODEL_WIDTH, fr)
    w_up = w[:, 1].reshape(MODEL_WIDTH, fr)
    w_down_t = w[:, 2].reshape(MODEL_WIDTH, fr)
    gate_pre, up_pre = nn(x, w_gate), nn(x, w_up)
    sigma = 1.0 / (1.0 + jnp.exp(-gate_pre))
    swish = gate_pre * sigma
    activated = (swish * up_pre).astype(BF)
    out = nt(activated, w_down_t).astype(BF).astype(F32)
    g = g_ref[0].reshape(nh * 2 * CAP, MODEL_WIDTH).astype(F32)
    d_gate = jnp.sum(out * g, axis=1, keepdims=True)
    d_out = (gate * g).astype(BF)
    scaled[0] = (gate * out).astype(BF).reshape(nh, 2 * CAP, MODEL_WIDTH)
    d_act = nn(d_out, w_down_t)
    d_gate_pre = (d_act * up_pre * sigma * (1.0 + gate_pre * (1.0 - sigma))).astype(BF)
    d_up_pre = (d_act * swish).astype(BF)
    back_rows = (nt(d_gate_pre, w_gate) + nt(d_up_pre, w_up)).astype(BF)
    d_rows[0] = back_rows.reshape(nh, 2 * CAP, MODEL_WIDTH)
    for h in range(nh):
        d_gate_row[0, h] = to_row(d_gate[h * 2 * CAP : (h + 1) * 2 * CAP])
    sums[0] += tn(x, d_gate_pre)
    sums[1] += tn(x, d_up_pre)
    sums[2] += tn(d_out, activated)

    @pl.when(step == nz - 1)
    def _():
        for j in range(3):
            for p in range(nb):
                grads[p, j] = sums[j, p * dl : (p + 1) * dl].astype(BF)


def experts(nz, nh, x, g, gate, w):
    fr = w.shape[-1]
    shape = jax.ShapeDtypeStruct
    wide = pl.BlockSpec((1,) + x.shape[1:], lambda i: (i, 0, 0, 0))
    line = pl.BlockSpec((1,) + gate.shape[1:], lambda i: (i, 0, 0, 0))
    whole = pl.BlockSpec(w.shape, lambda i: (0, 0, 0, 0))
    return pl.pallas_call(
        functools.partial(experts_kernel, nz, nh),
        grid=(nz,),
        out_shape=(shape(x.shape, BF), shape(x.shape, BF), shape(gate.shape, F32), shape(w.shape, BF)),
        in_specs=[wide, wide, line, whole],
        out_specs=[wide, wide, line, whole],
        scratch_shapes=[pltpu.VMEM((3, MODEL_WIDTH, fr), F32)],
        compiler_params=pltpu.CompilerParams(vmem_limit_bytes=60 * 2**20),
        name="experts",
    )(x, g, gate, w)


class Scatter:
    def __init__(self, at, sib_out, sib_in, z_out, z_in, sems):
        self.at, self.sib_out, self.sib_in, self.z_out, self.z_in = at, sib_out, sib_in, z_out, z_in
        self.sems = sems

    def across(self, z):
        return remote(
            self.sib_out.at[z],
            self.sib_in.at[z],
            self.sems.at[0, z],
            self.sems.at[1, z],
            self.at.in_blk(self.at.sibling),
        )

    def along(self, z):
        return remote(
            self.z_out.at[z],
            self.z_in.at[self.at.z],
            self.sems.at[2, z],
            self.sems.at[3, self.at.z],
            self.at.in_blk(2 * z + self.at.core),
        )

    def give_sibling(self, z, value):
        self.sib_out[z] = value.astype(BF)
        self.across(z).start()

    def from_sibling(self, z):
        self.across(z).wait_recv()
        return self.sib_in[z].astype(F32)

    def give(self, z, value):
        self.z_out[z] = value.astype(BF)
        self.along(z).start()

    def taken(self, z):
        remote(
            self.z_out.at[z],
            self.z_in.at[z],
            self.sems.at[2, z],
            self.sems.at[3, z],
            self.at.in_blk(2 * z + self.at.core),
        ).wait_recv()
        return self.z_in[z].astype(F32)

    def finish(self):
        at = self.at
        for z in range(at.nz):
            self.across(z).wait_send()
            pl.when(at.z != z)(lambda: self.along(z).wait_send())


class Total:
    def __init__(self, at, part, by_head, by_blk, whole, sems):
        self.at, self.part, self.by_head, self.by_blk, self.whole = at, part, by_head, by_blk, whole
        self.sems = sems

    def copy(self, stage, k):
        at = self.at
        peer = at.blk_peer(k) if stage == 1 else at.head_peer(k)
        device = at.in_blk(peer) if stage == 1 else at.in_head(peer)
        if stage == 0:
            src, dst = self.part.at[peer], self.by_head.at[at.h]
        elif stage == 1:
            src, dst = self.by_blk.at[at.b], self.by_blk.at[at.b]
        else:
            src, dst = self.whole.at[at.h], self.whole.at[at.h]
        return remote(src, dst, self.sems.at[0, stage, k], self.sems.at[1, stage, k], device)

    def peers(self, stage):
        return range(1, self.at.nb if stage == 1 else self.at.nh)

    def begin(self, stage):
        at = self.at
        if stage == 0:
            self.by_head[at.h] = self.part[at.h]
        elif stage == 1:
            self.by_blk[at.b] = sum_slots(self.by_head, at.nh)
        else:
            self.whole[at.h] = sum_slots(self.by_blk, at.nb)
        for k in self.peers(stage):
            self.copy(stage, k).start()

    def end(self, stage):
        for k in self.peers(stage):
            self.copy(stage, k).wait_recv()

    def finish(self):
        for stage in range(3):
            for k in self.peers(stage):
                self.copy(stage, k).wait_send()


def sum_slots(ref, n):
    total = ref[0]
    for s in range(1, n):
        total = total + ref[s]
    return total


def back_kernel(
    nb,
    nh,
    hl,
    kl,
    repeat,
    inputs,
    w_norm1,
    w_norm2,
    middle,
    n2,
    grad_out,
    router_t,
    slots,
    own_gates,
    d_gate_rows,
    wg,
    xg,
    ao_t,
    qt,
    kv,
    lse,
    attn_t,
    place_row,
    place_col,
    cos,
    sin,
    begin,
    d_rows,
    scaled,
    output,
    grad_in,
    grad_w,
    grad_n1,
    small_sum,
    dbg,
    perm,
    d_rows_ref,
    do_t,
    delta,
    dq_t,
    own_kv,
    kv_bufs,
    w_part,
    w_bufs,
    out_send,
    out_recv,
    n1_head,
    n1_blk,
    s_head,
    s_blk,
    d_sems,
    kv_sems,
    w_sems,
    o_sems,
    n_sems,
    s_sems,
    small,
    back_rows,
    in_dgate,
    own_part,
    d_middle,
    dg_out,
    dg_in,
    sc_bufs,
    sc_sems,
    mix_sems,
    ret_sems,
    eout_sems,
    dgate_sems,
    dg_sems,
    local_sems,
):
    at = Place(nb, nh)
    nz = at.nz
    rows = inputs.shape[0]
    group = rows * nh
    half = group // 2
    qw, kw = hl * HEAD_SIZE, kl * HEAD_SIZE
    width = qw + 2 * kw
    dl = MODEL_WIDTH // nb
    scale = 1.0 / math.sqrt(HEAD_SIZE)

    pair = 2 * rows
    own_expert = (at.b // repeat) * nh
    at.meet()

    def go(buf_out, buf_in, sems, z, k):
        peer = at.head_peer(k)
        return remote(
            buf_out.at[z, peer],
            buf_in.at[z, at.h],
            sems.at[0, z, k],
            sems.at[1, z, k],
            at.in_head(peer),
        )

    def keep(buf_out, j, z):
        return pltpu.make_async_copy(buf_out.at[z, at.h], back_rows.at[z, at.h], local_sems.at[j, z])

    def far_first(body):
        def step(t, unused):
            body(lax.rem(at.z + 1 + t, nz))
            return 0

        lax.fori_loop(0, nz, step, 0)

    def send_back(z):
        for k in range(1, nh):
            go(d_rows, back_rows, ret_sems, z, k).start()
            go(d_gate_rows, in_dgate, dgate_sems, z, k).start()
        keep(d_rows, 0, z).start()
        in_dgate[z, at.h] = d_gate_rows[z, at.h]

    far_first(send_back)
    n2_scatter = Scatter(at, *(sc_bufs.at[j] for j in range(4)), sc_sems)

    def dg_copy(p):
        return remote(
            dg_out.at[p], dg_in.at[at.b], dg_sems.at[0, p], dg_sems.at[1, at.b], at.in_blk(p)
        )

    def masks_of(z):
        return [
            hits(pick_targets(slots[z, pl.ds(own_expert + h, 1)], pair), pair) for h in range(nh)
        ]

    def spread(z, masks, scatter):
        hit_rows = jnp.concatenate([jnp.where(m, 1.0, 0.0).astype(BF) for m in masks], axis=0)
        part = tn(hit_rows, back_rows[z].reshape(nh * 2 * CAP, MODEL_WIDTH))
        own_part[0] = part[:rows]
        own_part[1] = part[rows:]
        scatter.give_sibling(z, own_part[1 - at.core])

        @pl.when(z != at.z)
        def _():
            scatter.give(z, own_part[at.core] + scatter.from_sibling(z))

    def gathered_part(scatter):
        own_part[2] = own_part[at.core] + scatter.from_sibling(at.z)
        for z in range(nz):

            @pl.when(at.z != z)
            def _():
                own_part[2] += scatter.taken(z)

        return own_part[2]

    def gather_back(z):
        for k in range(1, nh):
            go(d_rows, back_rows, ret_sems, z, k).wait_recv()
            go(d_gate_rows, in_dgate, dgate_sems, z, k).wait_recv()
        keep(d_rows, 0, z).wait()
        masks = masks_of(z)
        d_gates = jnp.concatenate(
            [
                jnp.sum(jnp.where(m, to_column(in_dgate[z, h]), 0.0), axis=0, keepdims=True)
                for h, m in enumerate(masks)
            ],
            axis=0,
        )
        dg_out[2 * z] = d_gates[:, :rows]
        dg_out[2 * z + 1] = d_gates[:, rows:]
        pl.when(z == at.z)(lambda: dg_copy(at.sibling).start())

        @pl.when(z != at.z)
        def _():
            dg_copy(2 * z).start()
            dg_copy(2 * z + 1).start()

        spread(z, masks, n2_scatter)

    far_first(gather_back)
    dg_in[at.b] = dg_out[at.b]
    for k in range(1, nb):
        p = at.blk_peer(k)
        remote(dg_out.at[p], dg_in.at[p], dg_sems.at[0, p], dg_sems.at[1, p], at.in_blk(p)).wait_recv()
    d_gates = jnp.concatenate(
        [sum_slots(dg_in.at[pl.ds(i * repeat, repeat)], repeat) for i in range(nb // repeat)], axis=0
    )
    d_logits = own_gates[...] * (
        d_gates - jnp.sum(own_gates[...] * d_gates, axis=0, keepdims=True)
    )
    from_logits = split_product(tn, d_logits, router_t[...])
    g_router = split_product(nn, d_logits, n2[...])
    mid = middle[...]
    factor_two = lax.rsqrt(jnp.mean(mid * mid, axis=-1, keepdims=True) + eps)
    unit_two = mid * factor_two
    d_n2 = gathered_part(n2_scatter) + from_logits
    weighted_two = d_n2 * w_norm2[...]
    d_middle[...] = grad_out[...].astype(F32) + factor_two * (
        weighted_two - unit_two * jnp.mean(unit_two * weighted_two, axis=-1, keepdims=True)
    )
    dbg[at.h] = d_middle[...].astype(BF)
    d_copies = [
        remote(dbg.at[at.h], dbg.at[at.h], d_sems.at[0, k], d_sems.at[1, k], at.in_head(at.head_peer(k)))
        for k in range(1, nh)
    ]
    for c in d_copies:
        c.start()
    g_norm = jnp.sum(d_n2 * unit_two, axis=0, keepdims=True)
    slab = MODEL_WIDTH // nh
    for h in range(nh):
        cols = slice(h * slab, (h + 1) * slab)
        small[h, :E] = g_router[:, cols]
        small[h, E:] = jnp.broadcast_to(g_norm[:, cols], (8, slab))
    totals = Total(at, small, s_head, s_blk, small_sum, s_sems)
    totals.begin(0)
    perm[...] = jnp.where(
        place_row[...] == sorted_place(at, half, (group, group), 0), 1.0, 0.0
    ).astype(BF)
    dq_t[...] = jnp.zeros(dq_t.shape, F32)
    for c in d_copies:
        c.wait_recv()

    def send_scaled(z):
        for k in range(1, nh):
            go(scaled, back_rows, eout_sems, z, k).start()
        keep(scaled, 1, z).start()

    far_first(send_scaled)
    totals.end(0)
    totals.begin(1)
    d_branch = dbg[...].reshape(group, MODEL_WIDTH)
    w = wg[...].reshape(MODEL_WIDTH, width + qw)
    d_attn_t = nn(d_branch, w[:, width:]).T.astype(BF)
    d_sorted = nt(d_attn_t, perm[...])
    for second in range(2):
        piece = d_sorted[:, second * half : (second + 1) * half]
        do_t[second] = piece.astype(BF)
        product = piece * attn_t[second]
        delta[second, :hl] = jnp.concatenate(
            [
                jnp.sum(product[a * HEAD_SIZE : (a + 1) * HEAD_SIZE], axis=0, keepdims=True)
                for a in range(hl)
            ],
            axis=0,
        )

    def step_back(p, second):
        block = kv[p, second]
        lse_all, delta_all = lse[second], delta[second]
        key_place = block_base(at, p, second, half) + lax.broadcasted_iota(
            jnp.int32, (half, half), 0
        )
        own_place = block_base(at, at.b, second, half) + lax.broadcasted_iota(
            jnp.int32, (half, half), 1
        )
        allowed = (key_place <= own_place) & (key_place >= begin[second])
        d_keys, d_values = [None] * kl, [None] * kl
        for a in range(hl):
            g = a // (hl // kl)
            rows_a = slice(a * HEAD_SIZE, (a + 1) * HEAD_SIZE)
            key = block[:, g * HEAD_SIZE : (g + 1) * HEAD_SIZE]
            value = block[:, kw + g * HEAD_SIZE : kw + (g + 1) * HEAD_SIZE]
            scores = jnp.where(allowed, nn(key, qt[second, rows_a]), -1e30)
            probs = jnp.exp(scores - lse_all[a : a + 1])
            d_probs = nn(value, do_t[second, rows_a])
            d_scores = (probs * (d_probs - delta_all[a : a + 1])).astype(BF)
            d_key = nt(qt[second, rows_a], d_scores)
            d_value = nt(do_t[second, rows_a], probs.astype(BF))
            d_keys[g] = d_key if d_keys[g] is None else d_keys[g] + d_key
            d_values[g] = d_value if d_values[g] is None else d_values[g] + d_value
            dq_t[second, rows_a] += tn(key, d_scores)
        return jnp.concatenate(d_keys + d_values, axis=0)

    scatter = Scatter(at, *(kv_bufs.at[j] for j in range(4)), kv_sems)

    def visit(step, unused):
        i = nz - 1 - step // 4
        second = lax.rem(step // 2, 2)
        same = lax.rem(step, 2) == 1
        z = jnp.where(second == 0, at.z - i, at.z + i)
        p = 2 * z + jnp.where(same, at.core, 1 - at.core)
        exists = (z >= 0) & (z < nz) & ((i > 0) | same | (at.core != second))

        @pl.when(exists)
        def _():
            part = step_back(p, second)

            @pl.when(jnp.logical_not(same))
            def _():
                scatter.give_sibling(z, part)

            @pl.when(same & (i > 0))
            def _():
                scatter.give(z, part + scatter.from_sibling(z))

            @pl.when(same & (i == 0))
            def _():
                own_kv[second] = part

        return 0

    lax.fori_loop(0, 4 * nz, visit, 0)
    totals.end(1)
    totals.begin(2)
    wide = 256

    def weight_part(first, left):
        for c in range(MODEL_WIDTH // wide):
            source = xg if first == 0 else dbg
            piece = nn(left, source[:, :, c * wide : (c + 1) * wide].reshape(group, wide))
            for j in range(wide // dl):
                w_part[c * (wide // dl) + j, first : first + left.shape[0]] = piece[
                    :, j * dl : (j + 1) * dl
                ]

    weight_part(width, ao_t[...])
    own_kv[at.core] += scatter.from_sibling(at.z)
    for z in range(nz):

        @pl.when(at.z != z)
        def _():
            own_kv[jnp.where(at.z < z, 0, 1)] += scatter.taken(z)

    d_sorted_t = []
    for second in range(2):
        cols = slice(second * half, (second + 1) * half)
        both = own_kv[second]
        turned = jnp.concatenate([dq_t[second] * scale, both[:kw]], axis=0)
        turned = turn_rows(turned, cos[:, cols], -sin[:, cols])
        d_sorted_t.append(jnp.concatenate([turned, both[kw:]], axis=0).astype(BF))
    back = jnp.where(place_col[...] == sorted_place(at, half, (group, group), 1), 1.0, 0.0).astype(BF)
    turned_back = (
        nt(back[:, :half], d_sorted_t[0]) + nt(back[:, half:], d_sorted_t[1])
    ).astype(BF)
    d_rows_ref[...] = turned_back.reshape(nh, rows, width)
    d_cols = (nn(d_sorted_t[0], perm[:half]) + nn(d_sorted_t[1], perm[half:])).astype(BF)
    o_copies = []
    for k in range(1, nh):
        peer = at.head_peer(k)
        out_send[peer] = nt(d_rows_ref[peer], w[:, :width]).astype(BF)
        c = remote(
            out_send.at[peer], out_recv.at[at.h], o_sems.at[0, k], o_sems.at[1, k], at.in_head(peer)
        )
        c.start()
        o_copies.append(c)
    own_normed = nt(d_rows_ref[at.h], w[:, :width])
    weight_part(0, d_cols)
    w_scatter = Scatter(at, *(w_bufs.at[j] for j in range(4)), w_sems)

    def w_sib(step, unused):
        z = lax.rem(at.z + 1 + step, nz)
        w_scatter.give_sibling(z, w_part[2 * z + 1 - at.core])
        return 0

    lax.fori_loop(0, nz, w_sib, 0)

    def w_along(step, unused):
        z = lax.rem(at.z + 1 + step, nz)
        w_scatter.give(z, w_part[2 * z + at.core] + w_scatter.from_sibling(z))
        return 0

    lax.fori_loop(0, nz - 1, w_along, 0)
    n2_scatter.finish()
    mix_scatter = Scatter(at, *(sc_bufs.at[j] for j in range(4)), mix_sems)

    def mix(z):
        for k in range(1, nh):
            go(scaled, back_rows, eout_sems, z, k).wait_recv()
        keep(scaled, 1, z).wait()
        spread(z, masks_of(z), mix_scatter)

    far_first(mix)
    for k in range(1, nh):
        o_copies[k - 1].wait_recv()
        own_normed = own_normed + out_recv[lax.rem(at.h + nh - k, nh)].astype(F32)
    hidden = inputs[...].astype(F32)
    factor = lax.rsqrt(jnp.mean(hidden * hidden, axis=-1, keepdims=True) + eps)
    unit = hidden * factor
    n1_head[at.h] = jnp.sum(own_normed * unit, axis=0, keepdims=True)
    n1_copies = [
        remote(n1_head.at[at.h], n1_head.at[at.h], n_sems.at[0, k], n_sems.at[1, k], at.in_head(at.head_peer(k)))
        for k in range(1, nh)
    ]
    for c in n1_copies:
        c.start()
    weighted = own_normed * w_norm1[...]
    grad_in[...] = d_middle[...] + factor * (
        weighted - unit * jnp.mean(unit * weighted, axis=-1, keepdims=True)
    )
    for c in n1_copies:
        c.wait_recv()
    n1_blk[at.b] = sum_slots(n1_head, nh)
    n1_blk_copies = [
        remote(n1_blk.at[at.b], n1_blk.at[at.b], n_sems.at[0, nh + k], n_sems.at[1, nh + k], at.in_blk(at.blk_peer(k)))
        for k in range(1, nb)
    ]
    for c in n1_blk_copies:
        c.start()
    total_w = w_part[at.b] + w_scatter.from_sibling(at.z)
    grad_w[...] = total_w
    for z in range(nz):

        @pl.when(at.z != z)
        def _():
            grad_w[...] += w_scatter.taken(z)

    for c in n1_blk_copies:
        c.wait_recv()
    grad_n1[...] = sum_slots(n1_blk, nb)
    totals.end(2)
    output[...] = (middle[...] + gathered_part(mix_scatter)).astype(BF)
    totals.finish()
    scatter.finish()
    mix_scatter.finish()

    def drain(z):
        for k in range(1, nh):
            go(d_rows, back_rows, ret_sems, z, k).wait_send()
            go(d_gate_rows, in_dgate, dgate_sems, z, k).wait_send()
            go(scaled, back_rows, eout_sems, z, k).wait_send()

    far_first(drain)
    for k in range(1, nb):
        dg_copy(at.blk_peer(k)).wait_send()
    w_scatter.finish()
    for c in d_copies + o_copies + n1_copies + n1_blk_copies:
        c.wait_send()


def back(nb, nh, hl, kl, repeat, *operands):
    rows = operands[0].shape[0]
    group, half = rows * nh, rows * nh // 2
    nz, dl = nb // 2, MODEL_WIDTH // nb
    qw, kw = hl * HEAD_SIZE, kl * HEAD_SIZE
    width = qw + 2 * kw
    shape = jax.ShapeDtypeStruct
    dma = pltpu.SemaphoreType.DMA
    chunk = (E + 8, MODEL_WIDTH // nh)
    line = (nz, nh, 1, 2 * CAP)
    return pl.pallas_call(
        functools.partial(back_kernel, nb, nh, hl, kl, repeat),
        out_shape=(
            shape((rows, MODEL_WIDTH), BF),
            shape((rows, MODEL_WIDTH), F32),
            shape((width + qw, dl), F32),
            shape((1, MODEL_WIDTH), F32),
            shape((nh,) + chunk, F32),
        ),
        in_specs=[VMEM] * 22 + [ANY] * 2,
        out_specs=[VMEM] * 5,
        scratch_shapes=[
            pltpu.VMEM((nh, rows, MODEL_WIDTH), BF),
            pltpu.VMEM((group, group), BF),
            pltpu.VMEM((nh, rows, width), BF),
            pltpu.VMEM((2, qw, half), BF),
            pltpu.VMEM((2, max(hl, 8), half), F32),
            pltpu.VMEM((2, qw, half), F32),
            pltpu.VMEM((2, 2 * kw, half), F32),
            pltpu.VMEM((4, nz, 2 * kw, half), BF),
            pltpu.VMEM((nb, width + qw, dl), F32),
            pltpu.VMEM((4, nz, width + qw, dl), BF),
            pltpu.VMEM((nh, rows, MODEL_WIDTH), BF),
            pltpu.VMEM((nh, rows, MODEL_WIDTH), BF),
            pltpu.VMEM((nh, 1, MODEL_WIDTH), F32),
            pltpu.VMEM((nb, 1, MODEL_WIDTH), F32),
            pltpu.VMEM((nh,) + chunk, F32),
            pltpu.VMEM((nb,) + chunk, F32),
            dma((2, nh)),
            dma((4, nz)),
            dma((4, nz)),
            dma((2, nh)),
            dma((2, nh + nb)),
            dma((2, 3, max(nh, nb))),
            pltpu.VMEM((nh,) + chunk, F32),
            pltpu.VMEM((nz, nh, 2 * CAP, MODEL_WIDTH), BF),
            pltpu.VMEM(line, F32),
            pltpu.VMEM((3, rows, MODEL_WIDTH), F32),
            pltpu.VMEM((rows, MODEL_WIDTH), F32),
            pltpu.VMEM((nb, nh, rows), F32),
            pltpu.VMEM((nb, nh, rows), F32),
            pltpu.VMEM((4, nz, rows, MODEL_WIDTH), BF),
            dma((4, nz)),
            dma((4, nz)),
            dma((2, nz, nh)),
            dma((2, nz, nh)),
            dma((2, nz, nh)),
            dma((2, nb)),
            dma((2, nz)),
        ],
        compiler_params=pltpu.CompilerParams(collective_id=2, vmem_limit_bytes=60 * 2**20),
        name="back",
    )(*operands)


def on_device(
    inputs,
    token_place,
    lengths,
    w_norm1,
    w_query,
    key_weight,
    value_weight,
    w_out,
    w_norm2,
    router,
    routes,
    slot_order,
    w_gate,
    w_up,
    w_down,
    grad_out,
):
    rows = inputs.shape[0]
    nb, nh = lax.axis_size("blk"), lax.axis_size("head")
    nz = nb // 2
    hl = w_query.shape[1] // HEAD_SIZE
    kl = key_weight.shape[1] // HEAD_SIZE
    local, dl, hidden_units = w_gate.shape
    repeat = nb // local
    fr = hidden_units // repeat
    qw, kw = hl * HEAD_SIZE, kl * HEAD_SIZE

    def by_part(v):
        v = v.reshape(local, dl, repeat, fr).transpose(0, 2, 1, 3)
        return v.reshape(nb, dl, fr)

    projections = jnp.stack(
        [by_part(w_gate), by_part(w_up), by_part(w_down.transpose(0, 2, 1))], axis=1
    )
    projections = lax.all_to_all(projections, "blk", split_axis=0, concat_axis=0, tiled=True)
    own, begin_s, cos_o, sin_o, cos_s, sin_s, w_own = head_inputs(
        nb, nh, rows, token_place, lengths, w_query, key_weight, value_weight, w_out
    )
    gain_one, gain_two = w_norm1.reshape(1, -1), w_norm2.reshape(1, -1)
    place_row, place_col = own.reshape(1, -1), own.reshape(-1, 1)
    sizes = (nb, nh, hl, kl, repeat)
    router_t = router.T.reshape(nh, local, MODEL_WIDTH).transpose(1, 0, 2).reshape(E, MODEL_WIDTH)
    (
        gathered,
        weights,
        turned_q,
        kv,
        lse,
        attn_t,
        ao_t,
        middle,
        normed_two,
        slots,
        own_gates,
        in_gate,
        in_rows,
        in_g,
    ) = front(
        *sizes,
        inputs,
        gain_one,
        gain_two,
        w_own,
        place_row,
        place_col,
        cos_o,
        sin_o,
        begin_s,
        grad_out,
        slot_table(nb, nh, repeat, routes, slot_order),
        router_t,
    )
    d_rows, scaled, d_gate_rows, grads = experts(nz, nh, in_rows, in_g, in_gate, projections)
    grads = lax.all_to_all(grads, "blk", split_axis=0, concat_axis=0, tiled=True)
    output, grad_inputs, grad_w, grad_norm1, small = back(
        *sizes,
        inputs,
        gain_one,
        gain_two,
        middle,
        normed_two,
        grad_out,
        router_t,
        slots,
        own_gates,
        d_gate_rows,
        weights,
        gathered,
        ao_t,
        turned_q,
        kv,
        lse,
        attn_t,
        place_row,
        place_col,
        cos_s,
        sin_s,
        begin_s,
        d_rows,
        scaled,
    )

    small = small.transpose(1, 0, 2).reshape(E + 8, MODEL_WIDTH)
    grad_router = (
        small[:E].reshape(local, nh, MODEL_WIDTH).transpose(1, 0, 2).reshape(E, MODEL_WIDTH).T
    )

    def whole_part(v):
        v = v.reshape(local, repeat, dl, fr).transpose(0, 2, 1, 3)
        return v.reshape(local, dl, hidden_units).astype(F32)

    return (
        output,
        grad_inputs,
        grad_norm1.reshape(-1),
        grad_w[:qw].T,
        grad_w[qw : qw + kw].T,
        grad_w[qw + kw : qw + 2 * kw].T,
        grad_w[qw + 2 * kw :],
        small[E],
        grad_router,
        whole_part(grads[:, 0]),
        whole_part(grads[:, 1]),
        whole_part(grads[:, 2]).transpose(0, 2, 1),
    )


def solution(mesh):
    rows, whole = P(("blk", "head"), None), P()
    pair, out = P("blk", "head"), P("head", "blk")
    first, last = P("head", "blk", None), P("head", None, "blk")
    return jax.shard_map(
        on_device,
        mesh=mesh,
        in_specs=(
            rows,
            whole,
            whole,
            whole,
            pair,
            pair,
            pair,
            out,
            whole,
            whole,
            rows,
            rows,
            first,
            first,
            last,
            rows,
        ),
        out_specs=(
            rows,
            rows,
            whole,
            pair,
            pair,
            pair,
            out,
            whole,
            whole,
            first,
            first,
            last,
        ),
        check_vma=False,
    )
```

```python
import functools
import math

import jax
import jax.numpy as jnp
from jax import lax
from jax.experimental import pallas as pl
from jax.experimental.pallas import tpu as pltpu
from jax.sharding import PartitionSpec as P

MODEL_WIDTH = 1024
HEAD_SIZE = 64
E = 32
TOPK = 8
CAP = 40
MESH = pl.DeviceIdType.MESH
VMEM = pl.BlockSpec(memory_space=pltpu.VMEM)
ANY = pl.BlockSpec(memory_space=pl.ANY)
BF = jnp.bfloat16
F32 = jnp.float32
FRONT_DEAL = (0.1, 0.6)
BACK_DEAL = (0.1, 0.4, 0.55)

eps = 1e-06
rope_base = 10000.0


def nn(a, b, **kw):
    return lax.dot_general(a, b, (((1,), (0,)), ((), ())), preferred_element_type=F32, **kw)


def nt(a, b, **kw):
    return lax.dot_general(a, b, (((1,), (1,)), ((), ())), preferred_element_type=F32, **kw)


def tn(a, b, **kw):
    return lax.dot_general(a, b, (((0,), (0,)), ((), ())), preferred_element_type=F32, **kw)


def remote(src, dst, send, recv, device):
    return pltpu.make_async_remote_copy(
        src_ref=src,
        dst_ref=dst,
        send_sem=send,
        recv_sem=recv,
        device_id=device,
        device_id_type=MESH,
    )


def start_pieces(copy, src, dst, count, *rest):
    rows = src.shape[0] // count
    for i in range(count):
        part = pl.ds(i * rows, rows)
        copy(src.at[part], dst.at[part], *rest).start()


class Copy:
    def __init__(self, src, dst, count, *rest):
        self.src, self.dst, self.count, self.rest = src, dst, count, rest

    def start(self):
        start_pieces(remote, self.src, self.dst, self.count, *self.rest)

    def wait_send(self):
        remote(self.src, self.dst, *self.rest).wait_send()

    def wait_recv(self):
        remote(self.src, self.dst, *self.rest).wait_recv()


def piece_count(shape, size):
    count = max(1, shape[0] * shape[1] * 2 // size)
    while shape[0] % (16 * count):
        count -= 1
    return count


class Place:
    def __init__(self, nb, nh):
        self.nb, self.nh, self.nz = nb, nh, nb // 2
        self.b, self.h = lax.axis_index("blk"), lax.axis_index("head")
        self.z, self.core = self.b // 2, lax.rem(self.b, 2)
        self.sibling = 2 * self.z + 1 - self.core

    def in_blk(self, b):
        return (b, self.h)

    def in_head(self, h):
        return (self.b, h)

    def head_peer(self, k):
        return lax.rem(self.h + k, self.nh)

    def blk_peer(self, k):
        return lax.rem(self.b + k, self.nb)

    def meet(self):
        barrier = pltpu.get_barrier_semaphore()
        for k in range(1, self.nh):
            pl.semaphore_signal(
                barrier, inc=1, device_id=self.in_head(self.head_peer(k)), device_id_type=MESH
            )
        for k in range(1, self.nb):
            pl.semaphore_signal(
                barrier, inc=1, device_id=self.in_blk(self.blk_peer(k)), device_id_type=MESH
            )
        pl.semaphore_wait(barrier, self.nh + self.nb - 2)


class Relay:
    def __init__(self, at, buf, send, recv, count=1):
        self.at, self.buf, self.send, self.recv, self.count = at, buf, send, recv, count

    def copy(self, s, way, device):
        return Copy(
            self.buf.at[s], self.buf.at[s], self.count, self.send.at[way, s], self.recv.at[s], device
        )

    def right(self, s):
        return self.copy(s, 0, self.at.in_blk(jnp.minimum(self.at.b + 2, self.at.nb - 2 + self.at.core)))

    def left(self, s):
        return self.copy(s, 1, self.at.in_blk(jnp.maximum(self.at.b - 2, self.at.core)))

    def across(self, s):
        return self.copy(s, 2, self.at.in_blk(self.at.sibling))

    def begin(self):
        at = self.at
        pl.when(at.z + 1 < at.nz)(lambda: self.right(at.b).start())
        pl.when(at.z > 0)(lambda: self.left(at.b).start())
        self.across(at.b).start()

    def hop(self, i):
        at = self.at

        @pl.when(at.z >= i)
        def _():
            s = at.b - 2 * i
            self.across(s).wait_recv()
            pl.when(at.z + 1 < at.nz)(lambda: self.right(s).start())
            self.across(s).start()

        @pl.when(at.z + i < at.nz)
        def _():
            s = at.b + 2 * i
            self.across(s).wait_recv()
            pl.when(at.z > 0)(lambda: self.left(s).start())
            self.across(s).start()

    def take_sibling(self, z):
        self.across(2 * z + 1 - self.at.core).wait_recv()

    def finish(self):
        at = self.at
        for i in range(at.nz):

            @pl.when(at.z >= i)
            def _():
                s = at.b - 2 * i
                pl.when(at.z + 1 < at.nz)(lambda: self.right(s).wait_send())
                self.across(s).wait_send()

            if i == 0:
                pl.when(at.z > 0)(lambda: self.left(at.b).wait_send())
            else:

                @pl.when(at.z + i < at.nz)
                def _():
                    s = at.b + 2 * i
                    pl.when(at.z > 0)(lambda: self.left(s).wait_send())
                    self.across(s).wait_send()

    def all(self):
        self.begin()
        for i in range(1, self.at.nz):
            self.hop(i)
        for z in range(self.at.nz):
            self.take_sibling(z)


class Deal:
    def __init__(self, at, chunk, arrived, sems, local_sems):
        self.at, self.chunk, self.arrived = at, chunk, arrived
        self.sems, self.local_sems = sems, local_sems

    def ends(self, j, k):
        at = self.at
        p = at.blk_peer(k)
        return (
            self.chunk(j, p),
            self.arrived[j].at[at.b],
            self.sems.at[0, j, k],
            self.sems.at[1, j, k],
            at.in_blk(p),
        )

    def own(self, j):
        at = self.at
        return pltpu.make_async_copy(
            self.chunk(j, at.b), self.arrived[j].at[at.b], self.local_sems.at[j]
        )

    def start(self, first, last):
        for i in range(first, last):
            remote(*self.ends(i % 3, 1 + i // 3)).start()
        if first == 0 < last:
            for j in range(3):
                self.own(j).start()

    def end(self):
        for j in range(3):
            for k in range(1, self.at.nb):
                move = remote(*self.ends(j, k))
                move.wait_recv()
                move.wait_send()
            self.own(j).wait()

    def share(self, part):
        return int(3 * (self.at.nb - 1) * part)


def sorted_place(at, half, shape, axis):
    s = lax.broadcasted_iota(jnp.int32, shape, axis)
    return jnp.where(
        s < half, at.b * half + s, (2 * at.nb - 1 - at.b) * half + s - half
    )


def block_base(at, b, second, half):
    return jnp.where(second == 0, b * half, (2 * at.nb - 1 - b) * half)


def turn_rows(values, cos, sin):
    half = HEAD_SIZE // 2
    pieces = []
    for first in range(0, values.shape[0], HEAD_SIZE):
        lead = values[first : first + half]
        trail = values[first + half : first + HEAD_SIZE]
        pieces.append(lead * cos - trail * sin)
        pieces.append(trail * cos + lead * sin)
    return jnp.concatenate(pieces, axis=0)


def pick_targets(slots, pair_rows):
    lane = lax.broadcasted_iota(jnp.int32, slots.shape, 1)
    kept = (slots >= 0) & (slots < CAP)
    return jnp.where(kept, slots + jnp.where(lane >= pair_rows // 2, CAP, 0), -1)


def hits(target_row, pair_rows):
    return lax.broadcasted_iota(jnp.int32, (2 * CAP, pair_rows), 0) == target_row


def diagonal():
    shape = (2 * CAP, 2 * CAP)
    return lax.broadcasted_iota(jnp.int32, shape, 0) == lax.broadcasted_iota(jnp.int32, shape, 1)


def to_row(column):
    return jnp.sum(jnp.where(diagonal(), column, 0.0), axis=0, keepdims=True)


def to_column(row):
    return jnp.sum(jnp.where(diagonal(), row, 0.0), axis=1, keepdims=True)


def split_product(dot, left, right):
    high = left.astype(BF)
    low = (left - high.astype(F32)).astype(BF)
    return dot(high, right) + dot(low, right)


def front_kernel(
    nb,
    nh,
    hl,
    kl,
    repeat,
    inputs,
    w_norm1,
    w_norm2,
    w_own,
    place_row,
    place_col,
    cos,
    sin,
    begin,
    grad_out,
    table,
    router_t,
    w_gate,
    w_up,
    w_down,
    xg,
    wg,
    qt,
    kv,
    lse,
    attn_t,
    ao_t,
    middle,
    n2,
    slots,
    own_gates,
    in_gate,
    in_rows,
    in_g,
    gate_in,
    up_in,
    down_in,
    ao,
    perm,
    top,
    total,
    out_send,
    out_recv,
    x_sems,
    w_send,
    w_recv,
    kv_send,
    kv_recv,
    o_sems,
    slot_all,
    g_all,
    n2_all,
    gates,
    out_rows,
    out_g,
    out_gate,
    s_send,
    s_recv,
    g_send,
    g_recv,
    n_send,
    n_recv,
    row_sems,
    g_sems,
    gate_sems,
    local_sems,
    deal_sems,
    deal_local,
):
    at = Place(nb, nh)
    rows = inputs.shape[0]
    group = rows * nh
    half = group // 2
    qw, kw = hl * HEAD_SIZE, kl * HEAD_SIZE
    width = qw + 2 * kw

    hidden = inputs[...].astype(F32)
    unit = hidden * lax.rsqrt(jnp.mean(hidden * hidden, axis=-1, keepdims=True) + eps)
    xg[at.h] = (unit * w_norm1[...]).astype(BF)
    wg[at.b] = w_own[...]
    slot_all[at.b] = table[...]
    g_all[at.b] = grad_out[...]
    at.meet()
    x_copies = [
        remote(xg.at[at.h], xg.at[at.h], x_sems.at[0, k], x_sems.at[1, k], at.in_head(at.head_peer(k)))
        for k in range(1, nh)
    ]
    for c in x_copies:
        c.start()
    weights = Relay(at, wg, w_send, w_recv)
    weights.begin()
    slot_relay = Relay(at, slot_all, s_send, s_recv)
    slot_relay.begin()
    g_relay = Relay(at, g_all, g_send, g_recv, 4)
    g_relay.begin()
    pair = 2 * rows
    own_expert = (at.b // repeat) * nh

    def chunk(j, p):
        w_j = (w_gate, w_up, w_down)[j]
        if repeat == 1:
            return w_j.at[p]
        fr = w_gate.shape[2] // repeat
        part = pl.ds(pl.multiple_of(lax.rem(p, repeat) * fr, fr), fr)
        return w_j.at[p // repeat, part] if j == 2 else w_j.at[p // repeat, :, part]

    deal = Deal(at, chunk, (gate_in, up_in, down_in), deal_sems, deal_local)

    def go(buf_out, buf_in, sems, z, k, count=1):
        peer = at.head_peer(k)
        return Copy(
            buf_out.at[z, peer],
            buf_in.at[z, at.h],
            count,
            sems.at[0, z, k],
            sems.at[1, z, k],
            at.in_head(peer),
        )

    def keep(buf_out, buf_in, j, z):
        return pltpu.make_async_copy(buf_out.at[z, at.h], buf_in.at[z, at.h], local_sems.at[j, z])

    def outward(relay, body, first, last):
        def step(t, unused):
            d, side = t // 2, lax.rem(t, 2)
            z = jnp.where(side == 0, at.z - d, at.z + d)
            pl.when((side == 0) & (d > 0))(lambda: relay.hop(d))

            @pl.when((z >= 0) & (z < at.nz) & ((d > 0) | (side == 0)))
            def _():
                relay.take_sibling(z)
                body(z)

            return 0

        lax.fori_loop(2 * first, 2 * last, step, 0)

    def send_g(z):
        x = g_all[pl.ds(2 * z, 2)].reshape(pair, MODEL_WIDTH)
        for k in list(range(1, nh)) + [0]:
            peer = at.head_peer(k)
            hit = hits(pick_targets(slots[z, pl.ds(own_expert + peer, 1)], pair), pair)
            out_g[z, peer] = nn(jnp.where(hit, 1.0, 0.0).astype(BF), x).astype(BF)
            if k == 0:
                keep(out_g, in_g, 0, z).start()
            else:
                go(out_g, in_g, g_sems, z, k, 5).start()

    def send_rows(z):
        x = n2_all[pl.ds(2 * z, 2)].reshape(pair, MODEL_WIDTH)
        routed = slots[z] >= 0
        logits = jnp.where(routed, nt(router_t[...], x), -1e30)
        shifted = jnp.exp(logits - jnp.max(logits, axis=0, keepdims=True))
        shifted = jnp.where(routed, shifted, 0.0)
        gates[z] = shifted / jnp.sum(shifted, axis=0, keepdims=True)
        for k in list(range(1, nh)) + [0]:
            peer = at.head_peer(k)
            hit = hits(pick_targets(slots[z, pl.ds(own_expert + peer, 1)], pair), pair)
            gate_row = gates[z, pl.ds(own_expert + peer, 1)]
            gate = to_row(jnp.sum(jnp.where(hit, gate_row, 0.0), axis=1, keepdims=True))
            out_rows[z, peer] = nn(jnp.where(hit, 1.0, 0.0).astype(BF), x).astype(BF)
            if k == 0:
                keep(out_rows, in_rows, 1, z).start()
                in_gate[z, at.h] = gate
            else:
                go(out_rows, in_rows, row_sems, z, k).start()
                out_gate[z, peer] = gate
                go(out_gate, in_gate, gate_sems, z, k).start()

    perm[...] = jnp.where(
        place_row[...] == sorted_place(at, half, (group, group), 0), 1.0, 0.0
    ).astype(BF)
    for i in range(1, nb // 2):
        slot_relay.hop(i)
        weights.hop(i)
    for z in range(nb // 2):
        slot_relay.take_sibling(z)
    for z in range(nb // 2):
        slots[z] = jnp.concatenate([slot_all[2 * z], slot_all[2 * z + 1]], axis=1)
    outward(g_relay, send_g, 0, 1)
    deal.start(0, deal.share(FRONT_DEAL[0]))
    for z in range(nb // 2):
        weights.take_sibling(z)
    for c in x_copies:
        c.wait_recv()
    x = xg[...].reshape(group, MODEL_WIDTH)
    w = wg[...].reshape(MODEL_WIDTH, width + qw)
    qkv_t = nn(x, w[:, :width]).T
    qkv_t = jnp.concatenate(
        [turn_rows(qkv_t[: qw + kw], cos[...], sin[...]), qkv_t[qw + kw :]], axis=0
    ).astype(BF)
    order = perm[...]
    kv_rows = nt(order, qkv_t[qw:]).astype(BF)
    kv[at.b, 0] = kv_rows[:half]
    kv[at.b, 1] = kv_rows[half:]

    def kv_copy(p, second, way, device):
        return remote(
            kv.at[p, second], kv.at[p, second], kv_send.at[way, p], kv_recv.at[p], device
        )

    right = at.in_blk(jnp.minimum(at.b + 2, nb - 2 + at.core))
    left = at.in_blk(jnp.maximum(at.b - 2, at.core))
    across = at.in_blk(at.sibling)
    pl.when(at.z + 1 < at.nz)(lambda: kv_copy(at.b, 0, 0, right).start())
    pl.when(at.z > 0)(lambda: kv_copy(at.b, 1, 0, left).start())
    kv_copy(at.b, at.core, 1, across).start()
    q_cols = (nt(qkv_t[:qw], order) * (1.0 / math.sqrt(HEAD_SIZE))).astype(BF)
    qt[0] = q_cols[:, :half]
    qt[1] = q_cols[:, half:]
    outward(g_relay, send_g, 1, 2)
    top[...] = jnp.full(top.shape, -1e30, F32)
    total[...] = jnp.zeros(total.shape, F32)
    attn_t[...] = jnp.zeros(attn_t.shape, F32)

    def attend(p, second):
        old_top, old_total = top[second], total[second]
        tops, totals = [], []
        block = kv[p, second]
        key_place = block_base(at, p, second, half) + lax.broadcasted_iota(
            jnp.int32, (half, half), 0
        )
        own_place = block_base(at, at.b, second, half) + lax.broadcasted_iota(
            jnp.int32, (half, half), 1
        )
        allowed = (key_place <= own_place) & (key_place >= begin[second])
        for a in range(hl):
            g = a // (hl // kl)
            rows_a = slice(a * HEAD_SIZE, (a + 1) * HEAD_SIZE)
            scores = nn(block[:, g * HEAD_SIZE : (g + 1) * HEAD_SIZE], qt[second, rows_a])
            scores = jnp.where(allowed, scores, -1e30)
            old = old_top[a : a + 1]
            new = jnp.maximum(old, jnp.max(scores, axis=0, keepdims=True))
            probs = jnp.exp(scores - new)
            fade = jnp.exp(old - new)
            totals.append(old_total[a : a + 1] * fade + jnp.sum(probs, axis=0, keepdims=True))
            tops.append(new)
            attn_t[second, rows_a] = attn_t[second, rows_a] * fade + tn(
                block[:, kw + g * HEAD_SIZE : kw + (g + 1) * HEAD_SIZE], probs.astype(BF)
            )
        top[second, :hl] = jnp.concatenate(tops, axis=0)
        total[second, :hl] = jnp.concatenate(totals, axis=0)

    def visit(step, unused):
        i = step // 4
        second = lax.rem(step, 2)
        same = lax.rem(step // 2, 2) == 0
        z = jnp.where(second == 0, at.z - i, at.z + i)
        p = 2 * z + jnp.where(same, at.core, 1 - at.core)
        exists = (z >= 0) & (z < nb // 2) & ((i > 0) | same | (at.core != second))

        @pl.when(exists)
        def _():
            @pl.when(p != at.b)
            def _():
                kv_copy(p, second, 1, across).wait_recv()

            @pl.when((i > 0) & same)
            def _():
                @pl.when((second == 0) & (at.z + 1 < at.nz))
                def _():
                    kv_copy(p, second, 0, right).start()

                @pl.when((second == 1) & (at.z > 0))
                def _():
                    kv_copy(p, second, 0, left).start()

                kv_copy(p, second, 1, across).start()

            attend(p, second)

        return 0

    lax.fori_loop(0, 4 * (nb // 2), visit, 0)
    deal.start(deal.share(FRONT_DEAL[0]), deal.share(FRONT_DEAL[1]))
    for second in range(2):
        sums = total[second]
        for a in range(hl):
            rows_a = slice(a * HEAD_SIZE, (a + 1) * HEAD_SIZE)
            attn_t[second, rows_a] = attn_t[second, rows_a] / sums[a : a + 1]
    lse[...] = top[...] + jnp.log(total[...])
    back = jnp.where(place_col[...] == sorted_place(at, half, (group, group), 1), 1.0, 0.0).astype(BF)
    attn_rows = (
        nt(back[:, :half], attn_t[0].astype(BF)) + nt(back[:, half:], attn_t[1].astype(BF))
    ).astype(BF)
    ao[...] = attn_rows
    ao_t[...] = (
        nn(attn_t[0].astype(BF), perm[:half]) + nn(attn_t[1].astype(BF), perm[half:])
    ).astype(BF)
    o_copies = []
    for k in range(nh):
        peer = at.head_peer(k)
        chunk = nt(ao[pl.ds(peer * rows, rows)], w[:, width:])
        if k == 0:
            middle[...] = hidden + chunk
            continue
        out_send[peer] = chunk.astype(BF)
        c = remote(
            out_send.at[peer], out_recv.at[at.h], o_sems.at[0, k], o_sems.at[1, k], at.in_head(peer)
        )
        c.start()
        o_copies.append(c)
    outward(g_relay, send_g, 2, at.nz)
    for k in range(1, nh):
        o_copies[k - 1].wait_recv()
        middle[...] += out_recv[lax.rem(at.h + nh - k, nh)].astype(F32)
    mid = middle[...]
    n2[...] = (
        mid * lax.rsqrt(jnp.mean(mid * mid, axis=-1, keepdims=True) + eps) * w_norm2[...]
    ).astype(BF)
    n2_all[at.b] = n2[...]
    n_relay = Relay(at, n2_all, n_send, n_recv)
    n_relay.begin()
    outward(n_relay, send_rows, 0, at.nz)
    deal.start(deal.share(FRONT_DEAL[1]), deal.share(1))
    own_gates[...] = jnp.where(at.core == 0, gates[at.z, :, :rows], gates[at.z, :, rows:])
    for relay in (weights, slot_relay, g_relay, n_relay):
        relay.finish()
    for c in x_copies + o_copies:
        c.wait_send()

    def drain(step, unused):
        i = step // 2
        second = lax.rem(step, 2)
        z = jnp.where(second == 0, at.z - i, at.z + i)
        p = 2 * z + at.core

        @pl.when((z >= 0) & (z < nb // 2))
        def _():
            @pl.when((second == 0) & (at.z + 1 < at.nz))
            def _():
                kv_copy(p, second, 0, right).wait_send()

            @pl.when((second == 1) & (at.z > 0))
            def _():
                kv_copy(p, second, 0, left).wait_send()

            @pl.when((i > 0) | (second == at.core))
            def _():
                kv_copy(p, second, 1, across).wait_send()

        return 0

    lax.fori_loop(0, nb, drain, 0)

    def end(z, unused):
        for k in range(1, nh):
            for move in (
                go(out_g, in_g, g_sems, z, k),
                go(out_rows, in_rows, row_sems, z, k),
                go(out_gate, in_gate, gate_sems, z, k),
            ):
                move.wait_recv()
                move.wait_send()
        keep(out_g, in_g, 0, z).wait()
        keep(out_rows, in_rows, 1, z).wait()
        return 0

    lax.fori_loop(0, at.nz, end, 0)
    deal.end()


def front(nb, nh, hl, kl, repeat, *operands):
    inputs, w_own = operands[0], operands[3]
    hidden_units = operands[12].shape[2]
    fr = hidden_units // repeat
    rows = inputs.shape[0]
    group, half = rows * nh, rows * nh // 2
    nz = nb // 2
    dl, wide = w_own.shape
    qw, kw = hl * HEAD_SIZE, kl * HEAD_SIZE
    shape = jax.ShapeDtypeStruct
    dma = pltpu.SemaphoreType.DMA
    chunk = (nz, nh, 2 * CAP, MODEL_WIDTH)
    line = (nz, nh, 1, 2 * CAP)
    relay_sems = [dma((3, nb)), dma((nb,))]
    return pl.pallas_call(
        functools.partial(front_kernel, nb, nh, hl, kl, repeat),
        out_shape=(
            shape((nh, rows, MODEL_WIDTH), BF),
            shape((nb, dl, wide), BF),
            shape((2, qw, half), BF),
            shape((nb, 2, half, 2 * kw), BF),
            shape((2, max(hl, 8), half), F32),
            shape((2, qw, half), F32),
            shape((qw, group), BF),
            shape((rows, MODEL_WIDTH), F32),
            shape((rows, MODEL_WIDTH), BF),
            shape((nz, E, 2 * rows), jnp.int32),
            shape((E, rows), F32),
            shape(line, F32),
            shape(chunk, BF),
            shape(chunk, BF),
            shape((nb, dl, fr), BF),
            shape((nb, dl, fr), BF),
            shape((nb, fr, dl), BF),
        ),
        in_specs=[VMEM] * 12 + [ANY] * 3,
        out_specs=[VMEM] * 12 + [ANY] * 5,
        scratch_shapes=[
            pltpu.VMEM((group, qw), BF),
            pltpu.VMEM((group, group), BF),
            pltpu.VMEM((2, max(hl, 8), half), F32),
            pltpu.VMEM((2, max(hl, 8), half), F32),
            pltpu.VMEM((nh, rows, MODEL_WIDTH), BF),
            pltpu.VMEM((nh, rows, MODEL_WIDTH), BF),
            dma((2, nh)),
            dma((3, nb)),
            dma((nb,)),
            dma((2, nb)),
            dma((nb,)),
            dma((2, nh)),
            pltpu.VMEM((nb, E, rows), jnp.int32),
            pltpu.VMEM((nb, rows, MODEL_WIDTH), BF),
            pltpu.VMEM((nb, rows, MODEL_WIDTH), BF),
            pltpu.VMEM((nz, E, 2 * rows), F32),
            pltpu.VMEM(chunk, BF),
            pltpu.VMEM(chunk, BF),
            pltpu.VMEM(line, F32),
            *relay_sems,
            *relay_sems,
            *relay_sems,
            dma((2, nz, nh)),
            dma((2, nz, nh)),
            dma((2, nz, nh)),
            dma((2, nz)),
            dma((2, 3, nb)),
            dma((3,)),
        ],
        compiler_params=pltpu.CompilerParams(collective_id=1, vmem_limit_bytes=60 * 2**20),
        name="front",
    )(*operands)


def seq_begin(token_position, lengths):
    starts = jnp.cumsum(lengths) - lengths
    inside = token_position[:, None] >= starts[None, 1:]
    return jnp.sum(jnp.where(inside, lengths[None, :-1], 0), axis=1)


def rotation_rows(token_position, begin_index):
    half = HEAD_SIZE // 2
    freq = jnp.exp(
        jnp.arange(half, dtype=F32) * (-2.0 * math.log(rope_base) / HEAD_SIZE)
    )
    angle = freq[:, None] * (token_position - begin_index).astype(F32)[None, :]
    return jnp.cos(angle), jnp.sin(angle)


def head_inputs(nb, nh, rows, token_place, lengths, w_query, key_weight, value_weight, w_out):
    group, half = rows * nh, rows * nh // 2
    b = lax.axis_index("blk")
    own = lax.dynamic_slice_in_dim(token_place, b * group, group)
    s = jnp.arange(group, dtype=jnp.int32)
    in_order = jnp.where(s < half, b * half + s, (2 * nb - 1 - b) * half + s - half)
    begin_s = seq_begin(in_order, lengths)
    cos_o, sin_o = rotation_rows(own, seq_begin(own, lengths))
    cos_s, sin_s = rotation_rows(in_order, begin_s)
    w_own = jnp.concatenate([w_query, key_weight, value_weight, w_out.T], axis=1)
    return own, begin_s.reshape(2, 1, half), cos_o, sin_o, cos_s, sin_s, w_own


def slot_table(nb, nh, repeat, routes, slot_order):
    local = E // nh
    mine = (routes % local) * nh + routes // local
    match = mine.T[:, None, :] == jnp.arange(E, dtype=jnp.int32)[None, :, None]
    order = jnp.min(jnp.where(match, slot_order.T[:, None, :], 1 << 20), axis=0)
    before = jnp.sum((order[:, :, None] < order[:, None, :]).astype(jnp.int32), axis=1)
    return jnp.where(order < (1 << 20), before, -1)


def experts_kernel(
    nz,
    nh,
    x_ref,
    g_ref,
    gate_ref,
    w_gate_ref,
    w_up_ref,
    w_down_ref,
    d_rows,
    scaled,
    d_gate_row,
    grad_gate,
    grad_up,
    grad_down,
    w_down,
    sum_gate,
    sum_up,
    sum_down,
):
    step = pl.program_id(0)
    nb, dl, fr = w_gate_ref.shape

    @pl.when(step == 0)
    def _():
        w_down[...] = jnp.concatenate([w_down_ref[p] for p in range(nb)], axis=1)
        for total in (sum_gate, sum_up, sum_down):
            total[...] = jnp.zeros(total.shape, F32)

    x = x_ref[0].reshape(nh * 2 * CAP, MODEL_WIDTH)
    gate = jnp.concatenate([to_column(gate_ref[0, h]) for h in range(nh)], axis=0)
    w_gate = w_gate_ref[...].reshape(MODEL_WIDTH, fr)
    w_up = w_up_ref[...].reshape(MODEL_WIDTH, fr)
    gate_pre, up_pre = nn(x, w_gate), nn(x, w_up)
    sigma = 1.0 / (1.0 + jnp.exp(-gate_pre))
    swish = gate_pre * sigma
    activated = (swish * up_pre).astype(BF)
    out = nn(activated, w_down[...]).astype(BF).astype(F32)
    g = g_ref[0].reshape(nh * 2 * CAP, MODEL_WIDTH).astype(F32)
    d_gate = jnp.sum(out * g, axis=1, keepdims=True)
    d_out = (gate * g).astype(BF)
    scaled[0] = (gate * out).astype(BF).reshape(nh, 2 * CAP, MODEL_WIDTH)
    d_act = nt(d_out, w_down[...])
    d_gate_pre = (d_act * up_pre * sigma * (1.0 + gate_pre * (1.0 - sigma))).astype(BF)
    d_up_pre = (d_act * swish).astype(BF)
    back_rows = (nt(d_gate_pre, w_gate) + nt(d_up_pre, w_up)).astype(BF)
    d_rows[0] = back_rows.reshape(nh, 2 * CAP, MODEL_WIDTH)
    for h in range(nh):
        d_gate_row[0, h] = to_row(d_gate[h * 2 * CAP : (h + 1) * 2 * CAP])
    sum_gate[...] += tn(x, d_gate_pre)
    sum_up[...] += tn(x, d_up_pre)
    sum_down[...] += tn(activated, d_out)

    @pl.when(step == nz - 1)
    def _():
        for p in range(nb):
            own = slice(p * dl, (p + 1) * dl)
            grad_gate[p] = sum_gate[own].astype(BF)
            grad_up[p] = sum_up[own].astype(BF)
            grad_down[p] = sum_down[:, own].astype(BF)


def experts(nz, nh, x, g, gate, w_gate, w_up, w_down):
    nb, dl, fr = w_gate.shape
    shape = jax.ShapeDtypeStruct
    wide = pl.BlockSpec((1,) + x.shape[1:], lambda i: (i, 0, 0, 0))
    line = pl.BlockSpec((1,) + gate.shape[1:], lambda i: (i, 0, 0, 0))
    deep = pl.BlockSpec(w_gate.shape, lambda i: (0, 0, 0))
    flat = pl.BlockSpec(w_down.shape, lambda i: (0, 0, 0))
    return pl.pallas_call(
        functools.partial(experts_kernel, nz, nh),
        grid=(nz,),
        out_shape=(
            shape(x.shape, BF),
            shape(x.shape, BF),
            shape(gate.shape, F32),
            shape(w_gate.shape, BF),
            shape(w_up.shape, BF),
            shape(w_down.shape, BF),
        ),
        in_specs=[wide, wide, line, deep, deep, flat],
        out_specs=[wide, wide, line, deep, deep, flat],
        scratch_shapes=[
            pltpu.VMEM((fr, MODEL_WIDTH), BF),
            pltpu.VMEM((MODEL_WIDTH, fr), F32),
            pltpu.VMEM((MODEL_WIDTH, fr), F32),
            pltpu.VMEM((fr, MODEL_WIDTH), F32),
        ],
        compiler_params=pltpu.CompilerParams(vmem_limit_bytes=60 * 2**20),
        name="experts",
    )(x, g, gate, w_gate, w_up, w_down)


class Scatter:
    def __init__(self, at, bufs, sems):
        self.at, self.sems = at, sems
        self.sib_out, self.sib_in, self.z_out, self.z_in = (bufs.at[j] for j in range(4))

    def across(self, z):
        return remote(
            self.sib_out.at[z],
            self.sib_in.at[z],
            self.sems.at[0, z],
            self.sems.at[1, z],
            self.at.in_blk(self.at.sibling),
        )

    def along(self, z):
        at = self.at
        slot = jnp.where(z == at.z - 1, at.nz, z)
        ahead = jnp.clip(jnp.where(z > at.z, at.z + 1, at.z - 1), 0, at.nz - 1)
        return remote(
            self.z_out.at[z],
            self.z_in.at[slot],
            self.sems.at[2, z],
            self.sems.at[3, slot],
            at.in_blk(2 * ahead + at.core),
        )

    def arrived(self, slot):
        at = self.at
        remote(
            self.z_out.at[0],
            self.z_in.at[slot],
            self.sems.at[2, 0],
            self.sems.at[3, slot],
            at.in_blk(at.sibling),
        ).wait_recv()
        return self.z_in[slot].astype(F32)

    def give_sibling(self, z, value):
        self.sib_out[z] = value.astype(BF)
        self.across(z).start()

    def from_sibling(self, z):
        self.across(z).wait_recv()
        return self.sib_in[z].astype(F32)

    def give(self, z, value):
        at = self.at
        joins = ((z > at.z) & (at.z > 0)) | ((z < at.z) & (at.z < at.nz - 1))

        @pl.when(joins)
        def _():
            self.z_out[z] = (value + self.arrived(z)).astype(BF)

        @pl.when(jnp.logical_not(joins))
        def _():
            self.z_out[z] = value.astype(BF)

        self.along(z).start()

    def take(self, add):
        at = self.at
        pl.when(at.z > 0)(lambda: add(self.arrived(at.z), True))
        pl.when(at.z < at.nz - 1)(lambda: add(self.arrived(at.nz), False))

    def finish(self):
        at = self.at
        for z in range(at.nz):
            self.across(z).wait_send()
            pl.when(at.z != z)(lambda: self.along(z).wait_send())


class Total:
    def __init__(self, at, part, by_head, by_blk, whole, sems):
        self.at, self.part, self.by_head, self.by_blk, self.whole = at, part, by_head, by_blk, whole
        self.sems = sems

    def copy(self, stage, k):
        at = self.at
        peer = at.blk_peer(k) if stage == 1 else at.head_peer(k)
        device = at.in_blk(peer) if stage == 1 else at.in_head(peer)
        if stage == 0:
            src, dst = self.part.at[peer], self.by_head.at[at.h]
        elif stage == 1:
            src, dst = self.by_blk.at[at.b], self.by_blk.at[at.b]
        else:
            src, dst = self.whole.at[at.h], self.whole.at[at.h]
        return remote(src, dst, self.sems.at[0, stage, k], self.sems.at[1, stage, k], device)

    def peers(self, stage):
        return range(1, self.at.nb if stage == 1 else self.at.nh)

    def begin(self, stage):
        at = self.at
        if stage == 0:
            self.by_head[at.h] = self.part[at.h]
        elif stage == 1:
            self.by_blk[at.b] = sum_slots(self.by_head, at.nh)
        else:
            self.whole[at.h] = sum_slots(self.by_blk, at.nb)
        for k in self.peers(stage):
            self.copy(stage, k).start()

    def end(self, stage):
        for k in self.peers(stage):
            self.copy(stage, k).wait_recv()

    def finish(self):
        for stage in range(3):
            for k in self.peers(stage):
                self.copy(stage, k).wait_send()


def sum_slots(ref, n):
    total = ref[0]
    for s in range(1, n):
        total = total + ref[s]
    return total


def back_kernel(
    nb,
    nh,
    hl,
    kl,
    repeat,
    inputs,
    w_norm1,
    w_norm2,
    middle,
    n2,
    grad_out,
    router_t,
    slots,
    own_gates,
    d_gate_rows,
    wg,
    xg,
    ao_t,
    qt,
    kv,
    lse,
    attn_t,
    place_row,
    place_col,
    cos,
    sin,
    begin,
    d_rows,
    scaled,
    gate_sum,
    up_sum,
    down_sum,
    output,
    grad_in,
    grad_w,
    grad_n1,
    small_sum,
    gate_in,
    up_in,
    down_in,
    dbg,
    perm,
    d_rows_ref,
    do_t,
    delta,
    dq_t,
    own_kv,
    kv_bufs,
    w_part,
    w_bufs,
    out_send,
    out_recv,
    n1_head,
    n1_blk,
    s_head,
    s_blk,
    d_sems,
    kv_sems,
    w_sems,
    o_sems,
    n_sems,
    s_sems,
    small,
    back_rows,
    in_dgate,
    own_part,
    d_middle,
    dg_out,
    dg_in,
    sc_bufs,
    sc_sems,
    mix_sems,
    ret_sems,
    eout_sems,
    dgate_sems,
    dg_sems,
    local_sems,
    deal_sems,
    deal_local,
):
    at = Place(nb, nh)
    nz = at.nz
    rows = inputs.shape[0]
    group = rows * nh
    half = group // 2
    qw, kw = hl * HEAD_SIZE, kl * HEAD_SIZE
    width = qw + 2 * kw
    dl = MODEL_WIDTH // nb
    scale = 1.0 / math.sqrt(HEAD_SIZE)

    pair = 2 * rows
    own_expert = (at.b // repeat) * nh
    at.meet()

    def go(buf_out, buf_in, sems, z, k, count=1):
        peer = at.head_peer(k)
        return Copy(
            buf_out.at[z, peer],
            buf_in.at[z, at.h],
            count,
            sems.at[0, z, k],
            sems.at[1, z, k],
            at.in_head(peer),
        )

    def keep(buf_out, j, z):
        return pltpu.make_async_copy(buf_out.at[z, at.h], back_rows.at[z, at.h], local_sems.at[j, z])

    def far_first(body):
        def step(t, unused):
            d, side = nz - 1 - t // 2, lax.rem(t, 2)
            z = jnp.where(side == 0, at.z - d, at.z + d)

            @pl.when((z >= 0) & (z < nz) & ((d > 0) | (side == 0)))
            def _():
                body(z)

            return 0

        lax.fori_loop(0, 2 * nz, step, 0)

    def send_back(z):
        for k in range(1, nh):
            go(d_rows, back_rows, ret_sems, z, k).start()
            go(d_gate_rows, in_dgate, dgate_sems, z, k).start()
        keep(d_rows, 0, z).start()
        in_dgate[z, at.h] = d_gate_rows[z, at.h]

    far_first(send_back)
    sums_of = (gate_sum, up_sum, down_sum)
    deal = Deal(at, lambda j, p: sums_of[j].at[p], (gate_in, up_in, down_in), deal_sems, deal_local)
    n2_scatter = Scatter(at, sc_bufs, sc_sems)

    def dg_copy(p):
        return remote(
            dg_out.at[p], dg_in.at[at.b], dg_sems.at[0, p], dg_sems.at[1, at.b], at.in_blk(p)
        )

    def masks_of(z):
        return [
            hits(pick_targets(slots[z, pl.ds(own_expert + h, 1)], pair), pair) for h in range(nh)
        ]

    def spread(z, masks, scatter):
        hit_rows = jnp.concatenate([jnp.where(m, 1.0, 0.0).astype(BF) for m in masks], axis=0)
        part = tn(hit_rows, back_rows[z].reshape(nh * 2 * CAP, MODEL_WIDTH))
        own_part[0] = part[:rows]
        own_part[1] = part[rows:]
        scatter.give_sibling(z, own_part[1 - at.core])

        @pl.when(z != at.z)
        def _():
            scatter.give(z, own_part[at.core] + scatter.from_sibling(z))

    def gathered_part(scatter):
        own_part[2] = own_part[at.core] + scatter.from_sibling(at.z)

        def add(value, from_left):
            own_part[2] += value

        scatter.take(add)
        return own_part[2]

    def gather_back(z):
        for k in range(1, nh):
            go(d_rows, back_rows, ret_sems, z, k).wait_recv()
            go(d_gate_rows, in_dgate, dgate_sems, z, k).wait_recv()
        keep(d_rows, 0, z).wait()
        masks = masks_of(z)
        d_gates = jnp.concatenate(
            [
                jnp.sum(jnp.where(m, to_column(in_dgate[z, h]), 0.0), axis=0, keepdims=True)
                for h, m in enumerate(masks)
            ],
            axis=0,
        )
        dg_out[2 * z] = d_gates[:, :rows]
        dg_out[2 * z + 1] = d_gates[:, rows:]
        pl.when(z == at.z)(lambda: dg_copy(at.sibling).start())

        @pl.when(z != at.z)
        def _():
            dg_copy(2 * z).start()
            dg_copy(2 * z + 1).start()

        spread(z, masks, n2_scatter)

    deal.start(0, deal.share(BACK_DEAL[0]))
    far_first(gather_back)
    dg_in[at.b] = dg_out[at.b]
    for k in range(1, nb):
        p = at.blk_peer(k)
        remote(dg_out.at[p], dg_in.at[p], dg_sems.at[0, p], dg_sems.at[1, p], at.in_blk(p)).wait_recv()
    d_gates = jnp.concatenate(
        [sum_slots(dg_in.at[pl.ds(i * repeat, repeat)], repeat) for i in range(nb // repeat)], axis=0
    )
    d_logits = own_gates[...] * (
        d_gates - jnp.sum(own_gates[...] * d_gates, axis=0, keepdims=True)
    )
    from_logits = split_product(tn, d_logits, router_t[...])
    g_router = split_product(nn, d_logits, n2[...])
    mid = middle[...]
    factor_two = lax.rsqrt(jnp.mean(mid * mid, axis=-1, keepdims=True) + eps)
    unit_two = mid * factor_two
    d_n2 = gathered_part(n2_scatter) + from_logits
    weighted_two = d_n2 * w_norm2[...]
    d_middle[...] = grad_out[...].astype(F32) + factor_two * (
        weighted_two - unit_two * jnp.mean(unit_two * weighted_two, axis=-1, keepdims=True)
    )
    dbg[at.h] = d_middle[...].astype(BF)
    d_copies = [
        remote(dbg.at[at.h], dbg.at[at.h], d_sems.at[0, k], d_sems.at[1, k], at.in_head(at.head_peer(k)))
        for k in range(1, nh)
    ]
    for c in d_copies:
        c.start()
    g_norm = jnp.sum(d_n2 * unit_two, axis=0, keepdims=True)
    slab = MODEL_WIDTH // nh
    for h in range(nh):
        cols = slice(h * slab, (h + 1) * slab)
        small[h, :E] = g_router[:, cols]
        small[h, E:] = jnp.broadcast_to(g_norm[:, cols], (8, slab))
    totals = Total(at, small, s_head, s_blk, small_sum, s_sems)
    totals.begin(0)
    perm[...] = jnp.where(
        place_row[...] == sorted_place(at, half, (group, group), 0), 1.0, 0.0
    ).astype(BF)
    dq_t[...] = jnp.zeros(dq_t.shape, F32)
    for c in d_copies:
        c.wait_recv()

    def send_scaled(z):
        for k in range(1, nh):
            go(scaled, back_rows, eout_sems, z, k, 5).start()
        keep(scaled, 1, z).start()

    far_first(send_scaled)
    totals.end(0)
    totals.begin(1)
    deal.start(deal.share(BACK_DEAL[0]), deal.share(BACK_DEAL[1]))
    d_branch = dbg[...].reshape(group, MODEL_WIDTH)
    w = wg[...].reshape(MODEL_WIDTH, width + qw)
    d_attn_t = nn(d_branch, w[:, width:]).T.astype(BF)
    d_sorted = nt(d_attn_t, perm[...])
    for second in range(2):
        piece = d_sorted[:, second * half : (second + 1) * half]
        do_t[second] = piece.astype(BF)
        product = piece * attn_t[second]
        delta[second, :hl] = jnp.concatenate(
            [
                jnp.sum(product[a * HEAD_SIZE : (a + 1) * HEAD_SIZE], axis=0, keepdims=True)
                for a in range(hl)
            ],
            axis=0,
        )

    def step_back(p, second):
        block = kv[p, second]
        lse_all, delta_all = lse[second], delta[second]
        key_place = block_base(at, p, second, half) + lax.broadcasted_iota(
            jnp.int32, (half, half), 0
        )
        own_place = block_base(at, at.b, second, half) + lax.broadcasted_iota(
            jnp.int32, (half, half), 1
        )
        allowed = (key_place <= own_place) & (key_place >= begin[second])
        d_keys, d_values = [None] * kl, [None] * kl
        for a in range(hl):
            g = a // (hl // kl)
            rows_a = slice(a * HEAD_SIZE, (a + 1) * HEAD_SIZE)
            key = block[:, g * HEAD_SIZE : (g + 1) * HEAD_SIZE]
            value = block[:, kw + g * HEAD_SIZE : kw + (g + 1) * HEAD_SIZE]
            scores = jnp.where(allowed, nn(key, qt[second, rows_a]), -1e30)
            probs = jnp.exp(scores - lse_all[a : a + 1])
            d_probs = nn(value, do_t[second, rows_a])
            d_scores = (probs * (d_probs - delta_all[a : a + 1])).astype(BF)
            d_key = nt(qt[second, rows_a], d_scores)
            d_value = nt(do_t[second, rows_a], probs.astype(BF))
            d_keys[g] = d_key if d_keys[g] is None else d_keys[g] + d_key
            d_values[g] = d_value if d_values[g] is None else d_values[g] + d_value
            dq_t[second, rows_a] += tn(key, d_scores)
        return jnp.concatenate(d_keys + d_values, axis=0)

    scatter = Scatter(at, kv_bufs, kv_sems)

    def visit(step, unused):
        i = nz - 1 - step // 4
        second = lax.rem(step // 2, 2)
        same = lax.rem(step, 2) == 1
        z = jnp.where(second == 0, at.z - i, at.z + i)
        p = 2 * z + jnp.where(same, at.core, 1 - at.core)
        exists = (z >= 0) & (z < nz) & ((i > 0) | same | (at.core != second))

        @pl.when(exists)
        def _():
            part = step_back(p, second)

            @pl.when(jnp.logical_not(same))
            def _():
                scatter.give_sibling(z, part)

            @pl.when(same & (i > 0))
            def _():
                scatter.give(z, part + scatter.from_sibling(z))

            @pl.when(same & (i == 0))
            def _():
                own_kv[second] = part

        return 0

    lax.fori_loop(0, 4 * nz, visit, 0)
    totals.end(1)
    totals.begin(2)
    wide = 256

    def weight_part(first, left):
        for c in range(MODEL_WIDTH // wide):
            source = xg if first == 0 else dbg
            piece = nn(left, source[:, :, c * wide : (c + 1) * wide].reshape(group, wide))
            for j in range(wide // dl):
                w_part[c * (wide // dl) + j, first : first + left.shape[0]] = piece[
                    :, j * dl : (j + 1) * dl
                ]

    weight_part(width, ao_t[...])
    own_kv[at.core] += scatter.from_sibling(at.z)

    def add_kv(value, from_left):
        own_kv[1 if from_left else 0] += value

    scatter.take(add_kv)
    deal.start(deal.share(BACK_DEAL[1]), deal.share(BACK_DEAL[2]))

    d_sorted_t = []
    for second in range(2):
        cols = slice(second * half, (second + 1) * half)
        both = own_kv[second]
        turned = jnp.concatenate([dq_t[second] * scale, both[:kw]], axis=0)
        turned = turn_rows(turned, cos[:, cols], -sin[:, cols])
        d_sorted_t.append(jnp.concatenate([turned, both[kw:]], axis=0).astype(BF))
    back = jnp.where(place_col[...] == sorted_place(at, half, (group, group), 1), 1.0, 0.0).astype(BF)
    turned_back = (
        nt(back[:, :half], d_sorted_t[0]) + nt(back[:, half:], d_sorted_t[1])
    ).astype(BF)
    d_rows_ref[...] = turned_back.reshape(nh, rows, width)
    d_cols = (nn(d_sorted_t[0], perm[:half]) + nn(d_sorted_t[1], perm[half:])).astype(BF)
    o_copies = []
    for k in range(1, nh):
        peer = at.head_peer(k)
        out_send[peer] = nt(d_rows_ref[peer], w[:, :width]).astype(BF)
        c = remote(
            out_send.at[peer], out_recv.at[at.h], o_sems.at[0, k], o_sems.at[1, k], at.in_head(peer)
        )
        c.start()
        o_copies.append(c)
    own_normed = nt(d_rows_ref[at.h], w[:, :width])
    weight_part(0, d_cols)
    w_scatter = Scatter(at, w_bufs, w_sems)

    def w_pass(z):
        w_scatter.give_sibling(z, w_part[2 * z + 1 - at.core])

    def w_along(z):
        pl.when(z != at.z)(
            lambda: w_scatter.give(z, w_part[2 * z + at.core] + w_scatter.from_sibling(z))
        )

    far_first(w_pass)
    far_first(w_along)
    n2_scatter.finish()
    mix_scatter = Scatter(at, sc_bufs, mix_sems)

    def mix(z):
        for k in range(1, nh):
            go(scaled, back_rows, eout_sems, z, k).wait_recv()
        keep(scaled, 1, z).wait()
        spread(z, masks_of(z), mix_scatter)

    far_first(mix)
    deal.start(deal.share(BACK_DEAL[2]), deal.share(1))
    for k in range(1, nh):
        o_copies[k - 1].wait_recv()
        own_normed = own_normed + out_recv[lax.rem(at.h + nh - k, nh)].astype(F32)
    hidden = inputs[...].astype(F32)
    factor = lax.rsqrt(jnp.mean(hidden * hidden, axis=-1, keepdims=True) + eps)
    unit = hidden * factor
    n1_head[at.h] = jnp.sum(own_normed * unit, axis=0, keepdims=True)
    n1_copies = [
        remote(n1_head.at[at.h], n1_head.at[at.h], n_sems.at[0, k], n_sems.at[1, k], at.in_head(at.head_peer(k)))
        for k in range(1, nh)
    ]
    for c in n1_copies:
        c.start()
    weighted = own_normed * w_norm1[...]
    grad_in[...] = d_middle[...] + factor * (
        weighted - unit * jnp.mean(unit * weighted, axis=-1, keepdims=True)
    )
    for c in n1_copies:
        c.wait_recv()
    n1_blk[at.b] = sum_slots(n1_head, nh)
    n1_blk_copies = [
        remote(n1_blk.at[at.b], n1_blk.at[at.b], n_sems.at[0, nh + k], n_sems.at[1, nh + k], at.in_blk(at.blk_peer(k)))
        for k in range(1, nb)
    ]
    for c in n1_blk_copies:
        c.start()
    grad_w[...] = w_part[at.b] + w_scatter.from_sibling(at.z)

    def add_w(value, from_left):
        grad_w[...] += value

    w_scatter.take(add_w)

    for c in n1_blk_copies:
        c.wait_recv()
    grad_n1[...] = sum_slots(n1_blk, nb)
    totals.end(2)
    output[...] = (middle[...] + gathered_part(mix_scatter)).astype(BF)
    totals.finish()
    scatter.finish()
    mix_scatter.finish()

    def drain(z):
        for k in range(1, nh):
            go(d_rows, back_rows, ret_sems, z, k).wait_send()
            go(d_gate_rows, in_dgate, dgate_sems, z, k).wait_send()
            go(scaled, back_rows, eout_sems, z, k).wait_send()

    far_first(drain)
    deal.end()
    for k in range(1, nb):
        dg_copy(at.blk_peer(k)).wait_send()
    w_scatter.finish()
    for c in d_copies + o_copies + n1_copies + n1_blk_copies:
        c.wait_send()


def back(nb, nh, hl, kl, repeat, *operands):
    rows = operands[0].shape[0]
    group, half = rows * nh, rows * nh // 2
    nz, dl = nb // 2, MODEL_WIDTH // nb
    qw, kw = hl * HEAD_SIZE, kl * HEAD_SIZE
    width = qw + 2 * kw
    shape = jax.ShapeDtypeStruct
    dma = pltpu.SemaphoreType.DMA
    chunk = (E + 8, MODEL_WIDTH // nh)
    line = (nz, nh, 1, 2 * CAP)
    return pl.pallas_call(
        functools.partial(back_kernel, nb, nh, hl, kl, repeat),
        out_shape=(
            shape((rows, MODEL_WIDTH), BF),
            shape((rows, MODEL_WIDTH), F32),
            shape((width + qw, dl), F32),
            shape((1, MODEL_WIDTH), F32),
            shape((nh,) + chunk, F32),
            *(shape(v.shape, BF) for v in operands[-3:]),
        ),
        in_specs=[VMEM] * 22 + [ANY] * 5,
        out_specs=[VMEM] * 5 + [ANY] * 3,
        scratch_shapes=[
            pltpu.VMEM((nh, rows, MODEL_WIDTH), BF),
            pltpu.VMEM((group, group), BF),
            pltpu.VMEM((nh, rows, width), BF),
            pltpu.VMEM((2, qw, half), BF),
            pltpu.VMEM((2, max(hl, 8), half), F32),
            pltpu.VMEM((2, qw, half), F32),
            pltpu.VMEM((2, 2 * kw, half), F32),
            pltpu.VMEM((4, nz + 1, 2 * kw, half), BF),
            pltpu.VMEM((nb, width + qw, dl), F32),
            pltpu.VMEM((4, nz + 1, width + qw, dl), BF),
            pltpu.VMEM((nh, rows, MODEL_WIDTH), BF),
            pltpu.VMEM((nh, rows, MODEL_WIDTH), BF),
            pltpu.VMEM((nh, 1, MODEL_WIDTH), F32),
            pltpu.VMEM((nb, 1, MODEL_WIDTH), F32),
            pltpu.VMEM((nh,) + chunk, F32),
            pltpu.VMEM((nb,) + chunk, F32),
            dma((2, nh)),
            dma((4, nz + 1)),
            dma((4, nz + 1)),
            dma((2, nh)),
            dma((2, nh + nb)),
            dma((2, 3, max(nh, nb))),
            pltpu.VMEM((nh,) + chunk, F32),
            pltpu.VMEM((nz, nh, 2 * CAP, MODEL_WIDTH), BF),
            pltpu.VMEM(line, F32),
            pltpu.VMEM((3, rows, MODEL_WIDTH), F32),
            pltpu.VMEM((rows, MODEL_WIDTH), F32),
            pltpu.VMEM((nb, nh, rows), F32),
            pltpu.VMEM((nb, nh, rows), F32),
            pltpu.VMEM((4, nz + 1, rows, MODEL_WIDTH), BF),
            dma((4, nz + 1)),
            dma((4, nz + 1)),
            dma((2, nz, nh)),
            dma((2, nz, nh)),
            dma((2, nz, nh)),
            dma((2, nb)),
            dma((2, nz)),
            dma((2, 3, nb)),
            dma((3,)),
        ],
        compiler_params=pltpu.CompilerParams(collective_id=2, vmem_limit_bytes=62 * 2**20),
        name="back",
    )(*operands)


def on_device(
    inputs,
    token_place,
    lengths,
    w_norm1,
    w_query,
    key_weight,
    value_weight,
    w_out,
    w_norm2,
    router,
    routes,
    slot_order,
    w_gate,
    w_up,
    w_down,
    grad_out,
):
    rows = inputs.shape[0]
    nb, nh = lax.axis_size("blk"), lax.axis_size("head")
    nz = nb // 2
    hl = w_query.shape[1] // HEAD_SIZE
    kl = key_weight.shape[1] // HEAD_SIZE
    local, dl, hidden_units = w_gate.shape
    repeat = nb // local
    fr = hidden_units // repeat
    qw, kw = hl * HEAD_SIZE, kl * HEAD_SIZE

    own, begin_s, cos_o, sin_o, cos_s, sin_s, w_own = head_inputs(
        nb, nh, rows, token_place, lengths, w_query, key_weight, value_weight, w_out
    )
    gain_one, gain_two = w_norm1.reshape(1, -1), w_norm2.reshape(1, -1)
    place_row, place_col = own.reshape(1, -1), own.reshape(-1, 1)
    sizes = (nb, nh, hl, kl, repeat)
    router_t = router.T.reshape(nh, local, MODEL_WIDTH).transpose(1, 0, 2).reshape(E, MODEL_WIDTH)
    (
        gathered,
        weights,
        turned_q,
        kv,
        lse,
        attn_t,
        ao_t,
        middle,
        normed_two,
        slots,
        own_gates,
        in_gate,
        in_rows,
        in_g,
        *projections,
    ) = front(
        *sizes,
        inputs,
        gain_one,
        gain_two,
        w_own,
        place_row,
        place_col,
        cos_o,
        sin_o,
        begin_s,
        grad_out,
        slot_table(nb, nh, repeat, routes, slot_order),
        router_t,
        w_gate,
        w_up,
        w_down,
    )
    d_rows, scaled, d_gate_rows, *sums = experts(nz, nh, in_rows, in_g, in_gate, *projections)
    output, grad_inputs, grad_w, grad_norm1, small, *sums = back(
        *sizes,
        inputs,
        gain_one,
        gain_two,
        middle,
        normed_two,
        grad_out,
        router_t,
        slots,
        own_gates,
        d_gate_rows,
        weights,
        gathered,
        ao_t,
        turned_q,
        kv,
        lse,
        attn_t,
        place_row,
        place_col,
        cos_s,
        sin_s,
        begin_s,
        d_rows,
        scaled,
        *sums,
    )

    small = small.transpose(1, 0, 2).reshape(E + 8, MODEL_WIDTH)
    grad_router = (
        small[:E].reshape(local, nh, MODEL_WIDTH).transpose(1, 0, 2).reshape(E, MODEL_WIDTH).T
    )

    def whole_part(v, axis):
        v = v.reshape((local, repeat) + v.shape[1:])
        v = v if repeat == 1 else jnp.moveaxis(v, 1, axis)
        return v.reshape((local, dl, hidden_units) if axis == 2 else (local, hidden_units, dl)).astype(F32)

    return (
        output,
        grad_inputs,
        grad_norm1.reshape(-1),
        grad_w[:qw].T,
        grad_w[qw : qw + kw].T,
        grad_w[qw + kw : qw + 2 * kw].T,
        grad_w[qw + 2 * kw :],
        small[E],
        grad_router,
        whole_part(sums[0], 2),
        whole_part(sums[1], 2),
        whole_part(sums[2], 1),
    )


def solution(mesh):
    rows, whole = P(("blk", "head"), None), P()
    pair, out = P("blk", "head"), P("head", "blk")
    first, last = P("head", "blk", None), P("head", None, "blk")
    return jax.shard_map(
        on_device,
        mesh=mesh,
        in_specs=(
            rows,
            whole,
            whole,
            whole,
            pair,
            pair,
            pair,
            out,
            whole,
            whole,
            rows,
            rows,
            first,
            first,
            last,
            rows,
        ),
        out_specs=(
            rows,
            rows,
            whole,
            pair,
            pair,
            pair,
            out,
            whole,
            whole,
            first,
            first,
            last,
        ),
        check_vma=False,
    )
```

```python
import functools
import math

import jax
import jax.numpy as jnp
from jax import lax
from jax.experimental import pallas as pl
from jax.experimental.pallas import tpu as pltpu
from jax.sharding import PartitionSpec as P

MODEL_WIDTH = 1024
HEAD_SIZE = 64
E = 32
TOPK = 8
CAP = 40
MESH = pl.DeviceIdType.MESH
VMEM = pl.BlockSpec(memory_space=pltpu.VMEM)
ANY = pl.BlockSpec(memory_space=pl.ANY)
SMEM = pl.BlockSpec(memory_space=pltpu.SMEM)
BF = jnp.bfloat16
F32 = jnp.float32
FRONT_DEAL = (0.25, 0.8)
BACK_DEAL = (0.25, 0.42, 0.6)

eps = 1e-06
rope_base = 10000.0


def nn(a, b, **kw):
    return lax.dot_general(a, b, (((1,), (0,)), ((), ())), preferred_element_type=F32, **kw)


def nt(a, b, **kw):
    return lax.dot_general(a, b, (((1,), (1,)), ((), ())), preferred_element_type=F32, **kw)


def tn(a, b, **kw):
    return lax.dot_general(a, b, (((0,), (0,)), ((), ())), preferred_element_type=F32, **kw)


def remote(src, dst, send, recv, device):
    return pltpu.make_async_remote_copy(
        src_ref=src,
        dst_ref=dst,
        send_sem=send,
        recv_sem=recv,
        device_id=device,
        device_id_type=MESH,
    )


def start_pieces(copy, src, dst, count, *rest):
    rows = src.shape[0] // count
    for i in range(count):
        part = pl.ds(i * rows, rows)
        copy(src.at[part], dst.at[part], *rest).start()


class Copy:
    def __init__(self, src, dst, count, *rest):
        self.src, self.dst, self.count, self.rest = src, dst, count, rest

    def start(self):
        start_pieces(remote, self.src, self.dst, self.count, *self.rest)

    def wait_send(self):
        remote(self.src, self.dst, *self.rest).wait_send()

    def wait_recv(self):
        remote(self.src, self.dst, *self.rest).wait_recv()


def piece_count(shape, size):
    count = max(1, shape[0] * shape[1] * 2 // size)
    while shape[0] % (16 * count):
        count -= 1
    return count


class Place:
    def __init__(self, nb, nh):
        self.nb, self.nh, self.nz = nb, nh, nb // 2
        self.b, self.h = lax.axis_index("blk"), lax.axis_index("head")
        self.z, self.core = self.b // 2, lax.rem(self.b, 2)
        self.sibling = 2 * self.z + 1 - self.core

    def in_blk(self, b):
        return (b, self.h)

    def in_head(self, h):
        return (self.b, h)

    def head_peer(self, k):
        return lax.rem(self.h + k, self.nh)

    def blk_peer(self, k):
        return lax.rem(self.b + k, self.nb)

    def meet(self):
        barrier = pltpu.get_barrier_semaphore()
        for k in range(1, self.nh):
            pl.semaphore_signal(
                barrier, inc=1, device_id=self.in_head(self.head_peer(k)), device_id_type=MESH
            )
        for k in range(1, self.nb):
            pl.semaphore_signal(
                barrier, inc=1, device_id=self.in_blk(self.blk_peer(k)), device_id_type=MESH
            )
        pl.semaphore_wait(barrier, self.nh + self.nb - 2)


class Relay:
    def __init__(self, at, buf, send, recv, count=1):
        self.at, self.buf, self.send, self.recv, self.count = at, buf, send, recv, count

    def copy(self, s, way, device):
        return Copy(
            self.buf.at[s], self.buf.at[s], self.count, self.send.at[way, s], self.recv.at[s], device
        )

    def right(self, s):
        return self.copy(s, 0, self.at.in_blk(jnp.minimum(self.at.b + 2, self.at.nb - 2 + self.at.core)))

    def left(self, s):
        return self.copy(s, 1, self.at.in_blk(jnp.maximum(self.at.b - 2, self.at.core)))

    def across(self, s):
        return self.copy(s, 2, self.at.in_blk(self.at.sibling))

    def begin(self):
        at = self.at
        pl.when(at.z + 1 < at.nz)(lambda: self.right(at.b).start())
        pl.when(at.z > 0)(lambda: self.left(at.b).start())
        self.across(at.b).start()

    def hop(self, i):
        at = self.at

        @pl.when(at.z >= i)
        def _():
            s = at.b - 2 * i
            self.across(s).wait_recv()
            pl.when(at.z + 1 < at.nz)(lambda: self.right(s).start())
            self.across(s).start()

        @pl.when(at.z + i < at.nz)
        def _():
            s = at.b + 2 * i
            self.across(s).wait_recv()
            pl.when(at.z > 0)(lambda: self.left(s).start())
            self.across(s).start()

    def take_sibling(self, z):
        self.across(2 * z + 1 - self.at.core).wait_recv()

    def finish(self):
        at = self.at
        for i in range(at.nz):

            @pl.when(at.z >= i)
            def _():
                s = at.b - 2 * i
                pl.when(at.z + 1 < at.nz)(lambda: self.right(s).wait_send())
                self.across(s).wait_send()

            if i == 0:
                pl.when(at.z > 0)(lambda: self.left(at.b).wait_send())
            else:

                @pl.when(at.z + i < at.nz)
                def _():
                    s = at.b + 2 * i
                    pl.when(at.z > 0)(lambda: self.left(s).wait_send())
                    self.across(s).wait_send()

    def all(self):
        self.begin()
        for i in range(1, self.at.nz):
            self.hop(i)
        for z in range(self.at.nz):
            self.take_sibling(z)


class Deal:
    def __init__(self, at, chunk, arrived, sems, local_sems):
        self.at, self.chunk, self.arrived = at, chunk, arrived
        self.sems, self.local_sems = sems, local_sems

    def ends(self, j, k):
        at = self.at
        p = at.blk_peer(k)
        return (
            self.chunk(j, p),
            self.arrived[j].at[at.b],
            self.sems.at[0, j, k],
            self.sems.at[1, j, k],
            at.in_blk(p),
        )

    def own(self, j):
        at = self.at
        return pltpu.make_async_copy(
            self.chunk(j, at.b), self.arrived[j].at[at.b], self.local_sems.at[j]
        )

    def start(self, first, last):
        nb = self.at.nb
        if first == 0:
            for j in range(3):
                self.own(j).start()
        rest = [(0, k) for k in range(nb // 2 + 1, nb)]
        rest += [(j, k) for k in range(1, nb) for j in (1, 2)]
        for j, k in rest[int(len(rest) * first) : int(len(rest) * last)]:
            remote(*self.ends(j, k)).start()

    def one(self, z):
        remote(*self.ends(0, 1 + z)).start()

    def end(self):
        for j in range(3):
            for k in range(1, self.at.nb):
                move = remote(*self.ends(j, k))
                move.wait_recv()
                move.wait_send()
            self.own(j).wait()


def sorted_place(at, half, shape, axis):
    s = lax.broadcasted_iota(jnp.int32, shape, axis)
    return jnp.where(
        s < half, at.b * half + s, (2 * at.nb - 1 - at.b) * half + s - half
    )


def begin_of(place, lengths):
    start, begin = 0, jnp.zeros_like(place)
    for i in range(lengths.shape[0] - 1):
        start = start + lengths[i]
        begin = begin + jnp.where(place >= start, lengths[i], 0)
    return begin


def rotation(place, begin):
    shape = (HEAD_SIZE // 2, place.shape[1])
    index = lax.broadcasted_iota(jnp.int32, shape, 0).astype(F32)
    freq = jnp.exp(index * (-2.0 * math.log(rope_base) / HEAD_SIZE))
    angle = freq * (place - begin).astype(F32)
    return jnp.cos(angle), jnp.sin(angle)


def column_of(row):
    wide = jnp.broadcast_to(row.astype(F32), (128, row.shape[1]))
    return wide.T[:, :1].astype(jnp.int32)


def block_base(at, b, second, half):
    return jnp.where(second == 0, b * half, (2 * at.nb - 1 - b) * half)


def turn_rows(values, cos, sin):
    half = HEAD_SIZE // 2
    pieces = []
    for first in range(0, values.shape[0], HEAD_SIZE):
        lead = values[first : first + half]
        trail = values[first + half : first + HEAD_SIZE]
        pieces.append(lead * cos - trail * sin)
        pieces.append(trail * cos + lead * sin)
    return jnp.concatenate(pieces, axis=0)


def pick_targets(slots, pair_rows):
    lane = lax.broadcasted_iota(jnp.int32, slots.shape, 1)
    kept = (slots >= 0) & (slots < CAP)
    return jnp.where(kept, slots + jnp.where(lane >= pair_rows // 2, CAP, 0), -1)


def hits(target_row, pair_rows):
    return lax.broadcasted_iota(jnp.int32, (2 * CAP, pair_rows), 0) == target_row


def diagonal():
    shape = (2 * CAP, 2 * CAP)
    return lax.broadcasted_iota(jnp.int32, shape, 0) == lax.broadcasted_iota(jnp.int32, shape, 1)


def to_row(column):
    return jnp.sum(jnp.where(diagonal(), column, 0.0), axis=0, keepdims=True)


def to_column(row):
    return jnp.sum(jnp.where(diagonal(), row, 0.0), axis=1, keepdims=True)


def split_product(dot, left, right):
    high = left.astype(BF)
    low = (left - high.astype(F32)).astype(BF)
    return dot(high, right) + dot(low, right)


def front_kernel(
    nb,
    nh,
    hl,
    kl,
    repeat,
    inputs,
    w_norm1,
    w_norm2,
    w_own,
    places,
    lengths,
    grad_out,
    table,
    router_t,
    w_gate,
    w_up,
    w_down,
    xg,
    wg,
    qt,
    kv,
    lse,
    attn_t,
    ao_t,
    middle,
    n2,
    slots,
    own_gates,
    in_gate,
    in_rows,
    in_g,
    gate_in,
    up_in,
    down_in,
    ao,
    perm,
    top,
    total,
    out_send,
    out_recv,
    x_sems,
    w_send,
    w_recv,
    kv_send,
    kv_recv,
    o_sems,
    slot_all,
    g_all,
    n2_all,
    gates,
    out_rows,
    out_g,
    out_gate,
    s_send,
    s_recv,
    g_send,
    g_recv,
    n_send,
    n_recv,
    row_sems,
    g_sems,
    gate_sems,
    local_sems,
    deal_sems,
    deal_local,
    begin,
):
    at = Place(nb, nh)
    rows = inputs.shape[0]
    group = rows * nh
    half = group // 2
    qw, kw = hl * HEAD_SIZE, kl * HEAD_SIZE
    width = qw + 2 * kw

    hidden = inputs[...].astype(F32)
    unit = hidden * lax.rsqrt(jnp.mean(hidden * hidden, axis=-1, keepdims=True) + eps)
    xg[at.h] = (unit * w_norm1[...]).astype(BF)
    wg[at.b] = w_own[...]
    slot_all[at.b] = table[...]
    g_all[at.b] = grad_out[...]
    at.meet()
    x_copies = [
        remote(xg.at[at.h], xg.at[at.h], x_sems.at[0, k], x_sems.at[1, k], at.in_head(at.head_peer(k)))
        for k in range(1, nh)
    ]
    for c in x_copies:
        c.start()
    weights = Relay(at, wg, w_send, w_recv)
    weights.begin()
    slot_relay = Relay(at, slot_all, s_send, s_recv)
    slot_relay.begin()
    g_relay = Relay(at, g_all, g_send, g_recv, 4)
    g_relay.begin()
    pair = 2 * rows
    own_expert = (at.b // repeat) * nh

    def chunk(j, p):
        w_j = (w_gate, w_up, w_down)[j]
        if repeat == 1:
            return w_j.at[p]
        fr = w_gate.shape[2] // repeat
        part = pl.ds(pl.multiple_of(lax.rem(p, repeat) * fr, fr), fr)
        return w_j.at[p // repeat, part] if j == 2 else w_j.at[p // repeat, :, part]

    deal = Deal(at, chunk, (gate_in, up_in, down_in), deal_sems, deal_local)

    def go(buf_out, buf_in, sems, z, k, count=1):
        peer = at.head_peer(k)
        return Copy(
            buf_out.at[z, peer],
            buf_in.at[z, at.h],
            count,
            sems.at[0, z, k],
            sems.at[1, z, k],
            at.in_head(peer),
        )

    def keep(buf_out, buf_in, j, z):
        return pltpu.make_async_copy(buf_out.at[z, at.h], buf_in.at[z, at.h], local_sems.at[j, z])

    def outward(relay, body, first, last):
        def step(t, unused):
            d, side = t // 2, lax.rem(t, 2)
            z = jnp.where(side == 0, at.z - d, at.z + d)
            pl.when((side == 0) & (d > 0))(lambda: relay.hop(d))

            @pl.when((z >= 0) & (z < at.nz) & ((d > 0) | (side == 0)))
            def _():
                relay.take_sibling(z)
                body(z)

            return 0

        lax.fori_loop(2 * first, 2 * last, step, 0)

    def send_g(z):
        x = g_all[pl.ds(2 * z, 2)].reshape(pair, MODEL_WIDTH)
        for k in list(range(1, nh)) + [0]:
            peer = at.head_peer(k)
            hit = hits(pick_targets(slots[z, pl.ds(own_expert + peer, 1)], pair), pair)
            out_g[z, peer] = nn(jnp.where(hit, 1.0, 0.0).astype(BF), x).astype(BF)
            if k == 0:
                keep(out_g, in_g, 0, z).start()
            else:
                go(out_g, in_g, g_sems, z, k, 5).start()

    def send_rows(z):
        x = n2_all[pl.ds(2 * z, 2)].reshape(pair, MODEL_WIDTH)
        routed = slots[z] >= 0
        logits = jnp.where(routed, nt(router_t[...], x), -1e30)
        shifted = jnp.exp(logits - jnp.max(logits, axis=0, keepdims=True))
        shifted = jnp.where(routed, shifted, 0.0)
        gates[z] = shifted / jnp.sum(shifted, axis=0, keepdims=True)
        for k in list(range(1, nh)) + [0]:
            peer = at.head_peer(k)
            hit = hits(pick_targets(slots[z, pl.ds(own_expert + peer, 1)], pair), pair)
            gate_row = gates[z, pl.ds(own_expert + peer, 1)]
            gate = to_row(jnp.sum(jnp.where(hit, gate_row, 0.0), axis=1, keepdims=True))
            out_rows[z, peer] = nn(jnp.where(hit, 1.0, 0.0).astype(BF), x).astype(BF)
            if k == 0:
                keep(out_rows, in_rows, 1, z).start()
                in_gate[z, at.h] = gate
            else:
                go(out_rows, in_rows, row_sems, z, k).start()
                out_gate[z, peer] = gate
                go(out_gate, in_gate, gate_sems, z, k).start()

    place_row = places[at.b]
    cos, sin = rotation(place_row, begin_of(place_row, lengths))
    in_order = begin_of(sorted_place(at, half, (1, group), 1), lengths)
    begin[0] = in_order[:, :half]
    begin[1] = in_order[:, half:]
    place_col = column_of(place_row)
    perm[...] = jnp.where(
        place_row == sorted_place(at, half, (group, group), 0), 1.0, 0.0
    ).astype(BF)
    for i in range(1, nb // 2):
        slot_relay.hop(i)
        weights.hop(i)
    for z in range(nb // 2):
        slot_relay.take_sibling(z)
    for z in range(nb // 2):
        slots[z] = jnp.concatenate([slot_all[2 * z], slot_all[2 * z + 1]], axis=1)
    outward(g_relay, send_g, 0, 1)
    deal.start(0, FRONT_DEAL[0])
    for z in range(nb // 2):
        weights.take_sibling(z)
    for c in x_copies:
        c.wait_recv()
    x = xg[...].reshape(group, MODEL_WIDTH)
    w = wg[...].reshape(MODEL_WIDTH, width + qw)
    qkv_t = nn(x, w[:, :width]).T
    qkv_t = jnp.concatenate(
        [turn_rows(qkv_t[: qw + kw], cos, sin), qkv_t[qw + kw :]], axis=0
    ).astype(BF)
    order = perm[...]
    kv_rows = nt(order, qkv_t[qw:]).astype(BF)
    kv[at.b, 0] = kv_rows[:half]
    kv[at.b, 1] = kv_rows[half:]

    def kv_copy(p, second, way, device):
        return remote(
            kv.at[p, second], kv.at[p, second], kv_send.at[way, p], kv_recv.at[p], device
        )

    right = at.in_blk(jnp.minimum(at.b + 2, nb - 2 + at.core))
    left = at.in_blk(jnp.maximum(at.b - 2, at.core))
    across = at.in_blk(at.sibling)
    pl.when(at.z + 1 < at.nz)(lambda: kv_copy(at.b, 0, 0, right).start())
    pl.when(at.z > 0)(lambda: kv_copy(at.b, 1, 0, left).start())
    kv_copy(at.b, at.core, 1, across).start()
    q_cols = (nt(qkv_t[:qw], order) * (1.0 / math.sqrt(HEAD_SIZE))).astype(BF)
    qt[0] = q_cols[:, :half]
    qt[1] = q_cols[:, half:]
    outward(g_relay, send_g, 1, 2)
    top[...] = jnp.full(top.shape, -1e30, F32)
    total[...] = jnp.zeros(total.shape, F32)
    attn_t[...] = jnp.zeros(attn_t.shape, F32)

    def attend(p, second):
        old_top, old_total = top[second], total[second]
        tops, totals = [], []
        block = kv[p, second]
        key_place = block_base(at, p, second, half) + lax.broadcasted_iota(
            jnp.int32, (half, half), 0
        )
        own_place = block_base(at, at.b, second, half) + lax.broadcasted_iota(
            jnp.int32, (half, half), 1
        )
        allowed = (key_place <= own_place) & (key_place >= begin[second])
        for a in range(hl):
            g = a // (hl // kl)
            rows_a = slice(a * HEAD_SIZE, (a + 1) * HEAD_SIZE)
            scores = nn(block[:, g * HEAD_SIZE : (g + 1) * HEAD_SIZE], qt[second, rows_a])
            scores = jnp.where(allowed, scores, -1e30)
            old = old_top[a : a + 1]
            new = jnp.maximum(old, jnp.max(scores, axis=0, keepdims=True))
            probs = jnp.exp(scores - new)
            fade = jnp.exp(old - new)
            totals.append(old_total[a : a + 1] * fade + jnp.sum(probs, axis=0, keepdims=True))
            tops.append(new)
            attn_t[second, rows_a] = attn_t[second, rows_a] * fade + tn(
                block[:, kw + g * HEAD_SIZE : kw + (g + 1) * HEAD_SIZE], probs.astype(BF)
            )
        top[second, :hl] = jnp.concatenate(tops, axis=0)
        total[second, :hl] = jnp.concatenate(totals, axis=0)

    def visit(step, unused):
        i = step // 4
        second = lax.rem(step, 2)
        same = lax.rem(step // 2, 2) == 0
        z = jnp.where(second == 0, at.z - i, at.z + i)
        p = 2 * z + jnp.where(same, at.core, 1 - at.core)
        exists = (z >= 0) & (z < nb // 2) & ((i > 0) | same | (at.core != second))

        @pl.when(exists)
        def _():
            @pl.when(p != at.b)
            def _():
                kv_copy(p, second, 1, across).wait_recv()

            @pl.when((i > 0) & same)
            def _():
                @pl.when((second == 0) & (at.z + 1 < at.nz))
                def _():
                    kv_copy(p, second, 0, right).start()

                @pl.when((second == 1) & (at.z > 0))
                def _():
                    kv_copy(p, second, 0, left).start()

                kv_copy(p, second, 1, across).start()

            attend(p, second)

        return 0

    lax.fori_loop(0, 4 * (nb // 2), visit, 0)
    deal.start(FRONT_DEAL[0], FRONT_DEAL[1])
    for second in range(2):
        sums = total[second]
        for a in range(hl):
            rows_a = slice(a * HEAD_SIZE, (a + 1) * HEAD_SIZE)
            attn_t[second, rows_a] = attn_t[second, rows_a] / sums[a : a + 1]
    lse[...] = top[...] + jnp.log(total[...])
    back = jnp.where(place_col == sorted_place(at, half, (group, group), 1), 1.0, 0.0).astype(BF)
    attn_rows = (
        nt(back[:, :half], attn_t[0].astype(BF)) + nt(back[:, half:], attn_t[1].astype(BF))
    ).astype(BF)
    ao[...] = attn_rows
    ao_t[...] = (
        nn(attn_t[0].astype(BF), perm[:half]) + nn(attn_t[1].astype(BF), perm[half:])
    ).astype(BF)
    o_copies = []
    for k in range(nh):
        peer = at.head_peer(k)
        chunk = nt(ao[pl.ds(peer * rows, rows)], w[:, width:])
        if k == 0:
            middle[...] = hidden + chunk
            continue
        out_send[peer] = chunk.astype(BF)
        c = remote(
            out_send.at[peer], out_recv.at[at.h], o_sems.at[0, k], o_sems.at[1, k], at.in_head(peer)
        )
        c.start()
        o_copies.append(c)
    outward(g_relay, send_g, 2, at.nz)
    for k in range(1, nh):
        o_copies[k - 1].wait_recv()
        middle[...] += out_recv[lax.rem(at.h + nh - k, nh)].astype(F32)
    mid = middle[...]
    n2[...] = (
        mid * lax.rsqrt(jnp.mean(mid * mid, axis=-1, keepdims=True) + eps) * w_norm2[...]
    ).astype(BF)
    n2_all[at.b] = n2[...]
    n_relay = Relay(at, n2_all, n_send, n_recv)
    n_relay.begin()

    def send_both(z):
        send_rows(z)
        deal.one(z)

    outward(n_relay, send_both, 0, at.nz)
    deal.start(FRONT_DEAL[1], 1)
    own_gates[...] = jnp.where(at.core == 0, gates[at.z, :, :rows], gates[at.z, :, rows:])
    for relay in (weights, slot_relay, g_relay, n_relay):
        relay.finish()
    for c in x_copies + o_copies:
        c.wait_send()

    def drain(step, unused):
        i = step // 2
        second = lax.rem(step, 2)
        z = jnp.where(second == 0, at.z - i, at.z + i)
        p = 2 * z + at.core

        @pl.when((z >= 0) & (z < nb // 2))
        def _():
            @pl.when((second == 0) & (at.z + 1 < at.nz))
            def _():
                kv_copy(p, second, 0, right).wait_send()

            @pl.when((second == 1) & (at.z > 0))
            def _():
                kv_copy(p, second, 0, left).wait_send()

            @pl.when((i > 0) | (second == at.core))
            def _():
                kv_copy(p, second, 1, across).wait_send()

        return 0

    lax.fori_loop(0, nb, drain, 0)

    def end(z, unused):
        for k in range(1, nh):
            for move in (
                go(out_g, in_g, g_sems, z, k),
                go(out_rows, in_rows, row_sems, z, k),
                go(out_gate, in_gate, gate_sems, z, k),
            ):
                move.wait_recv()
                move.wait_send()
        keep(out_g, in_g, 0, z).wait()
        keep(out_rows, in_rows, 1, z).wait()
        return 0

    lax.fori_loop(0, at.nz, end, 0)
    deal.end()


def front(nb, nh, hl, kl, repeat, *operands):
    inputs, w_own = operands[0], operands[3]
    hidden_units = operands[9].shape[2]
    fr = hidden_units // repeat
    rows = inputs.shape[0]
    group, half = rows * nh, rows * nh // 2
    nz = nb // 2
    dl, wide = w_own.shape
    qw, kw = hl * HEAD_SIZE, kl * HEAD_SIZE
    shape = jax.ShapeDtypeStruct
    dma = pltpu.SemaphoreType.DMA
    chunk = (nz, nh, 2 * CAP, MODEL_WIDTH)
    line = (nz, nh, 1, 2 * CAP)
    relay_sems = [dma((3, nb)), dma((nb,))]
    return pl.pallas_call(
        functools.partial(front_kernel, nb, nh, hl, kl, repeat),
        out_shape=(
            shape((nh, rows, MODEL_WIDTH), BF),
            shape((nb, dl, wide), BF),
            shape((2, qw, half), BF),
            shape((nb, 2, half, 2 * kw), BF),
            shape((2, max(hl, 8), half), F32),
            shape((2, qw, half), F32),
            shape((qw, group), BF),
            shape((rows, MODEL_WIDTH), F32),
            shape((rows, MODEL_WIDTH), BF),
            shape((nz, E, 2 * rows), jnp.int32),
            shape((E, rows), F32),
            shape(line, F32),
            shape(chunk, BF),
            shape(chunk, BF),
            shape((nb, dl, fr), BF),
            shape((nb, dl, fr), BF),
            shape((nb, fr, dl), BF),
        ),
        in_specs=[VMEM] * 5 + [SMEM] + [VMEM] * 3 + [ANY] * 3,
        out_specs=[VMEM] * 12 + [ANY] * 5,
        scratch_shapes=[
            pltpu.VMEM((group, qw), BF),
            pltpu.VMEM((group, group), BF),
            pltpu.VMEM((2, max(hl, 8), half), F32),
            pltpu.VMEM((2, max(hl, 8), half), F32),
            pltpu.VMEM((nh, rows, MODEL_WIDTH), BF),
            pltpu.VMEM((nh, rows, MODEL_WIDTH), BF),
            dma((2, nh)),
            dma((3, nb)),
            dma((nb,)),
            dma((2, nb)),
            dma((nb,)),
            dma((2, nh)),
            pltpu.VMEM((nb, E, rows), jnp.int32),
            pltpu.VMEM((nb, rows, MODEL_WIDTH), BF),
            pltpu.VMEM((nb, rows, MODEL_WIDTH), BF),
            pltpu.VMEM((nz, E, 2 * rows), F32),
            pltpu.VMEM(chunk, BF),
            pltpu.VMEM(chunk, BF),
            pltpu.VMEM(line, F32),
            *relay_sems,
            *relay_sems,
            *relay_sems,
            dma((2, nz, nh)),
            dma((2, nz, nh)),
            dma((2, nz, nh)),
            dma((2, nz)),
            dma((2, 3, nb)),
            dma((3,)),
            pltpu.VMEM((2, 1, half), jnp.int32),
        ],
        compiler_params=pltpu.CompilerParams(collective_id=1, vmem_limit_bytes=60 * 2**20),
        name="front",
    )(*operands)


def slot_table(nb, nh, repeat, routes, slot_order):
    local = E // nh
    mine = (routes % local) * nh + routes // local
    match = mine.T[:, None, :] == jnp.arange(E, dtype=jnp.int32)[None, :, None]
    order = jnp.min(jnp.where(match, slot_order.T[:, None, :], 1 << 20), axis=0)
    before = jnp.sum((order[:, :, None] < order[:, None, :]).astype(jnp.int32), axis=1)
    return jnp.where(order < (1 << 20), before, -1)


def experts_kernel(
    nz,
    nh,
    x_ref,
    g_ref,
    gate_ref,
    w_gate_ref,
    w_up_ref,
    w_down_ref,
    d_rows,
    scaled,
    d_gate_row,
    grad_gate,
    grad_up,
    grad_down,
    w_down,
    sum_gate,
    sum_up,
    sum_down,
):
    step = pl.program_id(0)
    nb, dl, fr = w_gate_ref.shape

    @pl.when(step == 0)
    def _():
        w_down[...] = jnp.concatenate([w_down_ref[p] for p in range(nb)], axis=1)
        for total in (sum_gate, sum_up, sum_down):
            total[...] = jnp.zeros(total.shape, F32)

    x = x_ref[0].reshape(nh * 2 * CAP, MODEL_WIDTH)
    gate = jnp.concatenate([to_column(gate_ref[0, h]) for h in range(nh)], axis=0)
    w_gate = w_gate_ref[...].reshape(MODEL_WIDTH, fr)
    w_up = w_up_ref[...].reshape(MODEL_WIDTH, fr)
    gate_pre, up_pre = nn(x, w_gate), nn(x, w_up)
    sigma = 1.0 / (1.0 + jnp.exp(-gate_pre))
    swish = gate_pre * sigma
    activated = (swish * up_pre).astype(BF)
    out = nn(activated, w_down[...]).astype(BF).astype(F32)
    g = g_ref[0].reshape(nh * 2 * CAP, MODEL_WIDTH).astype(F32)
    d_gate = jnp.sum(out * g, axis=1, keepdims=True)
    d_out = (gate * g).astype(BF)
    scaled[0] = (gate * out).astype(BF).reshape(nh, 2 * CAP, MODEL_WIDTH)
    d_act = nt(d_out, w_down[...])
    d_gate_pre = (d_act * up_pre * sigma * (1.0 + gate_pre * (1.0 - sigma))).astype(BF)
    d_up_pre = (d_act * swish).astype(BF)
    back_rows = (nt(d_gate_pre, w_gate) + nt(d_up_pre, w_up)).astype(BF)
    d_rows[0] = back_rows.reshape(nh, 2 * CAP, MODEL_WIDTH)
    for h in range(nh):
        d_gate_row[0, h] = to_row(d_gate[h * 2 * CAP : (h + 1) * 2 * CAP])
    sum_gate[...] += tn(x, d_gate_pre)
    sum_up[...] += tn(x, d_up_pre)
    sum_down[...] += tn(activated, d_out)

    @pl.when(step == nz - 1)
    def _():
        for p in range(nb):
            own = slice(p * dl, (p + 1) * dl)
            grad_gate[p] = sum_gate[own].astype(BF)
            grad_up[p] = sum_up[own].astype(BF)
            grad_down[p] = sum_down[:, own].astype(BF)


def experts(nz, nh, x, g, gate, w_gate, w_up, w_down):
    nb, dl, fr = w_gate.shape
    shape = jax.ShapeDtypeStruct
    wide = pl.BlockSpec((1,) + x.shape[1:], lambda i: (i, 0, 0, 0))
    line = pl.BlockSpec((1,) + gate.shape[1:], lambda i: (i, 0, 0, 0))
    deep = pl.BlockSpec(w_gate.shape, lambda i: (0, 0, 0))
    flat = pl.BlockSpec(w_down.shape, lambda i: (0, 0, 0))
    return pl.pallas_call(
        functools.partial(experts_kernel, nz, nh),
        grid=(nz,),
        out_shape=(
            shape(x.shape, BF),
            shape(x.shape, BF),
            shape(gate.shape, F32),
            shape(w_gate.shape, BF),
            shape(w_up.shape, BF),
            shape(w_down.shape, BF),
        ),
        in_specs=[wide, wide, line, deep, deep, flat],
        out_specs=[wide, wide, line, deep, deep, flat],
        scratch_shapes=[
            pltpu.VMEM((fr, MODEL_WIDTH), BF),
            pltpu.VMEM((MODEL_WIDTH, fr), F32),
            pltpu.VMEM((MODEL_WIDTH, fr), F32),
            pltpu.VMEM((fr, MODEL_WIDTH), F32),
        ],
        compiler_params=pltpu.CompilerParams(vmem_limit_bytes=60 * 2**20),
        name="experts",
    )(x, g, gate, w_gate, w_up, w_down)


class Scatter:
    def __init__(self, at, bufs, sems):
        self.at, self.sems = at, sems
        self.sib_out, self.sib_in, self.z_out, self.z_in = (bufs.at[j] for j in range(4))

    def across(self, z):
        return remote(
            self.sib_out.at[z],
            self.sib_in.at[z],
            self.sems.at[0, z],
            self.sems.at[1, z],
            self.at.in_blk(self.at.sibling),
        )

    def along(self, z):
        at = self.at
        slot = jnp.where(z == at.z - 1, at.nz, z)
        ahead = jnp.clip(jnp.where(z > at.z, at.z + 1, at.z - 1), 0, at.nz - 1)
        return remote(
            self.z_out.at[z],
            self.z_in.at[slot],
            self.sems.at[2, z],
            self.sems.at[3, slot],
            at.in_blk(2 * ahead + at.core),
        )

    def arrived(self, slot):
        at = self.at
        remote(
            self.z_out.at[0],
            self.z_in.at[slot],
            self.sems.at[2, 0],
            self.sems.at[3, slot],
            at.in_blk(at.sibling),
        ).wait_recv()
        return self.z_in[slot].astype(F32)

    def give_sibling(self, z, value):
        self.sib_out[z] = value.astype(BF)
        self.across(z).start()

    def from_sibling(self, z):
        self.across(z).wait_recv()
        return self.sib_in[z].astype(F32)

    def give(self, z, value):
        at = self.at
        joins = ((z > at.z) & (at.z > 0)) | ((z < at.z) & (at.z < at.nz - 1))

        @pl.when(joins)
        def _():
            self.z_out[z] = (value + self.arrived(z)).astype(BF)

        @pl.when(jnp.logical_not(joins))
        def _():
            self.z_out[z] = value.astype(BF)

        self.along(z).start()

    def take(self, add):
        at = self.at
        pl.when(at.z > 0)(lambda: add(self.arrived(at.z), True))
        pl.when(at.z < at.nz - 1)(lambda: add(self.arrived(at.nz), False))

    def finish(self):
        at = self.at
        for z in range(at.nz):
            self.across(z).wait_send()
            pl.when(at.z != z)(lambda: self.along(z).wait_send())


class Total:
    def __init__(self, at, part, by_head, by_blk, whole, sems):
        self.at, self.part, self.by_head, self.by_blk, self.whole = at, part, by_head, by_blk, whole
        self.sems = sems

    def copy(self, stage, k):
        at = self.at
        peer = at.blk_peer(k) if stage == 1 else at.head_peer(k)
        device = at.in_blk(peer) if stage == 1 else at.in_head(peer)
        if stage == 0:
            src, dst = self.part.at[peer], self.by_head.at[at.h]
        elif stage == 1:
            src, dst = self.by_blk.at[at.b], self.by_blk.at[at.b]
        else:
            src, dst = self.whole.at[at.h], self.whole.at[at.h]
        return remote(src, dst, self.sems.at[0, stage, k], self.sems.at[1, stage, k], device)

    def peers(self, stage):
        return range(1, self.at.nb if stage == 1 else self.at.nh)

    def begin(self, stage):
        at = self.at
        if stage == 0:
            self.by_head[at.h] = self.part[at.h]
        elif stage == 1:
            self.by_blk[at.b] = sum_slots(self.by_head, at.nh)
        else:
            self.whole[at.h] = sum_slots(self.by_blk, at.nb)
        for k in self.peers(stage):
            self.copy(stage, k).start()

    def end(self, stage):
        for k in self.peers(stage):
            self.copy(stage, k).wait_recv()

    def finish(self):
        for stage in range(3):
            for k in self.peers(stage):
                self.copy(stage, k).wait_send()


def sum_slots(ref, n):
    total = ref[0]
    for s in range(1, n):
        total = total + ref[s]
    return total


def back_kernel(
    nb,
    nh,
    hl,
    kl,
    repeat,
    inputs,
    w_norm1,
    w_norm2,
    middle,
    n2,
    grad_out,
    router_t,
    slots,
    own_gates,
    d_gate_rows,
    wg,
    xg,
    ao_t,
    qt,
    kv,
    lse,
    attn_t,
    places,
    lengths,
    d_rows,
    scaled,
    gate_sum,
    up_sum,
    down_sum,
    output,
    grad_in,
    grad_w,
    grad_n1,
    small_sum,
    gate_in,
    up_in,
    down_in,
    dbg,
    perm,
    d_rows_ref,
    do_t,
    delta,
    dq_t,
    own_kv,
    kv_bufs,
    w_part,
    w_bufs,
    out_send,
    out_recv,
    n1_head,
    n1_blk,
    s_head,
    s_blk,
    d_sems,
    kv_sems,
    w_sems,
    o_sems,
    n_sems,
    s_sems,
    small,
    back_rows,
    in_dgate,
    own_part,
    d_middle,
    dg_out,
    dg_in,
    sc_bufs,
    sc_sems,
    mix_sems,
    ret_sems,
    eout_sems,
    dgate_sems,
    dg_sems,
    local_sems,
    deal_sems,
    deal_local,
    begin,
    *loaded,
):
    at = Place(nb, nh)
    nz = at.nz
    rows = inputs.shape[0]
    group = rows * nh
    half = group // 2
    qw, kw = hl * HEAD_SIZE, kl * HEAD_SIZE
    width = qw + 2 * kw
    dl = MODEL_WIDTH // nb
    scale = 1.0 / math.sqrt(HEAD_SIZE)

    pair = 2 * rows
    own_expert = (at.b // repeat) * nh
    at.meet()

    def go(buf_out, buf_in, sems, z, k, count=1):
        peer = at.head_peer(k)
        return Copy(
            buf_out.at[z, peer],
            buf_in.at[z, at.h],
            count,
            sems.at[0, z, k],
            sems.at[1, z, k],
            at.in_head(peer),
        )

    def keep(buf_out, j, z):
        return pltpu.make_async_copy(buf_out.at[z, at.h], back_rows.at[z, at.h], local_sems.at[j, z])

    def far_first(body):
        def step(t, unused):
            d, side = nz - 1 - t // 2, lax.rem(t, 2)
            z = jnp.where(side == 0, at.z - d, at.z + d)

            @pl.when((z >= 0) & (z < nz) & ((d > 0) | (side == 0)))
            def _():
                body(z)

            return 0

        lax.fori_loop(0, 2 * nz, step, 0)

    def send_back(z):
        for k in range(1, nh):
            go(d_rows, back_rows, ret_sems, z, k).start()
            go(d_gate_rows, in_dgate, dgate_sems, z, k).start()
        keep(d_rows, 0, z).start()
        in_dgate[z, at.h] = d_gate_rows[z, at.h]

    far_first(send_back)
    load_sems = loaded[-1]
    sources = (wg, xg, ao_t, qt, kv, attn_t)
    loads = [
        pltpu.make_async_copy(src, dst, load_sems.at[i])
        for i, (src, dst) in enumerate(zip(sources, loaded[:-1]))
    ]
    for c in loads:
        c.start()
    wg, xg, ao_t, qt, kv, attn_t = loaded[:-1]
    place_row = places[at.b]
    sorted_row = sorted_place(at, half, (1, group), 1)
    in_order = begin_of(sorted_row, lengths)
    begin[0] = in_order[:, :half]
    begin[1] = in_order[:, half:]
    cos, sin = rotation(sorted_row, in_order)
    place_col = column_of(place_row)
    sums_of = (gate_sum, up_sum, down_sum)
    deal = Deal(at, lambda j, p: sums_of[j].at[p], (gate_in, up_in, down_in), deal_sems, deal_local)
    deal.start(0, BACK_DEAL[0])
    n2_scatter = Scatter(at, sc_bufs, sc_sems)

    def dg_copy(p):
        return remote(
            dg_out.at[p], dg_in.at[at.b], dg_sems.at[0, p], dg_sems.at[1, at.b], at.in_blk(p)
        )

    def masks_of(z):
        return [
            hits(pick_targets(slots[z, pl.ds(own_expert + h, 1)], pair), pair) for h in range(nh)
        ]

    def spread(z, masks, scatter):
        hit_rows = jnp.concatenate([jnp.where(m, 1.0, 0.0).astype(BF) for m in masks], axis=0)
        part = tn(hit_rows, back_rows[z].reshape(nh * 2 * CAP, MODEL_WIDTH))
        own_part[0] = part[:rows]
        own_part[1] = part[rows:]
        scatter.give_sibling(z, own_part[1 - at.core])

        @pl.when(z != at.z)
        def _():
            scatter.give(z, own_part[at.core] + scatter.from_sibling(z))

    def gathered_part(scatter):
        own_part[2] = own_part[at.core] + scatter.from_sibling(at.z)

        def add(value, from_left):
            own_part[2] += value

        scatter.take(add)
        return own_part[2]

    def gather_back(z):
        for k in range(1, nh):
            go(d_rows, back_rows, ret_sems, z, k).wait_recv()
            go(d_gate_rows, in_dgate, dgate_sems, z, k).wait_recv()
        keep(d_rows, 0, z).wait()
        masks = masks_of(z)
        d_gates = jnp.concatenate(
            [
                jnp.sum(jnp.where(m, to_column(in_dgate[z, h]), 0.0), axis=0, keepdims=True)
                for h, m in enumerate(masks)
            ],
            axis=0,
        )
        dg_out[2 * z] = d_gates[:, :rows]
        dg_out[2 * z + 1] = d_gates[:, rows:]
        pl.when(z == at.z)(lambda: dg_copy(at.sibling).start())

        @pl.when(z != at.z)
        def _():
            dg_copy(2 * z).start()
            dg_copy(2 * z + 1).start()

        spread(z, masks, n2_scatter)
        deal.one(z)

    far_first(gather_back)
    dg_in[at.b] = dg_out[at.b]
    for k in range(1, nb):
        p = at.blk_peer(k)
        remote(dg_out.at[p], dg_in.at[p], dg_sems.at[0, p], dg_sems.at[1, p], at.in_blk(p)).wait_recv()
    d_gates = jnp.concatenate(
        [sum_slots(dg_in.at[pl.ds(i * repeat, repeat)], repeat) for i in range(nb // repeat)], axis=0
    )
    d_logits = own_gates[...] * (
        d_gates - jnp.sum(own_gates[...] * d_gates, axis=0, keepdims=True)
    )
    from_logits = split_product(tn, d_logits, router_t[...])
    g_router = split_product(nn, d_logits, n2[...])
    mid = middle[...]
    factor_two = lax.rsqrt(jnp.mean(mid * mid, axis=-1, keepdims=True) + eps)
    unit_two = mid * factor_two
    d_n2 = gathered_part(n2_scatter) + from_logits
    weighted_two = d_n2 * w_norm2[...]
    d_middle[...] = grad_out[...].astype(F32) + factor_two * (
        weighted_two - unit_two * jnp.mean(unit_two * weighted_two, axis=-1, keepdims=True)
    )
    dbg[at.h] = d_middle[...].astype(BF)
    d_copies = [
        remote(dbg.at[at.h], dbg.at[at.h], d_sems.at[0, k], d_sems.at[1, k], at.in_head(at.head_peer(k)))
        for k in range(1, nh)
    ]
    for c in d_copies:
        c.start()
    g_norm = jnp.sum(d_n2 * unit_two, axis=0, keepdims=True)
    slab = MODEL_WIDTH // nh
    for h in range(nh):
        cols = slice(h * slab, (h + 1) * slab)
        small[h, :E] = g_router[:, cols]
        small[h, E:] = jnp.broadcast_to(g_norm[:, cols], (8, slab))
    totals = Total(at, small, s_head, s_blk, small_sum, s_sems)
    totals.begin(0)
    perm[...] = jnp.where(
        place_row == sorted_place(at, half, (group, group), 0), 1.0, 0.0
    ).astype(BF)
    dq_t[...] = jnp.zeros(dq_t.shape, F32)
    for c in d_copies:
        c.wait_recv()

    def send_scaled(z):
        for k in range(1, nh):
            go(scaled, back_rows, eout_sems, z, k, 5).start()
        keep(scaled, 1, z).start()

    far_first(send_scaled)
    totals.end(0)
    totals.begin(1)
    deal.start(BACK_DEAL[0], BACK_DEAL[1])
    for c in loads:
        c.wait()
    d_branch = dbg[...].reshape(group, MODEL_WIDTH)
    w = wg[...].reshape(MODEL_WIDTH, width + qw)
    d_attn_t = nn(d_branch, w[:, width:]).T.astype(BF)
    d_sorted = nt(d_attn_t, perm[...])
    for second in range(2):
        piece = d_sorted[:, second * half : (second + 1) * half]
        do_t[second] = piece.astype(BF)
        product = piece * attn_t[second]
        delta[second, :hl] = jnp.concatenate(
            [
                jnp.sum(product[a * HEAD_SIZE : (a + 1) * HEAD_SIZE], axis=0, keepdims=True)
                for a in range(hl)
            ],
            axis=0,
        )

    def step_back(p, second):
        block = kv[p, second]
        lse_all, delta_all = lse[second], delta[second]
        key_place = block_base(at, p, second, half) + lax.broadcasted_iota(
            jnp.int32, (half, half), 0
        )
        own_place = block_base(at, at.b, second, half) + lax.broadcasted_iota(
            jnp.int32, (half, half), 1
        )
        allowed = (key_place <= own_place) & (key_place >= begin[second])
        d_keys, d_values = [None] * kl, [None] * kl
        for a in range(hl):
            g = a // (hl // kl)
            rows_a = slice(a * HEAD_SIZE, (a + 1) * HEAD_SIZE)
            key = block[:, g * HEAD_SIZE : (g + 1) * HEAD_SIZE]
            value = block[:, kw + g * HEAD_SIZE : kw + (g + 1) * HEAD_SIZE]
            scores = jnp.where(allowed, nn(key, qt[second, rows_a]), -1e30)
            probs = jnp.exp(scores - lse_all[a : a + 1])
            d_probs = nn(value, do_t[second, rows_a])
            d_scores = (probs * (d_probs - delta_all[a : a + 1])).astype(BF)
            d_key = nt(qt[second, rows_a], d_scores)
            d_value = nt(do_t[second, rows_a], probs.astype(BF))
            d_keys[g] = d_key if d_keys[g] is None else d_keys[g] + d_key
            d_values[g] = d_value if d_values[g] is None else d_values[g] + d_value
            dq_t[second, rows_a] += tn(key, d_scores)
        return jnp.concatenate(d_keys + d_values, axis=0)

    scatter = Scatter(at, kv_bufs, kv_sems)

    def visit(step, unused):
        i = nz - 1 - step // 4
        second = lax.rem(step // 2, 2)
        same = lax.rem(step, 2) == 1
        z = jnp.where(second == 0, at.z - i, at.z + i)
        p = 2 * z + jnp.where(same, at.core, 1 - at.core)
        exists = (z >= 0) & (z < nz) & ((i > 0) | same | (at.core != second))

        @pl.when(exists)
        def _():
            part = step_back(p, second)

            @pl.when(jnp.logical_not(same))
            def _():
                scatter.give_sibling(z, part)

            @pl.when(same & (i > 0))
            def _():
                scatter.give(z, part + scatter.from_sibling(z))

            @pl.when(same & (i == 0))
            def _():
                own_kv[second] = part

        return 0

    lax.fori_loop(0, 4 * nz, visit, 0)
    deal.start(BACK_DEAL[1], BACK_DEAL[2])
    totals.end(1)
    totals.begin(2)
    wide = 256

    def weight_part(first, left):
        for c in range(MODEL_WIDTH // wide):
            source = xg if first == 0 else dbg
            piece = nn(left, source[:, :, c * wide : (c + 1) * wide].reshape(group, wide))
            for j in range(wide // dl):
                w_part[c * (wide // dl) + j, first : first + left.shape[0]] = piece[
                    :, j * dl : (j + 1) * dl
                ]

    weight_part(width, ao_t[...])
    own_kv[at.core] += scatter.from_sibling(at.z)

    def add_kv(value, from_left):
        own_kv[1 if from_left else 0] += value

    scatter.take(add_kv)

    d_sorted_t = []
    for second in range(2):
        cols = slice(second * half, (second + 1) * half)
        both = own_kv[second]
        turned = jnp.concatenate([dq_t[second] * scale, both[:kw]], axis=0)
        turned = turn_rows(turned, cos[:, cols], -sin[:, cols])
        d_sorted_t.append(jnp.concatenate([turned, both[kw:]], axis=0).astype(BF))
    back = jnp.where(place_col == sorted_place(at, half, (group, group), 1), 1.0, 0.0).astype(BF)
    turned_back = (
        nt(back[:, :half], d_sorted_t[0]) + nt(back[:, half:], d_sorted_t[1])
    ).astype(BF)
    d_rows_ref[...] = turned_back.reshape(nh, rows, width)
    d_cols = (nn(d_sorted_t[0], perm[:half]) + nn(d_sorted_t[1], perm[half:])).astype(BF)
    o_copies = []
    for k in range(1, nh):
        peer = at.head_peer(k)
        out_send[peer] = nt(d_rows_ref[peer], w[:, :width]).astype(BF)
        c = remote(
            out_send.at[peer], out_recv.at[at.h], o_sems.at[0, k], o_sems.at[1, k], at.in_head(peer)
        )
        c.start()
        o_copies.append(c)
    own_normed = nt(d_rows_ref[at.h], w[:, :width])
    weight_part(0, d_cols)
    w_scatter = Scatter(at, w_bufs, w_sems)

    def w_pass(z):
        w_scatter.give_sibling(z, w_part[2 * z + 1 - at.core])

    def w_along(z):
        pl.when(z != at.z)(
            lambda: w_scatter.give(z, w_part[2 * z + at.core] + w_scatter.from_sibling(z))
        )

    far_first(w_pass)
    far_first(w_along)
    n2_scatter.finish()
    mix_scatter = Scatter(at, sc_bufs, mix_sems)

    def mix(z):
        for k in range(1, nh):
            go(scaled, back_rows, eout_sems, z, k).wait_recv()
        keep(scaled, 1, z).wait()
        spread(z, masks_of(z), mix_scatter)

    far_first(mix)
    deal.start(BACK_DEAL[2], 1)
    for k in range(1, nh):
        o_copies[k - 1].wait_recv()
        own_normed = own_normed + out_recv[lax.rem(at.h + nh - k, nh)].astype(F32)
    hidden = inputs[...].astype(F32)
    factor = lax.rsqrt(jnp.mean(hidden * hidden, axis=-1, keepdims=True) + eps)
    unit = hidden * factor
    n1_head[at.h] = jnp.sum(own_normed * unit, axis=0, keepdims=True)
    n1_copies = [
        remote(n1_head.at[at.h], n1_head.at[at.h], n_sems.at[0, k], n_sems.at[1, k], at.in_head(at.head_peer(k)))
        for k in range(1, nh)
    ]
    for c in n1_copies:
        c.start()
    weighted = own_normed * w_norm1[...]
    grad_in[...] = d_middle[...] + factor * (
        weighted - unit * jnp.mean(unit * weighted, axis=-1, keepdims=True)
    )
    for c in n1_copies:
        c.wait_recv()
    n1_blk[at.b] = sum_slots(n1_head, nh)
    n1_blk_copies = [
        remote(n1_blk.at[at.b], n1_blk.at[at.b], n_sems.at[0, nh + k], n_sems.at[1, nh + k], at.in_blk(at.blk_peer(k)))
        for k in range(1, nb)
    ]
    for c in n1_blk_copies:
        c.start()
    grad_w[...] = w_part[at.b] + w_scatter.from_sibling(at.z)

    def add_w(value, from_left):
        grad_w[...] += value

    w_scatter.take(add_w)

    for c in n1_blk_copies:
        c.wait_recv()
    grad_n1[...] = sum_slots(n1_blk, nb)
    totals.end(2)
    output[...] = (middle[...] + gathered_part(mix_scatter)).astype(BF)
    totals.finish()
    scatter.finish()
    mix_scatter.finish()

    def drain(z):
        for k in range(1, nh):
            go(d_rows, back_rows, ret_sems, z, k).wait_send()
            go(d_gate_rows, in_dgate, dgate_sems, z, k).wait_send()
            go(scaled, back_rows, eout_sems, z, k).wait_send()

    far_first(drain)
    deal.end()
    for k in range(1, nb):
        dg_copy(at.blk_peer(k)).wait_send()
    w_scatter.finish()
    for c in d_copies + o_copies + n1_copies + n1_blk_copies:
        c.wait_send()


def back(nb, nh, hl, kl, repeat, *operands):
    rows = operands[0].shape[0]
    group, half = rows * nh, rows * nh // 2
    nz, dl = nb // 2, MODEL_WIDTH // nb
    qw, kw = hl * HEAD_SIZE, kl * HEAD_SIZE
    width = qw + 2 * kw
    shape = jax.ShapeDtypeStruct
    dma = pltpu.SemaphoreType.DMA
    chunk = (E + 8, MODEL_WIDTH // nh)
    line = (nz, nh, 1, 2 * CAP)
    return pl.pallas_call(
        functools.partial(back_kernel, nb, nh, hl, kl, repeat),
        out_shape=(
            shape((rows, MODEL_WIDTH), BF),
            shape((rows, MODEL_WIDTH), F32),
            shape((width + qw, dl), F32),
            shape((1, MODEL_WIDTH), F32),
            shape((nh,) + chunk, F32),
            *(shape(v.shape, BF) for v in operands[-3:]),
        ),
        in_specs=[VMEM] * 10 + [ANY] * 4 + [ANY, VMEM, ANY] + [VMEM, SMEM] + [ANY] * 5,
        out_specs=[VMEM] * 5 + [ANY] * 3,
        scratch_shapes=[
            pltpu.VMEM((nh, rows, MODEL_WIDTH), BF),
            pltpu.VMEM((group, group), BF),
            pltpu.VMEM((nh, rows, width), BF),
            pltpu.VMEM((2, qw, half), BF),
            pltpu.VMEM((2, max(hl, 8), half), F32),
            pltpu.VMEM((2, qw, half), F32),
            pltpu.VMEM((2, 2 * kw, half), F32),
            pltpu.VMEM((4, nz + 1, 2 * kw, half), BF),
            pltpu.VMEM((nb, width + qw, dl), F32),
            pltpu.VMEM((4, nz + 1, width + qw, dl), BF),
            pltpu.VMEM((nh, rows, MODEL_WIDTH), BF),
            pltpu.VMEM((nh, rows, MODEL_WIDTH), BF),
            pltpu.VMEM((nh, 1, MODEL_WIDTH), F32),
            pltpu.VMEM((nb, 1, MODEL_WIDTH), F32),
            pltpu.VMEM((nh,) + chunk, F32),
            pltpu.VMEM((nb,) + chunk, F32),
            dma((2, nh)),
            dma((4, nz + 1)),
            dma((4, nz + 1)),
            dma((2, nh)),
            dma((2, nh + nb)),
            dma((2, 3, max(nh, nb))),
            pltpu.VMEM((nh,) + chunk, F32),
            pltpu.VMEM((nz, nh, 2 * CAP, MODEL_WIDTH), BF),
            pltpu.VMEM(line, F32),
            pltpu.VMEM((3, rows, MODEL_WIDTH), F32),
            pltpu.VMEM((rows, MODEL_WIDTH), F32),
            pltpu.VMEM((nb, nh, rows), F32),
            pltpu.VMEM((nb, nh, rows), F32),
            pltpu.VMEM((4, nz + 1, rows, MODEL_WIDTH), BF),
            dma((4, nz + 1)),
            dma((4, nz + 1)),
            dma((2, nz, nh)),
            dma((2, nz, nh)),
            dma((2, nz, nh)),
            dma((2, nb)),
            dma((2, nz)),
            dma((2, 3, nb)),
            dma((3,)),
            pltpu.VMEM((2, 1, half), jnp.int32),
            *(pltpu.VMEM(operands[i].shape, operands[i].dtype) for i in (10, 11, 12, 13, 14, 16)),
            dma((6,)),
        ],
        compiler_params=pltpu.CompilerParams(collective_id=2, vmem_limit_bytes=62 * 2**20),
        name="back",
    )(*operands)


def on_device(
    inputs,
    token_place,
    lengths,
    w_norm1,
    w_query,
    key_weight,
    value_weight,
    w_out,
    w_norm2,
    router,
    routes,
    slot_order,
    w_gate,
    w_up,
    w_down,
    grad_out,
):
    rows = inputs.shape[0]
    nb, nh = lax.axis_size("blk"), lax.axis_size("head")
    nz = nb // 2
    hl = w_query.shape[1] // HEAD_SIZE
    kl = key_weight.shape[1] // HEAD_SIZE
    local, dl, hidden_units = w_gate.shape
    repeat = nb // local
    fr = hidden_units // repeat
    qw, kw = hl * HEAD_SIZE, kl * HEAD_SIZE

    w_own = jnp.concatenate([w_query, key_weight, value_weight, w_out.T], axis=1)
    places = token_place.reshape(nb, 1, rows * nh)
    gain_one, gain_two = w_norm1.reshape(1, -1), w_norm2.reshape(1, -1)
    sizes = (nb, nh, hl, kl, repeat)
    router_t = router.T.reshape(nh, local, MODEL_WIDTH).transpose(1, 0, 2).reshape(E, MODEL_WIDTH)
    (
        gathered,
        weights,
        turned_q,
        kv,
        lse,
        attn_t,
        ao_t,
        middle,
        normed_two,
        slots,
        own_gates,
        in_gate,
        in_rows,
        in_g,
        *projections,
    ) = front(
        *sizes,
        inputs,
        gain_one,
        gain_two,
        w_own,
        places,
        lengths,
        grad_out,
        slot_table(nb, nh, repeat, routes, slot_order),
        router_t,
        w_gate,
        w_up,
        w_down,
    )
    d_rows, scaled, d_gate_rows, *sums = experts(nz, nh, in_rows, in_g, in_gate, *projections)
    output, grad_inputs, grad_w, grad_norm1, small, *sums = back(
        *sizes,
        inputs,
        gain_one,
        gain_two,
        middle,
        normed_two,
        grad_out,
        router_t,
        slots,
        own_gates,
        d_gate_rows,
        weights,
        gathered,
        ao_t,
        turned_q,
        kv,
        lse,
        attn_t,
        places,
        lengths,
        d_rows,
        scaled,
        *sums,
    )

    small = small.transpose(1, 0, 2).reshape(E + 8, MODEL_WIDTH)
    grad_router = (
        small[:E].reshape(local, nh, MODEL_WIDTH).transpose(1, 0, 2).reshape(E, MODEL_WIDTH).T
    )

    def whole_part(v, axis):
        v = v.reshape((local, repeat) + v.shape[1:])
        v = v if repeat == 1 else jnp.moveaxis(v, 1, axis)
        return v.reshape((local, dl, hidden_units) if axis == 2 else (local, hidden_units, dl)).astype(F32)

    return (
        output,
        grad_inputs,
        grad_norm1.reshape(-1),
        grad_w[:qw].T,
        grad_w[qw : qw + kw].T,
        grad_w[qw + kw : qw + 2 * kw].T,
        grad_w[qw + 2 * kw :],
        small[E],
        grad_router,
        whole_part(sums[0], 2),
        whole_part(sums[1], 2),
        whole_part(sums[2], 1),
    )


def solution(mesh):
    rows, whole = P(("blk", "head"), None), P()
    pair, out = P("blk", "head"), P("head", "blk")
    first, last = P("head", "blk", None), P("head", None, "blk")
    return jax.shard_map(
        on_device,
        mesh=mesh,
        in_specs=(
            rows,
            whole,
            whole,
            whole,
            pair,
            pair,
            pair,
            out,
            whole,
            whole,
            rows,
            rows,
            first,
            first,
            last,
            rows,
        ),
        out_specs=(
            rows,
            rows,
            whole,
            pair,
            pair,
            pair,
            out,
            whole,
            whole,
            first,
            first,
            last,
        ),
        check_vma=False,
    )
```

```python
import functools
import math

import jax
import jax.numpy as jnp
from jax import lax
from jax.experimental import pallas as pl
from jax.experimental.pallas import tpu as pltpu
from jax.sharding import PartitionSpec as P

MODEL_WIDTH = 1024
HEAD_SIZE = 64
E = 32
TOPK = 8
CAP = 40
MESH = pl.DeviceIdType.MESH
VMEM = pl.BlockSpec(memory_space=pltpu.VMEM)
ANY = pl.BlockSpec(memory_space=pl.ANY)
SMEM = pl.BlockSpec(memory_space=pltpu.SMEM)
BF = jnp.bfloat16
F32 = jnp.float32
FRONT_DEAL = (0.36, 0.8)
BACK_DEAL = (0.36, 0.5, 0.7)

eps = 1e-06
rope_base = 10000.0


def nn(a, b, **kw):
    return lax.dot_general(a, b, (((1,), (0,)), ((), ())), preferred_element_type=F32, **kw)


def nt(a, b, **kw):
    return lax.dot_general(a, b, (((1,), (1,)), ((), ())), preferred_element_type=F32, **kw)


def tn(a, b, **kw):
    return lax.dot_general(a, b, (((0,), (0,)), ((), ())), preferred_element_type=F32, **kw)


def remote(src, dst, send, recv, device):
    return pltpu.make_async_remote_copy(
        src_ref=src,
        dst_ref=dst,
        send_sem=send,
        recv_sem=recv,
        device_id=device,
        device_id_type=MESH,
    )


def start_pieces(copy, src, dst, count, *rest):
    rows = src.shape[0] // count
    for i in range(count):
        part = pl.ds(i * rows, rows)
        copy(src.at[part], dst.at[part], *rest).start()


class Copy:
    def __init__(self, src, dst, count, *rest):
        self.src, self.dst, self.count, self.rest = src, dst, count, rest

    def start(self):
        start_pieces(remote, self.src, self.dst, self.count, *self.rest)

    def wait_send(self):
        remote(self.src, self.dst, *self.rest).wait_send()

    def wait_recv(self):
        remote(self.src, self.dst, *self.rest).wait_recv()


def piece_count(shape, size):
    count = max(1, shape[0] * shape[1] * 2 // size)
    while shape[0] % (16 * count):
        count -= 1
    return count


class Place:
    def __init__(self, nb, nh):
        self.nb, self.nh, self.nz = nb, nh, nb // 2
        self.b, self.h = lax.axis_index("blk"), lax.axis_index("head")
        self.z, self.core = self.b // 2, lax.rem(self.b, 2)
        self.sibling = 2 * self.z + 1 - self.core

    def in_blk(self, b):
        return (b, self.h)

    def in_head(self, h):
        return (self.b, h)

    def head_peer(self, k):
        return lax.rem(self.h + k, self.nh)

    def blk_peer(self, k):
        return lax.rem(self.b + k, self.nb)

    def meet(self):
        barrier = pltpu.get_barrier_semaphore()
        for k in range(1, self.nh):
            pl.semaphore_signal(
                barrier, inc=1, device_id=self.in_head(self.head_peer(k)), device_id_type=MESH
            )
        for k in range(1, self.nb):
            pl.semaphore_signal(
                barrier, inc=1, device_id=self.in_blk(self.blk_peer(k)), device_id_type=MESH
            )
        pl.semaphore_wait(barrier, self.nh + self.nb - 2)


class Relay:
    def __init__(self, at, buf, send, recv, count=1):
        self.at, self.buf, self.send, self.recv, self.count = at, buf, send, recv, count

    def copy(self, s, way, device):
        return Copy(
            self.buf.at[s], self.buf.at[s], self.count, self.send.at[way, s], self.recv.at[s], device
        )

    def right(self, s):
        return self.copy(s, 0, self.at.in_blk(jnp.minimum(self.at.b + 2, self.at.nb - 2 + self.at.core)))

    def left(self, s):
        return self.copy(s, 1, self.at.in_blk(jnp.maximum(self.at.b - 2, self.at.core)))

    def across(self, s):
        return self.copy(s, 2, self.at.in_blk(self.at.sibling))

    def begin(self):
        at = self.at
        pl.when(at.z + 1 < at.nz)(lambda: self.right(at.b).start())
        pl.when(at.z > 0)(lambda: self.left(at.b).start())
        self.across(at.b).start()

    def hop(self, i):
        at = self.at

        @pl.when(at.z >= i)
        def _():
            s = at.b - 2 * i
            self.across(s).wait_recv()
            pl.when(at.z + 1 < at.nz)(lambda: self.right(s).start())
            self.across(s).start()

        @pl.when(at.z + i < at.nz)
        def _():
            s = at.b + 2 * i
            self.across(s).wait_recv()
            pl.when(at.z > 0)(lambda: self.left(s).start())
            self.across(s).start()

    def take_sibling(self, z):
        self.across(2 * z + 1 - self.at.core).wait_recv()

    def finish(self):
        at = self.at
        for i in range(at.nz):

            @pl.when(at.z >= i)
            def _():
                s = at.b - 2 * i
                pl.when(at.z + 1 < at.nz)(lambda: self.right(s).wait_send())
                self.across(s).wait_send()

            if i == 0:
                pl.when(at.z > 0)(lambda: self.left(at.b).wait_send())
            else:

                @pl.when(at.z + i < at.nz)
                def _():
                    s = at.b + 2 * i
                    pl.when(at.z > 0)(lambda: self.left(s).wait_send())
                    self.across(s).wait_send()

    def all(self):
        self.begin()
        for i in range(1, self.at.nz):
            self.hop(i)
        for z in range(self.at.nz):
            self.take_sibling(z)


class Deal:
    def __init__(self, at, chunk, arrived, sems, local_sems):
        self.at, self.chunk, self.arrived = at, chunk, arrived
        self.sems, self.local_sems = sems, local_sems

    def ends(self, j, k):
        at = self.at
        p = at.blk_peer(k)
        return (
            self.chunk(j, p),
            self.arrived[j].at[at.b],
            self.sems.at[0, j, k],
            self.sems.at[1, j, k],
            at.in_blk(p),
        )

    def own(self, j):
        at = self.at
        return pltpu.make_async_copy(
            self.chunk(j, at.b), self.arrived[j].at[at.b], self.local_sems.at[j]
        )

    def start(self, first, last):
        nb = self.at.nb
        if first == 0:
            for j in range(3):
                self.own(j).start()
        rest = [(0, k) for k in range(nb // 2 + 1, nb)]
        rest += [(j, k) for k in range(1, nb) for j in (1, 2)]
        for j, k in rest[int(len(rest) * first) : int(len(rest) * last)]:
            remote(*self.ends(j, k)).start()

    def one(self, z):
        remote(*self.ends(0, 1 + z)).start()

    def end(self):
        for j in range(3):
            for k in range(1, self.at.nb):
                move = remote(*self.ends(j, k))
                move.wait_recv()
                move.wait_send()
            self.own(j).wait()


def sorted_place(at, half, shape, axis):
    s = lax.broadcasted_iota(jnp.int32, shape, axis)
    return jnp.where(
        s < half, at.b * half + s, (2 * at.nb - 1 - at.b) * half + s - half
    )


def begin_of(place, lengths):
    start, begin = 0, jnp.zeros_like(place)
    for i in range(lengths.shape[0] - 1):
        start = start + lengths[i]
        begin = begin + jnp.where(place >= start, lengths[i], 0)
    return begin


def rotation(place, begin):
    shape = (HEAD_SIZE // 2, place.shape[1])
    index = lax.broadcasted_iota(jnp.int32, shape, 0).astype(F32)
    freq = jnp.exp(index * (-2.0 * math.log(rope_base) / HEAD_SIZE))
    angle = freq * (place - begin).astype(F32)
    return jnp.cos(angle), jnp.sin(angle)


def column_of(row):
    wide = jnp.broadcast_to(row.astype(F32), (128, row.shape[1]))
    return wide.T[:, :1].astype(jnp.int32)


def block_base(at, b, second, half):
    return jnp.where(second == 0, b * half, (2 * at.nb - 1 - b) * half)


def turn_rows(values, cos, sin):
    half = HEAD_SIZE // 2
    pieces = []
    for first in range(0, values.shape[0], HEAD_SIZE):
        lead = values[first : first + half]
        trail = values[first + half : first + HEAD_SIZE]
        pieces.append(lead * cos - trail * sin)
        pieces.append(trail * cos + lead * sin)
    return jnp.concatenate(pieces, axis=0)


def pick_targets(slots, pair_rows):
    lane = lax.broadcasted_iota(jnp.int32, slots.shape, 1)
    kept = (slots >= 0) & (slots < CAP)
    return jnp.where(kept, slots + jnp.where(lane >= pair_rows // 2, CAP, 0), -1)


def hits(target_row, pair_rows):
    return lax.broadcasted_iota(jnp.int32, (2 * CAP, pair_rows), 0) == target_row


def diagonal():
    shape = (2 * CAP, 2 * CAP)
    return lax.broadcasted_iota(jnp.int32, shape, 0) == lax.broadcasted_iota(jnp.int32, shape, 1)


def to_row(column):
    return jnp.sum(jnp.where(diagonal(), column, 0.0), axis=0, keepdims=True)


def to_column(row):
    return jnp.sum(jnp.where(diagonal(), row, 0.0), axis=1, keepdims=True)


def split_product(dot, left, right):
    high = left.astype(BF)
    low = (left - high.astype(F32)).astype(BF)
    return dot(high, right) + dot(low, right)


def front_kernel(
    nb,
    nh,
    hl,
    kl,
    repeat,
    inputs,
    w_norm1,
    w_norm2,
    w_own,
    places,
    lengths,
    grad_out,
    table,
    router_t,
    w_gate,
    w_up,
    w_down,
    xg,
    wg,
    qt,
    kv,
    lse,
    attn_t,
    ao_t,
    middle,
    n2,
    slots,
    own_gates,
    in_gate,
    in_rows,
    in_g,
    gate_in,
    up_in,
    down_in,
    ao,
    perm,
    top,
    total,
    out_send,
    out_recv,
    x_sems,
    w_send,
    w_recv,
    kv_send,
    kv_recv,
    o_sems,
    slot_all,
    g_all,
    n2_all,
    gates,
    out_rows,
    out_g,
    out_gate,
    s_send,
    s_recv,
    g_send,
    g_recv,
    n_send,
    n_recv,
    row_sems,
    g_sems,
    gate_sems,
    local_sems,
    deal_sems,
    deal_local,
    begin,
):
    at = Place(nb, nh)
    rows = inputs.shape[0]
    group = rows * nh
    half = group // 2
    qw, kw = hl * HEAD_SIZE, kl * HEAD_SIZE
    width = qw + 2 * kw

    hidden = inputs[...].astype(F32)
    unit = hidden * lax.rsqrt(jnp.mean(hidden * hidden, axis=-1, keepdims=True) + eps)
    xg[at.h] = (unit * w_norm1[...]).astype(BF)
    wg[at.b] = w_own[...]
    slot_all[at.b] = table[...]
    g_all[at.b] = grad_out[...]
    at.meet()
    x_copies = [
        remote(xg.at[at.h], xg.at[at.h], x_sems.at[0, k], x_sems.at[1, k], at.in_head(at.head_peer(k)))
        for k in range(1, nh)
    ]
    for c in x_copies:
        c.start()
    weights = Relay(at, wg, w_send, w_recv)
    weights.begin()
    slot_relay = Relay(at, slot_all, s_send, s_recv)
    slot_relay.begin()
    g_relay = Relay(at, g_all, g_send, g_recv, 4)
    g_relay.begin()
    pair = 2 * rows
    own_expert = (at.b // repeat) * nh

    def chunk(j, p):
        w_j = (w_gate, w_up, w_down)[j]
        if repeat == 1:
            return w_j.at[p]
        fr = w_gate.shape[2] // repeat
        part = pl.ds(pl.multiple_of(lax.rem(p, repeat) * fr, fr), fr)
        return w_j.at[p // repeat, part] if j == 2 else w_j.at[p // repeat, :, part]

    deal = Deal(at, chunk, (gate_in, up_in, down_in), deal_sems, deal_local)

    def go(buf_out, buf_in, sems, z, k, count=1):
        peer = at.head_peer(k)
        return Copy(
            buf_out.at[z, peer],
            buf_in.at[z, at.h],
            count,
            sems.at[0, z, k],
            sems.at[1, z, k],
            at.in_head(peer),
        )

    def keep(buf_out, buf_in, j, z):
        return pltpu.make_async_copy(buf_out.at[z, at.h], buf_in.at[z, at.h], local_sems.at[j, z])

    def outward(relay, body, first, last, hopped=0):
        def step(t, unused):
            d, side = t // 2, lax.rem(t, 2)
            z = jnp.where(side == 0, at.z - d, at.z + d)
            pl.when((side == 0) & (d > hopped))(lambda: relay.hop(d))

            @pl.when((z >= 0) & (z < at.nz) & ((d > 0) | (side == 0)))
            def _():
                relay.take_sibling(z)
                body(z)

            return 0

        lax.fori_loop(2 * first, 2 * last, step, 0)

    def send_g(z):
        x = g_all[pl.ds(2 * z, 2)].reshape(pair, MODEL_WIDTH)
        for k in list(range(1, nh)) + [0]:
            peer = at.head_peer(k)
            hit = hits(pick_targets(slots[z, pl.ds(own_expert + peer, 1)], pair), pair)
            out_g[z, peer] = nn(jnp.where(hit, 1.0, 0.0).astype(BF), x).astype(BF)
            if k == 0:
                keep(out_g, in_g, 0, z).start()
            else:
                go(out_g, in_g, g_sems, z, k, 5).start()

    def send_rows(z):
        x = n2_all[pl.ds(2 * z, 2)].reshape(pair, MODEL_WIDTH)
        routed = slots[z] >= 0
        logits = jnp.where(routed, nt(router_t[...], x), -1e30)
        shifted = jnp.exp(logits - jnp.max(logits, axis=0, keepdims=True))
        shifted = jnp.where(routed, shifted, 0.0)
        gates[z] = shifted / jnp.sum(shifted, axis=0, keepdims=True)
        for k in list(range(1, nh)) + [0]:
            peer = at.head_peer(k)
            hit = hits(pick_targets(slots[z, pl.ds(own_expert + peer, 1)], pair), pair)
            gate_row = gates[z, pl.ds(own_expert + peer, 1)]
            gate = to_row(jnp.sum(jnp.where(hit, gate_row, 0.0), axis=1, keepdims=True))
            out_rows[z, peer] = nn(jnp.where(hit, 1.0, 0.0).astype(BF), x).astype(BF)
            if k == 0:
                keep(out_rows, in_rows, 1, z).start()
                in_gate[z, at.h] = gate
            else:
                go(out_rows, in_rows, row_sems, z, k).start()
                out_gate[z, peer] = gate
                go(out_gate, in_gate, gate_sems, z, k).start()

    place_row = places[at.b]
    cos, sin = rotation(place_row, begin_of(place_row, lengths))
    in_order = begin_of(sorted_place(at, half, (1, group), 1), lengths)
    begin[0] = in_order[:, :half]
    begin[1] = in_order[:, half:]
    place_col = column_of(place_row)
    perm[...] = jnp.where(
        place_row == sorted_place(at, half, (group, group), 0), 1.0, 0.0
    ).astype(BF)
    for i in range(1, nb // 2):
        slot_relay.hop(i)
        weights.hop(i)
    for z in range(nb // 2):
        slot_relay.take_sibling(z)
    for z in range(nb // 2):
        slots[z] = jnp.concatenate([slot_all[2 * z], slot_all[2 * z + 1]], axis=1)
    outward(g_relay, send_g, 0, 1)
    deal.start(0, FRONT_DEAL[0])
    for z in range(nb // 2):
        weights.take_sibling(z)
    for c in x_copies:
        c.wait_recv()
    x = xg[...].reshape(group, MODEL_WIDTH)
    w = wg[...].reshape(MODEL_WIDTH, width + qw)
    qkv_t = nn(x, w[:, :width]).T
    qkv_t = jnp.concatenate(
        [turn_rows(qkv_t[: qw + kw], cos, sin), qkv_t[qw + kw :]], axis=0
    ).astype(BF)
    order = perm[...]
    kv_rows = nt(order, qkv_t[qw:]).astype(BF)
    kv[at.b, 0] = kv_rows[:half]
    kv[at.b, 1] = kv_rows[half:]

    def kv_copy(p, second, way, device):
        return remote(
            kv.at[p, second], kv.at[p, second], kv_send.at[way, p], kv_recv.at[p], device
        )

    right = at.in_blk(jnp.minimum(at.b + 2, nb - 2 + at.core))
    left = at.in_blk(jnp.maximum(at.b - 2, at.core))
    across = at.in_blk(at.sibling)
    pl.when(at.z + 1 < at.nz)(lambda: kv_copy(at.b, 0, 0, right).start())
    pl.when(at.z > 0)(lambda: kv_copy(at.b, 1, 0, left).start())
    kv_copy(at.b, at.core, 1, across).start()
    q_cols = (nt(qkv_t[:qw], order) * (1.0 / math.sqrt(HEAD_SIZE))).astype(BF)
    qt[0] = q_cols[:, :half]
    qt[1] = q_cols[:, half:]
    outward(g_relay, send_g, 1, 2)
    top[...] = jnp.full(top.shape, -1e30, F32)
    total[...] = jnp.zeros(total.shape, F32)
    attn_t[...] = jnp.zeros(attn_t.shape, F32)

    def attend(p, second):
        old_top, old_total = top[second], total[second]
        tops, totals = [], []
        block = kv[p, second]
        key_place = block_base(at, p, second, half) + lax.broadcasted_iota(
            jnp.int32, (half, half), 0
        )
        own_place = block_base(at, at.b, second, half) + lax.broadcasted_iota(
            jnp.int32, (half, half), 1
        )
        allowed = (key_place <= own_place) & (key_place >= begin[second])
        for a in range(hl):
            g = a // (hl // kl)
            rows_a = slice(a * HEAD_SIZE, (a + 1) * HEAD_SIZE)
            scores = nn(block[:, g * HEAD_SIZE : (g + 1) * HEAD_SIZE], qt[second, rows_a])
            scores = jnp.where(allowed, scores, -1e30)
            old = old_top[a : a + 1]
            new = jnp.maximum(old, jnp.max(scores, axis=0, keepdims=True))
            probs = jnp.exp(scores - new)
            fade = jnp.exp(old - new)
            totals.append(old_total[a : a + 1] * fade + jnp.sum(probs, axis=0, keepdims=True))
            tops.append(new)
            attn_t[second, rows_a] = attn_t[second, rows_a] * fade + tn(
                block[:, kw + g * HEAD_SIZE : kw + (g + 1) * HEAD_SIZE], probs.astype(BF)
            )
        top[second, :hl] = jnp.concatenate(tops, axis=0)
        total[second, :hl] = jnp.concatenate(totals, axis=0)

    def visit(step, unused):
        i = step // 4
        second = lax.rem(step, 2)
        same = lax.rem(step // 2, 2) == 0
        z = jnp.where(second == 0, at.z - i, at.z + i)
        p = 2 * z + jnp.where(same, at.core, 1 - at.core)
        exists = (z >= 0) & (z < nb // 2) & ((i > 0) | same | (at.core != second))

        @pl.when(exists)
        def _():
            @pl.when(p != at.b)
            def _():
                kv_copy(p, second, 1, across).wait_recv()

            @pl.when((i > 0) & same)
            def _():
                @pl.when((second == 0) & (at.z + 1 < at.nz))
                def _():
                    kv_copy(p, second, 0, right).start()

                @pl.when((second == 1) & (at.z > 0))
                def _():
                    kv_copy(p, second, 0, left).start()

                kv_copy(p, second, 1, across).start()

            attend(p, second)

        return 0

    lax.fori_loop(0, 4 * (nb // 2), visit, 0)
    for i in range(2, min(3, at.nz)):
        g_relay.hop(i)
    deal.start(FRONT_DEAL[0], FRONT_DEAL[1])
    for second in range(2):
        sums = total[second]
        for a in range(hl):
            rows_a = slice(a * HEAD_SIZE, (a + 1) * HEAD_SIZE)
            attn_t[second, rows_a] = attn_t[second, rows_a] / sums[a : a + 1]
    lse[...] = top[...] + jnp.log(total[...])
    back = jnp.where(place_col == sorted_place(at, half, (group, group), 1), 1.0, 0.0).astype(BF)
    attn_rows = (
        nt(back[:, :half], attn_t[0].astype(BF)) + nt(back[:, half:], attn_t[1].astype(BF))
    ).astype(BF)
    ao[...] = attn_rows
    ao_t[...] = (
        nn(attn_t[0].astype(BF), perm[:half]) + nn(attn_t[1].astype(BF), perm[half:])
    ).astype(BF)
    o_copies = []
    for k in range(nh):
        peer = at.head_peer(k)
        chunk = nt(ao[pl.ds(peer * rows, rows)], w[:, width:])
        if k == 0:
            middle[...] = hidden + chunk
            continue
        out_send[peer] = chunk.astype(BF)
        c = remote(
            out_send.at[peer], out_recv.at[at.h], o_sems.at[0, k], o_sems.at[1, k], at.in_head(peer)
        )
        c.start()
        o_copies.append(c)
    outward(g_relay, send_g, 2, at.nz, 2)
    for k in range(1, nh):
        o_copies[k - 1].wait_recv()
        middle[...] += out_recv[lax.rem(at.h + nh - k, nh)].astype(F32)
    mid = middle[...]
    n2[...] = (
        mid * lax.rsqrt(jnp.mean(mid * mid, axis=-1, keepdims=True) + eps) * w_norm2[...]
    ).astype(BF)
    n2_all[at.b] = n2[...]
    n_relay = Relay(at, n2_all, n_send, n_recv)
    n_relay.begin()

    def send_both(z):
        send_rows(z)
        deal.one(z)

    outward(n_relay, send_both, 0, at.nz)
    deal.start(FRONT_DEAL[1], 1)
    own_gates[...] = jnp.where(at.core == 0, gates[at.z, :, :rows], gates[at.z, :, rows:])
    for relay in (weights, slot_relay, g_relay, n_relay):
        relay.finish()
    for c in x_copies + o_copies:
        c.wait_send()

    def drain(step, unused):
        i = step // 2
        second = lax.rem(step, 2)
        z = jnp.where(second == 0, at.z - i, at.z + i)
        p = 2 * z + at.core

        @pl.when((z >= 0) & (z < nb // 2))
        def _():
            @pl.when((second == 0) & (at.z + 1 < at.nz))
            def _():
                kv_copy(p, second, 0, right).wait_send()

            @pl.when((second == 1) & (at.z > 0))
            def _():
                kv_copy(p, second, 0, left).wait_send()

            @pl.when((i > 0) | (second == at.core))
            def _():
                kv_copy(p, second, 1, across).wait_send()

        return 0

    lax.fori_loop(0, nb, drain, 0)

    def end(z, unused):
        for k in range(1, nh):
            for move in (
                go(out_g, in_g, g_sems, z, k),
                go(out_rows, in_rows, row_sems, z, k),
                go(out_gate, in_gate, gate_sems, z, k),
            ):
                move.wait_recv()
                move.wait_send()
        keep(out_g, in_g, 0, z).wait()
        keep(out_rows, in_rows, 1, z).wait()
        return 0

    lax.fori_loop(0, at.nz, end, 0)
    deal.end()


def front(nb, nh, hl, kl, repeat, *operands):
    inputs, w_own = operands[0], operands[3]
    hidden_units = operands[9].shape[2]
    fr = hidden_units // repeat
    rows = inputs.shape[0]
    group, half = rows * nh, rows * nh // 2
    nz = nb // 2
    dl, wide = w_own.shape
    qw, kw = hl * HEAD_SIZE, kl * HEAD_SIZE
    shape = jax.ShapeDtypeStruct
    dma = pltpu.SemaphoreType.DMA
    chunk = (nz, nh, 2 * CAP, MODEL_WIDTH)
    line = (nz, nh, 1, 2 * CAP)
    relay_sems = [dma((3, nb)), dma((nb,))]
    return pl.pallas_call(
        functools.partial(front_kernel, nb, nh, hl, kl, repeat),
        out_shape=(
            shape((nh, rows, MODEL_WIDTH), BF),
            shape((nb, dl, wide), BF),
            shape((2, qw, half), BF),
            shape((nb, 2, half, 2 * kw), BF),
            shape((2, max(hl, 8), half), F32),
            shape((2, qw, half), F32),
            shape((qw, group), BF),
            shape((rows, MODEL_WIDTH), F32),
            shape((rows, MODEL_WIDTH), BF),
            shape((nz, E, 2 * rows), jnp.int32),
            shape((E, rows), F32),
            shape(line, F32),
            shape(chunk, BF),
            shape(chunk, BF),
            shape((nb, dl, fr), BF),
            shape((nb, dl, fr), BF),
            shape((nb, fr, dl), BF),
        ),
        in_specs=[VMEM] * 5 + [SMEM] + [VMEM] * 3 + [ANY] * 3,
        out_specs=[VMEM] * 12 + [ANY] * 5,
        scratch_shapes=[
            pltpu.VMEM((group, qw), BF),
            pltpu.VMEM((group, group), BF),
            pltpu.VMEM((2, max(hl, 8), half), F32),
            pltpu.VMEM((2, max(hl, 8), half), F32),
            pltpu.VMEM((nh, rows, MODEL_WIDTH), BF),
            pltpu.VMEM((nh, rows, MODEL_WIDTH), BF),
            dma((2, nh)),
            dma((3, nb)),
            dma((nb,)),
            dma((2, nb)),
            dma((nb,)),
            dma((2, nh)),
            pltpu.VMEM((nb, E, rows), jnp.int32),
            pltpu.VMEM((nb, rows, MODEL_WIDTH), BF),
            pltpu.VMEM((nb, rows, MODEL_WIDTH), BF),
            pltpu.VMEM((nz, E, 2 * rows), F32),
            pltpu.VMEM(chunk, BF),
            pltpu.VMEM(chunk, BF),
            pltpu.VMEM(line, F32),
            *relay_sems,
            *relay_sems,
            *relay_sems,
            dma((2, nz, nh)),
            dma((2, nz, nh)),
            dma((2, nz, nh)),
            dma((2, nz)),
            dma((2, 3, nb)),
            dma((3,)),
            pltpu.VMEM((2, 1, half), jnp.int32),
        ],
        compiler_params=pltpu.CompilerParams(collective_id=1, vmem_limit_bytes=60 * 2**20),
        name="front",
    )(*operands)


def slot_table(nb, nh, repeat, routes, slot_order):
    local = E // nh
    mine = (routes % local) * nh + routes // local
    match = mine.T[:, None, :] == jnp.arange(E, dtype=jnp.int32)[None, :, None]
    order = jnp.min(jnp.where(match, slot_order.T[:, None, :], 1 << 20), axis=0)
    before = jnp.sum((order[:, :, None] < order[:, None, :]).astype(jnp.int32), axis=1)
    return jnp.where(order < (1 << 20), before, -1)


def experts_kernel(
    nz,
    nh,
    x_ref,
    g_ref,
    gate_ref,
    w_gate_ref,
    w_up_ref,
    w_down_ref,
    d_rows,
    scaled,
    d_gate_row,
    grad_gate,
    grad_up,
    grad_down,
    w_down,
    sum_gate,
    sum_up,
    sum_down,
):
    step = pl.program_id(0)
    nb, dl, fr = w_gate_ref.shape

    @pl.when(step == 0)
    def _():
        w_down[...] = jnp.concatenate([w_down_ref[p] for p in range(nb)], axis=1)
        for total in (sum_gate, sum_up, sum_down):
            total[...] = jnp.zeros(total.shape, F32)

    x = x_ref[0].reshape(nh * 2 * CAP, MODEL_WIDTH)
    gate = jnp.concatenate([to_column(gate_ref[0, h]) for h in range(nh)], axis=0)
    w_gate = w_gate_ref[...].reshape(MODEL_WIDTH, fr)
    w_up = w_up_ref[...].reshape(MODEL_WIDTH, fr)
    gate_pre, up_pre = nn(x, w_gate), nn(x, w_up)
    sigma = 1.0 / (1.0 + jnp.exp(-gate_pre))
    swish = gate_pre * sigma
    activated = (swish * up_pre).astype(BF)
    out = nn(activated, w_down[...]).astype(BF).astype(F32)
    g = g_ref[0].reshape(nh * 2 * CAP, MODEL_WIDTH).astype(F32)
    d_gate = jnp.sum(out * g, axis=1, keepdims=True)
    d_out = (gate * g).astype(BF)
    scaled[0] = (gate * out).astype(BF).reshape(nh, 2 * CAP, MODEL_WIDTH)
    d_act = nt(d_out, w_down[...])
    d_gate_pre = (d_act * up_pre * sigma * (1.0 + gate_pre * (1.0 - sigma))).astype(BF)
    d_up_pre = (d_act * swish).astype(BF)
    back_rows = (nt(d_gate_pre, w_gate) + nt(d_up_pre, w_up)).astype(BF)
    d_rows[0] = back_rows.reshape(nh, 2 * CAP, MODEL_WIDTH)
    for h in range(nh):
        d_gate_row[0, h] = to_row(d_gate[h * 2 * CAP : (h + 1) * 2 * CAP])
    sum_gate[...] += tn(x, d_gate_pre)
    sum_up[...] += tn(x, d_up_pre)
    sum_down[...] += tn(activated, d_out)

    @pl.when(step == nz - 1)
    def _():
        for p in range(nb):
            own = slice(p * dl, (p + 1) * dl)
            grad_gate[p] = sum_gate[own].astype(BF)
            grad_up[p] = sum_up[own].astype(BF)
            grad_down[p] = sum_down[:, own].astype(BF)


def experts(nz, nh, x, g, gate, w_gate, w_up, w_down):
    nb, dl, fr = w_gate.shape
    shape = jax.ShapeDtypeStruct
    wide = pl.BlockSpec((1,) + x.shape[1:], lambda i: (i, 0, 0, 0))
    line = pl.BlockSpec((1,) + gate.shape[1:], lambda i: (i, 0, 0, 0))
    deep = pl.BlockSpec(w_gate.shape, lambda i: (0, 0, 0))
    flat = pl.BlockSpec(w_down.shape, lambda i: (0, 0, 0))
    return pl.pallas_call(
        functools.partial(experts_kernel, nz, nh),
        grid=(nz,),
        out_shape=(
            shape(x.shape, BF),
            shape(x.shape, BF),
            shape(gate.shape, F32),
            shape(w_gate.shape, BF),
            shape(w_up.shape, BF),
            shape(w_down.shape, BF),
        ),
        in_specs=[wide, wide, line, deep, deep, flat],
        out_specs=[wide, wide, line, deep, deep, flat],
        scratch_shapes=[
            pltpu.VMEM((fr, MODEL_WIDTH), BF),
            pltpu.VMEM((MODEL_WIDTH, fr), F32),
            pltpu.VMEM((MODEL_WIDTH, fr), F32),
            pltpu.VMEM((fr, MODEL_WIDTH), F32),
        ],
        compiler_params=pltpu.CompilerParams(vmem_limit_bytes=60 * 2**20),
        name="experts",
    )(x, g, gate, w_gate, w_up, w_down)


class Scatter:
    def __init__(self, at, bufs, sems):
        self.at, self.sems = at, sems
        self.sib_out, self.sib_in, self.z_out, self.z_in = (bufs.at[j] for j in range(4))

    def across(self, z):
        return remote(
            self.sib_out.at[z],
            self.sib_in.at[z],
            self.sems.at[0, z],
            self.sems.at[1, z],
            self.at.in_blk(self.at.sibling),
        )

    def along(self, z):
        at = self.at
        slot = jnp.where(z == at.z - 1, at.nz, z)
        ahead = jnp.clip(jnp.where(z > at.z, at.z + 1, at.z - 1), 0, at.nz - 1)
        return remote(
            self.z_out.at[z],
            self.z_in.at[slot],
            self.sems.at[2, z],
            self.sems.at[3, slot],
            at.in_blk(2 * ahead + at.core),
        )

    def arrived(self, slot):
        at = self.at
        remote(
            self.z_out.at[0],
            self.z_in.at[slot],
            self.sems.at[2, 0],
            self.sems.at[3, slot],
            at.in_blk(at.sibling),
        ).wait_recv()
        return self.z_in[slot].astype(F32)

    def give_sibling(self, z, value):
        self.sib_out[z] = value.astype(BF)
        self.across(z).start()

    def from_sibling(self, z):
        self.across(z).wait_recv()
        return self.sib_in[z].astype(F32)

    def give(self, z, value):
        at = self.at
        joins = ((z > at.z) & (at.z > 0)) | ((z < at.z) & (at.z < at.nz - 1))

        @pl.when(joins)
        def _():
            self.z_out[z] = (value + self.arrived(z)).astype(BF)

        @pl.when(jnp.logical_not(joins))
        def _():
            self.z_out[z] = value.astype(BF)

        self.along(z).start()

    def take(self, add):
        at = self.at
        pl.when(at.z > 0)(lambda: add(self.arrived(at.z), True))
        pl.when(at.z < at.nz - 1)(lambda: add(self.arrived(at.nz), False))

    def finish(self):
        at = self.at
        for z in range(at.nz):
            self.across(z).wait_send()
            pl.when(at.z != z)(lambda: self.along(z).wait_send())


class Total:
    def __init__(self, at, part, by_head, by_blk, whole, sems):
        self.at, self.part, self.by_head, self.by_blk, self.whole = at, part, by_head, by_blk, whole
        self.sems = sems

    def copy(self, stage, k):
        at = self.at
        peer = at.blk_peer(k) if stage == 1 else at.head_peer(k)
        device = at.in_blk(peer) if stage == 1 else at.in_head(peer)
        if stage == 0:
            src, dst = self.part.at[peer], self.by_head.at[at.h]
        elif stage == 1:
            src, dst = self.by_blk.at[at.b], self.by_blk.at[at.b]
        else:
            src, dst = self.whole.at[at.h], self.whole.at[at.h]
        return remote(src, dst, self.sems.at[0, stage, k], self.sems.at[1, stage, k], device)

    def peers(self, stage):
        return range(1, self.at.nb if stage == 1 else self.at.nh)

    def begin(self, stage):
        at = self.at
        if stage == 0:
            self.by_head[at.h] = self.part[at.h]
        elif stage == 1:
            self.by_blk[at.b] = sum_slots(self.by_head, at.nh)
        else:
            self.whole[at.h] = sum_slots(self.by_blk, at.nb)
        for k in self.peers(stage):
            self.copy(stage, k).start()

    def end(self, stage):
        for k in self.peers(stage):
            self.copy(stage, k).wait_recv()

    def finish(self):
        for stage in range(3):
            for k in self.peers(stage):
                self.copy(stage, k).wait_send()


def sum_slots(ref, n):
    total = ref[0]
    for s in range(1, n):
        total = total + ref[s]
    return total


def back_kernel(
    nb,
    nh,
    hl,
    kl,
    repeat,
    inputs,
    w_norm1,
    w_norm2,
    middle,
    n2,
    grad_out,
    router_t,
    slots,
    own_gates,
    d_gate_rows,
    wg,
    xg,
    ao_t,
    qt,
    kv,
    lse,
    attn_t,
    places,
    lengths,
    d_rows,
    scaled,
    gate_sum,
    up_sum,
    down_sum,
    output,
    grad_in,
    grad_q,
    grad_k,
    grad_v,
    grad_o,
    grad_n1,
    small_sum,
    gate_in,
    up_in,
    down_in,
    dbg,
    perm,
    d_rows_ref,
    do_t,
    delta,
    dq_t,
    own_kv,
    kv_bufs,
    w_part,
    w_bufs,
    out_send,
    out_recv,
    n1_head,
    n1_blk,
    s_head,
    s_blk,
    d_sems,
    kv_sems,
    w_sems,
    o_sems,
    n_sems,
    s_sems,
    small,
    back_rows,
    in_dgate,
    own_part,
    d_middle,
    dg_out,
    dg_in,
    sc_bufs,
    sc_sems,
    mix_sems,
    ret_sems,
    eout_sems,
    dgate_sems,
    dg_sems,
    local_sems,
    deal_sems,
    deal_local,
    begin,
    grad_w,
    *loaded,
):
    at = Place(nb, nh)
    nz = at.nz
    rows = inputs.shape[0]
    group = rows * nh
    half = group // 2
    qw, kw = hl * HEAD_SIZE, kl * HEAD_SIZE
    width = qw + 2 * kw
    dl = MODEL_WIDTH // nb
    scale = 1.0 / math.sqrt(HEAD_SIZE)

    pair = 2 * rows
    own_expert = (at.b // repeat) * nh
    at.meet()

    def go(buf_out, buf_in, sems, z, k, count=1):
        peer = at.head_peer(k)
        return Copy(
            buf_out.at[z, peer],
            buf_in.at[z, at.h],
            count,
            sems.at[0, z, k],
            sems.at[1, z, k],
            at.in_head(peer),
        )

    def keep(buf_out, j, z):
        return pltpu.make_async_copy(buf_out.at[z, at.h], back_rows.at[z, at.h], local_sems.at[j, z])

    def far_first(body):
        def step(t, unused):
            d, side = nz - 1 - t // 2, lax.rem(t, 2)
            z = jnp.where(side == 0, at.z - d, at.z + d)

            @pl.when((z >= 0) & (z < nz) & ((d > 0) | (side == 0)))
            def _():
                body(z)

            return 0

        lax.fori_loop(0, 2 * nz, step, 0)

    def send_back(z):
        for k in range(1, nh):
            go(d_rows, back_rows, ret_sems, z, k).start()
            go(d_gate_rows, in_dgate, dgate_sems, z, k).start()
        keep(d_rows, 0, z).start()
        in_dgate[z, at.h] = d_gate_rows[z, at.h]

    far_first(send_back)
    load_sems = loaded[-1]
    sources = (wg, xg, ao_t, qt, kv, attn_t)
    loads = [
        pltpu.make_async_copy(src, dst, load_sems.at[i])
        for i, (src, dst) in enumerate(zip(sources, loaded[:-1]))
    ]
    for c in loads:
        c.start()
    wg, xg, ao_t, qt, kv, attn_t = loaded[:-1]
    place_row = places[at.b]
    sorted_row = sorted_place(at, half, (1, group), 1)
    in_order = begin_of(sorted_row, lengths)
    begin[0] = in_order[:, :half]
    begin[1] = in_order[:, half:]
    cos, sin = rotation(sorted_row, in_order)
    place_col = column_of(place_row)
    sums_of = (gate_sum, up_sum, down_sum)
    deal = Deal(at, lambda j, p: sums_of[j].at[p], (gate_in, up_in, down_in), deal_sems, deal_local)
    deal.start(0, BACK_DEAL[0])
    n2_scatter = Scatter(at, sc_bufs, sc_sems)

    def dg_copy(p):
        return remote(
            dg_out.at[p], dg_in.at[at.b], dg_sems.at[0, p], dg_sems.at[1, at.b], at.in_blk(p)
        )

    def masks_of(z):
        return [
            hits(pick_targets(slots[z, pl.ds(own_expert + h, 1)], pair), pair) for h in range(nh)
        ]

    def spread(z, masks, scatter):
        hit_rows = jnp.concatenate([jnp.where(m, 1.0, 0.0).astype(BF) for m in masks], axis=0)
        part = tn(hit_rows, back_rows[z].reshape(nh * 2 * CAP, MODEL_WIDTH))
        own_part[0] = part[:rows]
        own_part[1] = part[rows:]
        scatter.give_sibling(z, own_part[1 - at.core])

        @pl.when(z != at.z)
        def _():
            scatter.give(z, own_part[at.core] + scatter.from_sibling(z))

    def gathered_part(scatter):
        own_part[2] = own_part[at.core] + scatter.from_sibling(at.z)

        def add(value, from_left):
            own_part[2] += value

        scatter.take(add)
        return own_part[2]

    def gather_back(z):
        for k in range(1, nh):
            go(d_rows, back_rows, ret_sems, z, k).wait_recv()
            go(d_gate_rows, in_dgate, dgate_sems, z, k).wait_recv()
        keep(d_rows, 0, z).wait()
        masks = masks_of(z)
        d_gates = jnp.concatenate(
            [
                jnp.sum(jnp.where(m, to_column(in_dgate[z, h]), 0.0), axis=0, keepdims=True)
                for h, m in enumerate(masks)
            ],
            axis=0,
        )
        dg_out[2 * z] = d_gates[:, :rows]
        dg_out[2 * z + 1] = d_gates[:, rows:]
        pl.when(z == at.z)(lambda: dg_copy(at.sibling).start())

        @pl.when(z != at.z)
        def _():
            dg_copy(2 * z).start()
            dg_copy(2 * z + 1).start()

        spread(z, masks, n2_scatter)
        deal.one(z)

    far_first(gather_back)
    dg_in[at.b] = dg_out[at.b]
    for k in range(1, nb):
        p = at.blk_peer(k)
        remote(dg_out.at[p], dg_in.at[p], dg_sems.at[0, p], dg_sems.at[1, p], at.in_blk(p)).wait_recv()
    d_gates = jnp.concatenate(
        [sum_slots(dg_in.at[pl.ds(i * repeat, repeat)], repeat) for i in range(nb // repeat)], axis=0
    )
    d_logits = own_gates[...] * (
        d_gates - jnp.sum(own_gates[...] * d_gates, axis=0, keepdims=True)
    )
    from_logits = split_product(tn, d_logits, router_t[...])
    g_router = split_product(nn, d_logits, n2[...])
    mid = middle[...]
    factor_two = lax.rsqrt(jnp.mean(mid * mid, axis=-1, keepdims=True) + eps)
    unit_two = mid * factor_two
    d_n2 = gathered_part(n2_scatter) + from_logits
    weighted_two = d_n2 * w_norm2[...]
    d_middle[...] = grad_out[...].astype(F32) + factor_two * (
        weighted_two - unit_two * jnp.mean(unit_two * weighted_two, axis=-1, keepdims=True)
    )
    dbg[at.h] = d_middle[...].astype(BF)
    d_copies = [
        remote(dbg.at[at.h], dbg.at[at.h], d_sems.at[0, k], d_sems.at[1, k], at.in_head(at.head_peer(k)))
        for k in range(1, nh)
    ]
    for c in d_copies:
        c.start()
    g_norm = jnp.sum(d_n2 * unit_two, axis=0, keepdims=True)
    slab = MODEL_WIDTH // nh
    for h in range(nh):
        cols = slice(h * slab, (h + 1) * slab)
        small[h, :E] = g_router[:, cols]
        small[h, E:] = jnp.broadcast_to(g_norm[:, cols], (8, slab))
    totals = Total(at, small, s_head, s_blk, small_sum, s_sems)
    totals.begin(0)
    perm[...] = jnp.where(
        place_row == sorted_place(at, half, (group, group), 0), 1.0, 0.0
    ).astype(BF)
    dq_t[...] = jnp.zeros(dq_t.shape, F32)
    for c in d_copies:
        c.wait_recv()

    def send_scaled(z):
        for k in range(1, nh):
            go(scaled, back_rows, eout_sems, z, k, 5).start()
        keep(scaled, 1, z).start()

    far_first(send_scaled)
    totals.end(0)
    totals.begin(1)
    deal.start(BACK_DEAL[0], BACK_DEAL[1])
    for c in loads:
        c.wait()
    d_branch = dbg[...].reshape(group, MODEL_WIDTH)
    w = wg[...].reshape(MODEL_WIDTH, width + qw)
    d_attn_t = nn(d_branch, w[:, width:]).T.astype(BF)
    d_sorted = nt(d_attn_t, perm[...])
    for second in range(2):
        piece = d_sorted[:, second * half : (second + 1) * half]
        do_t[second] = piece.astype(BF)
        product = piece * attn_t[second]
        delta[second, :hl] = jnp.concatenate(
            [
                jnp.sum(product[a * HEAD_SIZE : (a + 1) * HEAD_SIZE], axis=0, keepdims=True)
                for a in range(hl)
            ],
            axis=0,
        )

    def step_back(p, second):
        block = kv[p, second]
        lse_all, delta_all = lse[second], delta[second]
        key_place = block_base(at, p, second, half) + lax.broadcasted_iota(
            jnp.int32, (half, half), 0
        )
        own_place = block_base(at, at.b, second, half) + lax.broadcasted_iota(
            jnp.int32, (half, half), 1
        )
        allowed = (key_place <= own_place) & (key_place >= begin[second])
        d_keys, d_values = [None] * kl, [None] * kl
        for a in range(hl):
            g = a // (hl // kl)
            rows_a = slice(a * HEAD_SIZE, (a + 1) * HEAD_SIZE)
            key = block[:, g * HEAD_SIZE : (g + 1) * HEAD_SIZE]
            value = block[:, kw + g * HEAD_SIZE : kw + (g + 1) * HEAD_SIZE]
            scores = jnp.where(allowed, nn(key, qt[second, rows_a]), -1e30)
            probs = jnp.exp(scores - lse_all[a : a + 1])
            d_probs = nn(value, do_t[second, rows_a])
            d_scores = (probs * (d_probs - delta_all[a : a + 1])).astype(BF)
            d_key = nt(qt[second, rows_a], d_scores)
            d_value = nt(do_t[second, rows_a], probs.astype(BF))
            d_keys[g] = d_key if d_keys[g] is None else d_keys[g] + d_key
            d_values[g] = d_value if d_values[g] is None else d_values[g] + d_value
            dq_t[second, rows_a] += tn(key, d_scores)
        return jnp.concatenate(d_keys + d_values, axis=0)

    scatter = Scatter(at, kv_bufs, kv_sems)

    def visit(step, unused):
        i = nz - 1 - step // 4
        second = lax.rem(step // 2, 2)
        same = lax.rem(step, 2) == 1
        z = jnp.where(second == 0, at.z - i, at.z + i)
        p = 2 * z + jnp.where(same, at.core, 1 - at.core)
        exists = (z >= 0) & (z < nz) & ((i > 0) | same | (at.core != second))

        @pl.when(exists)
        def _():
            part = step_back(p, second)

            @pl.when(jnp.logical_not(same))
            def _():
                scatter.give_sibling(z, part)

            @pl.when(same & (i > 0))
            def _():
                scatter.give(z, part + scatter.from_sibling(z))

            @pl.when(same & (i == 0))
            def _():
                own_kv[second] = part

        return 0

    lax.fori_loop(0, 4 * nz, visit, 0)
    deal.start(BACK_DEAL[1], BACK_DEAL[2])
    totals.end(1)
    totals.begin(2)
    wide = 256

    def weight_part(first, left):
        for c in range(MODEL_WIDTH // wide):
            source = xg if first == 0 else dbg
            piece = nn(left, source[:, :, c * wide : (c + 1) * wide].reshape(group, wide))
            for j in range(wide // dl):
                w_part[c * (wide // dl) + j, first : first + left.shape[0]] = piece[
                    :, j * dl : (j + 1) * dl
                ]

    weight_part(width, ao_t[...])
    own_kv[at.core] += scatter.from_sibling(at.z)

    def add_kv(value, from_left):
        own_kv[1 if from_left else 0] += value

    scatter.take(add_kv)

    d_sorted_t = []
    for second in range(2):
        cols = slice(second * half, (second + 1) * half)
        both = own_kv[second]
        turned = jnp.concatenate([dq_t[second] * scale, both[:kw]], axis=0)
        turned = turn_rows(turned, cos[:, cols], -sin[:, cols])
        d_sorted_t.append(jnp.concatenate([turned, both[kw:]], axis=0).astype(BF))
    back = jnp.where(place_col == sorted_place(at, half, (group, group), 1), 1.0, 0.0).astype(BF)
    turned_back = (
        nt(back[:, :half], d_sorted_t[0]) + nt(back[:, half:], d_sorted_t[1])
    ).astype(BF)
    d_rows_ref[...] = turned_back.reshape(nh, rows, width)
    d_cols = (nn(d_sorted_t[0], perm[:half]) + nn(d_sorted_t[1], perm[half:])).astype(BF)
    o_copies = []
    for k in range(1, nh):
        peer = at.head_peer(k)
        out_send[peer] = nt(d_rows_ref[peer], w[:, :width]).astype(BF)
        c = remote(
            out_send.at[peer], out_recv.at[at.h], o_sems.at[0, k], o_sems.at[1, k], at.in_head(peer)
        )
        c.start()
        o_copies.append(c)
    own_normed = nt(d_rows_ref[at.h], w[:, :width])
    weight_part(0, d_cols)
    w_scatter = Scatter(at, w_bufs, w_sems)

    def w_pass(z):
        w_scatter.give_sibling(z, w_part[2 * z + 1 - at.core])

    def w_along(z):
        pl.when(z != at.z)(
            lambda: w_scatter.give(z, w_part[2 * z + at.core] + w_scatter.from_sibling(z))
        )

    far_first(w_pass)
    far_first(w_along)
    n2_scatter.finish()
    mix_scatter = Scatter(at, sc_bufs, mix_sems)

    def mix(z):
        for k in range(1, nh):
            go(scaled, back_rows, eout_sems, z, k).wait_recv()
        keep(scaled, 1, z).wait()
        spread(z, masks_of(z), mix_scatter)

    far_first(mix)
    deal.start(BACK_DEAL[2], 1)
    for k in range(1, nh):
        o_copies[k - 1].wait_recv()
        own_normed = own_normed + out_recv[lax.rem(at.h + nh - k, nh)].astype(F32)
    hidden = inputs[...].astype(F32)
    factor = lax.rsqrt(jnp.mean(hidden * hidden, axis=-1, keepdims=True) + eps)
    unit = hidden * factor
    n1_head[at.h] = jnp.sum(own_normed * unit, axis=0, keepdims=True)
    n1_copies = [
        remote(n1_head.at[at.h], n1_head.at[at.h], n_sems.at[0, k], n_sems.at[1, k], at.in_head(at.head_peer(k)))
        for k in range(1, nh)
    ]
    for c in n1_copies:
        c.start()
    weighted = own_normed * w_norm1[...]
    grad_in[...] = d_middle[...] + factor * (
        weighted - unit * jnp.mean(unit * weighted, axis=-1, keepdims=True)
    )
    for c in n1_copies:
        c.wait_recv()
    n1_blk[at.b] = sum_slots(n1_head, nh)
    n1_blk_copies = [
        remote(n1_blk.at[at.b], n1_blk.at[at.b], n_sems.at[0, nh + k], n_sems.at[1, nh + k], at.in_blk(at.blk_peer(k)))
        for k in range(1, nb)
    ]
    for c in n1_blk_copies:
        c.start()
    grad_w[...] = w_part[at.b] + w_scatter.from_sibling(at.z)

    def add_w(value, from_left):
        grad_w[...] += value

    w_scatter.take(add_w)
    grad_q[...] = grad_w[:qw].T
    grad_k[...] = grad_w[qw : qw + kw].T
    grad_v[...] = grad_w[qw + kw : width].T
    grad_o[...] = grad_w[width:]

    for c in n1_blk_copies:
        c.wait_recv()
    grad_n1[...] = sum_slots(n1_blk, nb)
    totals.end(2)
    output[...] = (middle[...] + gathered_part(mix_scatter)).astype(BF)
    totals.finish()
    scatter.finish()
    mix_scatter.finish()

    def drain(z):
        for k in range(1, nh):
            go(d_rows, back_rows, ret_sems, z, k).wait_send()
            go(d_gate_rows, in_dgate, dgate_sems, z, k).wait_send()
            go(scaled, back_rows, eout_sems, z, k).wait_send()

    far_first(drain)
    deal.end()
    for k in range(1, nb):
        dg_copy(at.blk_peer(k)).wait_send()
    w_scatter.finish()
    for c in d_copies + o_copies + n1_copies + n1_blk_copies:
        c.wait_send()


def back(nb, nh, hl, kl, repeat, *operands):
    rows = operands[0].shape[0]
    group, half = rows * nh, rows * nh // 2
    nz, dl = nb // 2, MODEL_WIDTH // nb
    qw, kw = hl * HEAD_SIZE, kl * HEAD_SIZE
    width = qw + 2 * kw
    shape = jax.ShapeDtypeStruct
    dma = pltpu.SemaphoreType.DMA
    chunk = (E + 8, MODEL_WIDTH // nh)
    line = (nz, nh, 1, 2 * CAP)
    return pl.pallas_call(
        functools.partial(back_kernel, nb, nh, hl, kl, repeat),
        out_shape=(
            shape((rows, MODEL_WIDTH), BF),
            shape((rows, MODEL_WIDTH), F32),
            shape((dl, qw), F32),
            shape((dl, kw), F32),
            shape((dl, kw), F32),
            shape((qw, dl), F32),
            shape((1, MODEL_WIDTH), F32),
            shape((nh,) + chunk, F32),
            *(shape(v.shape, BF) for v in operands[-3:]),
        ),
        in_specs=[VMEM] * 10 + [ANY] * 4 + [ANY, VMEM, ANY] + [VMEM, SMEM] + [ANY] * 5,
        out_specs=[VMEM] * 8 + [ANY] * 3,
        scratch_shapes=[
            pltpu.VMEM((nh, rows, MODEL_WIDTH), BF),
            pltpu.VMEM((group, group), BF),
            pltpu.VMEM((nh, rows, width), BF),
            pltpu.VMEM((2, qw, half), BF),
            pltpu.VMEM((2, max(hl, 8), half), F32),
            pltpu.VMEM((2, qw, half), F32),
            pltpu.VMEM((2, 2 * kw, half), F32),
            pltpu.VMEM((4, nz + 1, 2 * kw, half), BF),
            pltpu.VMEM((nb, width + qw, dl), F32),
            pltpu.VMEM((4, nz + 1, width + qw, dl), BF),
            pltpu.VMEM((nh, rows, MODEL_WIDTH), BF),
            pltpu.VMEM((nh, rows, MODEL_WIDTH), BF),
            pltpu.VMEM((nh, 1, MODEL_WIDTH), F32),
            pltpu.VMEM((nb, 1, MODEL_WIDTH), F32),
            pltpu.VMEM((nh,) + chunk, F32),
            pltpu.VMEM((nb,) + chunk, F32),
            dma((2, nh)),
            dma((4, nz + 1)),
            dma((4, nz + 1)),
            dma((2, nh)),
            dma((2, nh + nb)),
            dma((2, 3, max(nh, nb))),
            pltpu.VMEM((nh,) + chunk, F32),
            pltpu.VMEM((nz, nh, 2 * CAP, MODEL_WIDTH), BF),
            pltpu.VMEM(line, F32),
            pltpu.VMEM((3, rows, MODEL_WIDTH), F32),
            pltpu.VMEM((rows, MODEL_WIDTH), F32),
            pltpu.VMEM((nb, nh, rows), F32),
            pltpu.VMEM((nb, nh, rows), F32),
            pltpu.VMEM((4, nz + 1, rows, MODEL_WIDTH), BF),
            dma((4, nz + 1)),
            dma((4, nz + 1)),
            dma((2, nz, nh)),
            dma((2, nz, nh)),
            dma((2, nz, nh)),
            dma((2, nb)),
            dma((2, nz)),
            dma((2, 3, nb)),
            dma((3,)),
            pltpu.VMEM((2, 1, half), jnp.int32),
            pltpu.VMEM((width + qw, dl), F32),
            *(pltpu.VMEM(operands[i].shape, operands[i].dtype) for i in (10, 11, 12, 13, 14, 16)),
            dma((6,)),
        ],
        compiler_params=pltpu.CompilerParams(collective_id=2, vmem_limit_bytes=62 * 2**20),
        name="back",
    )(*operands)


def on_device(
    inputs,
    token_place,
    lengths,
    w_norm1,
    w_query,
    key_weight,
    value_weight,
    w_out,
    w_norm2,
    router,
    routes,
    slot_order,
    w_gate,
    w_up,
    w_down,
    grad_out,
):
    rows = inputs.shape[0]
    nb, nh = lax.axis_size("blk"), lax.axis_size("head")
    nz = nb // 2
    hl = w_query.shape[1] // HEAD_SIZE
    kl = key_weight.shape[1] // HEAD_SIZE
    local, dl, hidden_units = w_gate.shape
    repeat = nb // local
    fr = hidden_units // repeat
    qw, kw = hl * HEAD_SIZE, kl * HEAD_SIZE

    w_own = jnp.concatenate([w_query, key_weight, value_weight, w_out.T], axis=1)
    places = token_place.reshape(nb, 1, rows * nh)
    gain_one, gain_two = w_norm1.reshape(1, -1), w_norm2.reshape(1, -1)
    sizes = (nb, nh, hl, kl, repeat)
    router_t = router.T.reshape(nh, local, MODEL_WIDTH).transpose(1, 0, 2).reshape(E, MODEL_WIDTH)
    (
        gathered,
        weights,
        turned_q,
        kv,
        lse,
        attn_t,
        ao_t,
        middle,
        normed_two,
        slots,
        own_gates,
        in_gate,
        in_rows,
        in_g,
        *projections,
    ) = front(
        *sizes,
        inputs,
        gain_one,
        gain_two,
        w_own,
        places,
        lengths,
        grad_out,
        slot_table(nb, nh, repeat, routes, slot_order),
        router_t,
        w_gate,
        w_up,
        w_down,
    )
    d_rows, scaled, d_gate_rows, *sums = experts(nz, nh, in_rows, in_g, in_gate, *projections)
    output, grad_inputs, grad_q, grad_k, grad_v, grad_o, grad_norm1, small, *sums = back(
        *sizes,
        inputs,
        gain_one,
        gain_two,
        middle,
        normed_two,
        grad_out,
        router_t,
        slots,
        own_gates,
        d_gate_rows,
        weights,
        gathered,
        ao_t,
        turned_q,
        kv,
        lse,
        attn_t,
        places,
        lengths,
        d_rows,
        scaled,
        *sums,
    )

    small = small.transpose(1, 0, 2).reshape(E + 8, MODEL_WIDTH)
    grad_router = (
        small[:E].reshape(local, nh, MODEL_WIDTH).transpose(1, 0, 2).reshape(E, MODEL_WIDTH).T
    )

    def whole_part(v, axis):
        v = v.reshape((local, repeat) + v.shape[1:])
        v = v if repeat == 1 else jnp.moveaxis(v, 1, axis)
        return v.reshape((local, dl, hidden_units) if axis == 2 else (local, hidden_units, dl)).astype(F32)

    return (
        output,
        grad_inputs,
        grad_norm1.reshape(-1),
        grad_q,
        grad_k,
        grad_v,
        grad_o,
        small[E],
        grad_router,
        whole_part(sums[0], 2),
        whole_part(sums[1], 2),
        whole_part(sums[2], 1),
    )


def solution(mesh):
    rows, whole = P(("blk", "head"), None), P()
    pair, out = P("blk", "head"), P("head", "blk")
    first, last = P("head", "blk", None), P("head", None, "blk")
    return jax.shard_map(
        on_device,
        mesh=mesh,
        in_specs=(
            rows,
            whole,
            whole,
            whole,
            pair,
            pair,
            pair,
            out,
            whole,
            whole,
            rows,
            rows,
            first,
            first,
            last,
            rows,
        ),
        out_specs=(
            rows,
            rows,
            whole,
            pair,
            pair,
            pair,
            out,
            whole,
            whole,
            first,
            first,
            last,
        ),
        check_vma=False,
    )
```

```python
import functools
import math

import jax
import jax.numpy as jnp
from jax import lax
from jax.experimental import pallas as pl
from jax.experimental.pallas import tpu as pltpu
from jax.sharding import PartitionSpec as P

MODEL_WIDTH = 1024
HEAD_SIZE = 64
E = 32
TOPK = 8
CAP = 40
MESH = pl.DeviceIdType.MESH
VMEM = pl.BlockSpec(memory_space=pltpu.VMEM)
ANY = pl.BlockSpec(memory_space=pl.ANY)
SMEM = pl.BlockSpec(memory_space=pltpu.SMEM)
BF = jnp.bfloat16
F32 = jnp.float32
FRONT_DEAL = (0.36, 0.8)
BACK_DEAL = (0.36, 0.5, 0.7)

eps = 1e-06
rope_base = 10000.0


def nn(a, b, **kw):
    return lax.dot_general(a, b, (((1,), (0,)), ((), ())), preferred_element_type=F32, **kw)


def nt(a, b, **kw):
    return lax.dot_general(a, b, (((1,), (1,)), ((), ())), preferred_element_type=F32, **kw)


def tn(a, b, **kw):
    return lax.dot_general(a, b, (((0,), (0,)), ((), ())), preferred_element_type=F32, **kw)


def remote(src, dst, send, recv, device):
    return pltpu.make_async_remote_copy(
        src_ref=src,
        dst_ref=dst,
        send_sem=send,
        recv_sem=recv,
        device_id=device,
        device_id_type=MESH,
    )


def start_pieces(copy, src, dst, count, *rest):
    rows = src.shape[0] // count
    for i in range(count):
        part = pl.ds(i * rows, rows)
        copy(src.at[part], dst.at[part], *rest).start()


class Copy:
    def __init__(self, src, dst, count, *rest):
        self.src, self.dst, self.count, self.rest = src, dst, count, rest

    def start(self):
        start_pieces(remote, self.src, self.dst, self.count, *self.rest)

    def wait_send(self):
        remote(self.src, self.dst, *self.rest).wait_send()

    def wait_recv(self):
        remote(self.src, self.dst, *self.rest).wait_recv()


def piece_count(shape, size):
    count = max(1, shape[0] * shape[1] * 2 // size)
    while shape[0] % (16 * count):
        count -= 1
    return count


class Place:
    def __init__(self, nb, nh):
        self.nb, self.nh, self.nz = nb, nh, nb // 2
        self.b, self.h = lax.axis_index("blk"), lax.axis_index("head")
        self.z, self.core = self.b // 2, lax.rem(self.b, 2)
        self.sibling = 2 * self.z + 1 - self.core

    def in_blk(self, b):
        return (b, self.h)

    def in_head(self, h):
        return (self.b, h)

    def head_peer(self, k):
        return lax.rem(self.h + k, self.nh)

    def blk_peer(self, k):
        return lax.rem(self.b + k, self.nb)

    def meet(self):
        barrier = pltpu.get_barrier_semaphore()
        for k in range(1, self.nh):
            pl.semaphore_signal(
                barrier, inc=1, device_id=self.in_head(self.head_peer(k)), device_id_type=MESH
            )
        for k in range(1, self.nb):
            pl.semaphore_signal(
                barrier, inc=1, device_id=self.in_blk(self.blk_peer(k)), device_id_type=MESH
            )
        pl.semaphore_wait(barrier, self.nh + self.nb - 2)


class Relay:
    def __init__(self, at, buf, send, recv, count=1):
        self.at, self.buf, self.send, self.recv, self.count = at, buf, send, recv, count

    def copy(self, s, way, device):
        return Copy(
            self.buf.at[s], self.buf.at[s], self.count, self.send.at[way, s], self.recv.at[s], device
        )

    def right(self, s):
        return self.copy(s, 0, self.at.in_blk(jnp.minimum(self.at.b + 2, self.at.nb - 2 + self.at.core)))

    def left(self, s):
        return self.copy(s, 1, self.at.in_blk(jnp.maximum(self.at.b - 2, self.at.core)))

    def across(self, s):
        return self.copy(s, 2, self.at.in_blk(self.at.sibling))

    def begin(self):
        at = self.at
        pl.when(at.z + 1 < at.nz)(lambda: self.right(at.b).start())
        pl.when(at.z > 0)(lambda: self.left(at.b).start())
        self.across(at.b).start()

    def hop(self, i):
        at = self.at

        @pl.when(at.z >= i)
        def _():
            s = at.b - 2 * i
            self.across(s).wait_recv()
            pl.when(at.z + 1 < at.nz)(lambda: self.right(s).start())
            self.across(s).start()

        @pl.when(at.z + i < at.nz)
        def _():
            s = at.b + 2 * i
            self.across(s).wait_recv()
            pl.when(at.z > 0)(lambda: self.left(s).start())
            self.across(s).start()

    def take_sibling(self, z):
        self.across(2 * z + 1 - self.at.core).wait_recv()

    def finish(self):
        at = self.at
        for i in range(at.nz):

            @pl.when(at.z >= i)
            def _():
                s = at.b - 2 * i
                pl.when(at.z + 1 < at.nz)(lambda: self.right(s).wait_send())
                self.across(s).wait_send()

            if i == 0:
                pl.when(at.z > 0)(lambda: self.left(at.b).wait_send())
            else:

                @pl.when(at.z + i < at.nz)
                def _():
                    s = at.b + 2 * i
                    pl.when(at.z > 0)(lambda: self.left(s).wait_send())
                    self.across(s).wait_send()

    def all(self):
        self.begin()
        for i in range(1, self.at.nz):
            self.hop(i)
        for z in range(self.at.nz):
            self.take_sibling(z)


class Deal:
    def __init__(self, at, chunk, arrived, sems, local_sems):
        self.at, self.chunk, self.arrived = at, chunk, arrived
        self.sems, self.local_sems = sems, local_sems

    def ends(self, j, k):
        at = self.at
        p = at.blk_peer(k)
        return (
            self.chunk(j, p),
            self.arrived[j].at[at.b],
            self.sems.at[0, j, k],
            self.sems.at[1, j, k],
            at.in_blk(p),
        )

    def own(self, j):
        at = self.at
        return pltpu.make_async_copy(
            self.chunk(j, at.b), self.arrived[j].at[at.b], self.local_sems.at[j]
        )

    def start(self, first, last):
        nb = self.at.nb
        if first == 0:
            for j in range(3):
                self.own(j).start()
        rest = [(0, k) for k in range(nb // 2 + 1, nb)]
        rest += [(j, k) for k in range(1, nb) for j in (1, 2)]
        for j, k in rest[int(len(rest) * first) : int(len(rest) * last)]:
            remote(*self.ends(j, k)).start()

    def one(self, z):
        remote(*self.ends(0, 1 + z)).start()

    def end(self):
        for j in range(3):
            for k in range(1, self.at.nb):
                move = remote(*self.ends(j, k))
                move.wait_recv()
                move.wait_send()
            self.own(j).wait()


def sorted_place(at, half, shape, axis):
    s = lax.broadcasted_iota(jnp.int32, shape, axis)
    return jnp.where(
        s < half, at.b * half + s, (2 * at.nb - 1 - at.b) * half + s - half
    )


def begin_of(place, lengths):
    start, begin = 0, jnp.zeros_like(place)
    for i in range(lengths.shape[0] - 1):
        start = start + lengths[i]
        begin = begin + jnp.where(place >= start, lengths[i], 0)
    return begin


def rotation(place, begin):
    shape = (HEAD_SIZE // 2, place.shape[1])
    index = lax.broadcasted_iota(jnp.int32, shape, 0).astype(F32)
    freq = jnp.exp(index * (-2.0 * math.log(rope_base) / HEAD_SIZE))
    angle = freq * (place - begin).astype(F32)
    return jnp.cos(angle), jnp.sin(angle)


def column_of(row):
    wide = jnp.broadcast_to(row.astype(F32), (128, row.shape[1]))
    return wide.T[:, :1].astype(jnp.int32)


def block_base(at, b, second, half):
    return jnp.where(second == 0, b * half, (2 * at.nb - 1 - b) * half)


def turn_rows(values, cos, sin):
    half = HEAD_SIZE // 2
    pieces = []
    for first in range(0, values.shape[0], HEAD_SIZE):
        lead = values[first : first + half]
        trail = values[first + half : first + HEAD_SIZE]
        pieces.append(lead * cos - trail * sin)
        pieces.append(trail * cos + lead * sin)
    return jnp.concatenate(pieces, axis=0)


def pick_targets(slots, pair_rows):
    lane = lax.broadcasted_iota(jnp.int32, slots.shape, 1)
    kept = (slots >= 0) & (slots < CAP)
    return jnp.where(kept, slots + jnp.where(lane >= pair_rows // 2, CAP, 0), -1)


def hits(target_row, pair_rows):
    return lax.broadcasted_iota(jnp.int32, (2 * CAP, pair_rows), 0) == target_row


def diagonal():
    shape = (2 * CAP, 2 * CAP)
    return lax.broadcasted_iota(jnp.int32, shape, 0) == lax.broadcasted_iota(jnp.int32, shape, 1)


def to_row(column):
    return jnp.sum(jnp.where(diagonal(), column, 0.0), axis=0, keepdims=True)


def to_column(row):
    return jnp.sum(jnp.where(diagonal(), row, 0.0), axis=1, keepdims=True)


def split_product(dot, left, right):
    high = left.astype(BF)
    low = (left - high.astype(F32)).astype(BF)
    return dot(high, right) + dot(low, right)


def front_kernel(
    nb,
    nh,
    hl,
    kl,
    repeat,
    inputs,
    w_norm1,
    w_norm2,
    w_own,
    places,
    lengths,
    grad_out,
    table,
    router_t,
    w_gate,
    w_up,
    w_down,
    xg,
    wg,
    qt,
    kv,
    lse,
    attn_t,
    ao_t,
    middle,
    n2,
    slots,
    own_gates,
    in_gate,
    in_rows,
    in_g,
    gate_in,
    up_in,
    down_in,
    ao,
    perm,
    top,
    total,
    out_send,
    out_recv,
    x_sems,
    w_send,
    w_recv,
    kv_send,
    kv_recv,
    o_sems,
    slot_all,
    g_all,
    n2_all,
    gates,
    out_rows,
    out_g,
    out_gate,
    s_send,
    s_recv,
    g_send,
    g_recv,
    n_send,
    n_recv,
    row_sems,
    g_sems,
    gate_sems,
    local_sems,
    deal_sems,
    deal_local,
    begin,
):
    at = Place(nb, nh)
    rows = inputs.shape[0]
    group = rows * nh
    half = group // 2
    qw, kw = hl * HEAD_SIZE, kl * HEAD_SIZE
    width = qw + 2 * kw

    hidden = inputs[...].astype(F32)
    unit = hidden * lax.rsqrt(jnp.mean(hidden * hidden, axis=-1, keepdims=True) + eps)
    xg[at.h] = (unit * w_norm1[...]).astype(BF)
    wg[at.b] = w_own[...]
    slot_all[at.b] = table[...]
    g_all[at.b] = grad_out[...]
    at.meet()
    x_copies = [
        remote(xg.at[at.h], xg.at[at.h], x_sems.at[0, k], x_sems.at[1, k], at.in_head(at.head_peer(k)))
        for k in range(1, nh)
    ]
    for c in x_copies:
        c.start()
    weights = Relay(at, wg, w_send, w_recv)
    weights.begin()
    slot_relay = Relay(at, slot_all, s_send, s_recv)
    slot_relay.begin()
    g_relay = Relay(at, g_all, g_send, g_recv, 4)
    pair = 2 * rows
    own_expert = (at.b // repeat) * nh

    def chunk(j, p):
        w_j = (w_gate, w_up, w_down)[j]
        if repeat == 1:
            return w_j.at[p]
        fr = w_gate.shape[2] // repeat
        part = pl.ds(pl.multiple_of(lax.rem(p, repeat) * fr, fr), fr)
        return w_j.at[p // repeat, part] if j == 2 else w_j.at[p // repeat, :, part]

    deal = Deal(at, chunk, (gate_in, up_in, down_in), deal_sems, deal_local)

    def go(buf_out, buf_in, sems, z, k, count=1):
        peer = at.head_peer(k)
        return Copy(
            buf_out.at[z, peer],
            buf_in.at[z, at.h],
            count,
            sems.at[0, z, k],
            sems.at[1, z, k],
            at.in_head(peer),
        )

    def keep(buf_out, buf_in, j, z):
        return pltpu.make_async_copy(buf_out.at[z, at.h], buf_in.at[z, at.h], local_sems.at[j, z])

    def outward(relay, body, first, last, hopped=0):
        def step(t, unused):
            d, side = t // 2, lax.rem(t, 2)
            z = jnp.where(side == 0, at.z - d, at.z + d)
            pl.when((side == 0) & (d > hopped))(lambda: relay.hop(d))

            @pl.when((z >= 0) & (z < at.nz) & ((d > 0) | (side == 0)))
            def _():
                relay.take_sibling(z)
                body(z)

            return 0

        lax.fori_loop(2 * first, 2 * last, step, 0)

    def send_g(z):
        x = g_all[pl.ds(2 * z, 2)].reshape(pair, MODEL_WIDTH)
        for k in list(range(1, nh)) + [0]:
            peer = at.head_peer(k)
            hit = hits(pick_targets(slots[z, pl.ds(own_expert + peer, 1)], pair), pair)
            out_g[z, peer] = nn(jnp.where(hit, 1.0, 0.0).astype(BF), x).astype(BF)
            if k == 0:
                keep(out_g, in_g, 0, z).start()
            else:
                go(out_g, in_g, g_sems, z, k, 5).start()

    def send_rows(z):
        x = n2_all[pl.ds(2 * z, 2)].reshape(pair, MODEL_WIDTH)
        routed = slots[z] >= 0
        logits = jnp.where(routed, nt(router_t[...], x), -1e30)
        shifted = jnp.exp(logits - jnp.max(logits, axis=0, keepdims=True))
        shifted = jnp.where(routed, shifted, 0.0)
        gates[z] = shifted / jnp.sum(shifted, axis=0, keepdims=True)
        for k in list(range(1, nh)) + [0]:
            peer = at.head_peer(k)
            hit = hits(pick_targets(slots[z, pl.ds(own_expert + peer, 1)], pair), pair)
            gate_row = gates[z, pl.ds(own_expert + peer, 1)]
            gate = to_row(jnp.sum(jnp.where(hit, gate_row, 0.0), axis=1, keepdims=True))
            out_rows[z, peer] = nn(jnp.where(hit, 1.0, 0.0).astype(BF), x).astype(BF)
            if k == 0:
                keep(out_rows, in_rows, 1, z).start()
                in_gate[z, at.h] = gate
            else:
                go(out_rows, in_rows, row_sems, z, k).start()
                out_gate[z, peer] = gate
                go(out_gate, in_gate, gate_sems, z, k).start()

    place_row = places[at.b]
    cos, sin = rotation(place_row, begin_of(place_row, lengths))
    in_order = begin_of(sorted_place(at, half, (1, group), 1), lengths)
    begin[0] = in_order[:, :half]
    begin[1] = in_order[:, half:]
    place_col = column_of(place_row)
    perm[...] = jnp.where(
        place_row == sorted_place(at, half, (group, group), 0), 1.0, 0.0
    ).astype(BF)
    for i in range(1, nb // 2):
        slot_relay.hop(i)
        weights.hop(i)
    g_relay.begin()
    for z in range(nb // 2):
        slot_relay.take_sibling(z)
    for z in range(nb // 2):
        slots[z] = jnp.concatenate([slot_all[2 * z], slot_all[2 * z + 1]], axis=1)
    outward(g_relay, send_g, 0, 1)
    deal.start(0, FRONT_DEAL[0])
    for z in range(nb // 2):
        weights.take_sibling(z)
    for c in x_copies:
        c.wait_recv()
    x = xg[...].reshape(group, MODEL_WIDTH)
    w = wg[...].reshape(MODEL_WIDTH, width + qw)
    qkv_t = nn(x, w[:, :width]).T
    qkv_t = jnp.concatenate(
        [turn_rows(qkv_t[: qw + kw], cos, sin), qkv_t[qw + kw :]], axis=0
    ).astype(BF)
    order = perm[...]
    kv_rows = nt(order, qkv_t[qw:]).astype(BF)
    kv[at.b, 0] = kv_rows[:half]
    kv[at.b, 1] = kv_rows[half:]

    def kv_copy(p, second, way, device):
        return remote(
            kv.at[p, second], kv.at[p, second], kv_send.at[way, p], kv_recv.at[p], device
        )

    right = at.in_blk(jnp.minimum(at.b + 2, nb - 2 + at.core))
    left = at.in_blk(jnp.maximum(at.b - 2, at.core))
    across = at.in_blk(at.sibling)
    pl.when(at.z + 1 < at.nz)(lambda: kv_copy(at.b, 0, 0, right).start())
    pl.when(at.z > 0)(lambda: kv_copy(at.b, 1, 0, left).start())
    kv_copy(at.b, at.core, 1, across).start()
    q_cols = (nt(qkv_t[:qw], order) * (1.0 / math.sqrt(HEAD_SIZE))).astype(BF)
    qt[0] = q_cols[:, :half]
    qt[1] = q_cols[:, half:]
    outward(g_relay, send_g, 1, 2)
    top[...] = jnp.full(top.shape, -1e30, F32)
    total[...] = jnp.zeros(total.shape, F32)
    attn_t[...] = jnp.zeros(attn_t.shape, F32)

    def attend(p, second):
        old_top, old_total = top[second], total[second]
        tops, totals = [], []
        block = kv[p, second]
        key_place = block_base(at, p, second, half) + lax.broadcasted_iota(
            jnp.int32, (half, half), 0
        )
        own_place = block_base(at, at.b, second, half) + lax.broadcasted_iota(
            jnp.int32, (half, half), 1
        )
        allowed = (key_place <= own_place) & (key_place >= begin[second])
        for a in range(hl):
            g = a // (hl // kl)
            rows_a = slice(a * HEAD_SIZE, (a + 1) * HEAD_SIZE)
            scores = nn(block[:, g * HEAD_SIZE : (g + 1) * HEAD_SIZE], qt[second, rows_a])
            scores = jnp.where(allowed, scores, -1e30)
            old = old_top[a : a + 1]
            new = jnp.maximum(old, jnp.max(scores, axis=0, keepdims=True))
            probs = jnp.exp(scores - new)
            fade = jnp.exp(old - new)
            totals.append(old_total[a : a + 1] * fade + jnp.sum(probs, axis=0, keepdims=True))
            tops.append(new)
            attn_t[second, rows_a] = attn_t[second, rows_a] * fade + tn(
                block[:, kw + g * HEAD_SIZE : kw + (g + 1) * HEAD_SIZE], probs.astype(BF)
            )
        top[second, :hl] = jnp.concatenate(tops, axis=0)
        total[second, :hl] = jnp.concatenate(totals, axis=0)

    def visit(step, unused):
        i = step // 4
        second = lax.rem(step, 2)
        same = lax.rem(step // 2, 2) == 0
        z = jnp.where(second == 0, at.z - i, at.z + i)
        p = 2 * z + jnp.where(same, at.core, 1 - at.core)
        exists = (z >= 0) & (z < nb // 2) & ((i > 0) | same | (at.core != second))

        @pl.when(exists)
        def _():
            @pl.when(p != at.b)
            def _():
                kv_copy(p, second, 1, across).wait_recv()

            @pl.when((i > 0) & same)
            def _():
                @pl.when((second == 0) & (at.z + 1 < at.nz))
                def _():
                    kv_copy(p, second, 0, right).start()

                @pl.when((second == 1) & (at.z > 0))
                def _():
                    kv_copy(p, second, 0, left).start()

                kv_copy(p, second, 1, across).start()

            attend(p, second)

        return 0

    lax.fori_loop(0, 4 * (nb // 2), visit, 0)
    for i in range(2, min(3, at.nz)):
        g_relay.hop(i)
    deal.start(FRONT_DEAL[0], FRONT_DEAL[1])
    for second in range(2):
        sums = total[second]
        for a in range(hl):
            rows_a = slice(a * HEAD_SIZE, (a + 1) * HEAD_SIZE)
            attn_t[second, rows_a] = attn_t[second, rows_a] / sums[a : a + 1]
    lse[...] = top[...] + jnp.log(total[...])
    back = jnp.where(place_col == sorted_place(at, half, (group, group), 1), 1.0, 0.0).astype(BF)
    attn_rows = (
        nt(back[:, :half], attn_t[0].astype(BF)) + nt(back[:, half:], attn_t[1].astype(BF))
    ).astype(BF)
    ao[...] = attn_rows
    ao_t[...] = (
        nn(attn_t[0].astype(BF), perm[:half]) + nn(attn_t[1].astype(BF), perm[half:])
    ).astype(BF)
    o_copies = []
    for k in range(nh):
        peer = at.head_peer(k)
        chunk = nt(ao[pl.ds(peer * rows, rows)], w[:, width:])
        if k == 0:
            middle[...] = hidden + chunk
            continue
        out_send[peer] = chunk.astype(BF)
        c = remote(
            out_send.at[peer], out_recv.at[at.h], o_sems.at[0, k], o_sems.at[1, k], at.in_head(peer)
        )
        c.start()
        o_copies.append(c)
    outward(g_relay, send_g, 2, at.nz, 2)
    for k in range(1, nh):
        o_copies[k - 1].wait_recv()
        middle[...] += out_recv[lax.rem(at.h + nh - k, nh)].astype(F32)
    mid = middle[...]
    n2[...] = (
        mid * lax.rsqrt(jnp.mean(mid * mid, axis=-1, keepdims=True) + eps) * w_norm2[...]
    ).astype(BF)
    n2_all[at.b] = n2[...]
    n_relay = Relay(at, n2_all, n_send, n_recv)
    n_relay.begin()

    def send_both(z):
        send_rows(z)
        deal.one(z)

    outward(n_relay, send_both, 0, at.nz)
    deal.start(FRONT_DEAL[1], 1)
    own_gates[...] = jnp.where(at.core == 0, gates[at.z, :, :rows], gates[at.z, :, rows:])
    for relay in (weights, slot_relay, g_relay, n_relay):
        relay.finish()
    for c in x_copies + o_copies:
        c.wait_send()

    def drain(step, unused):
        i = step // 2
        second = lax.rem(step, 2)
        z = jnp.where(second == 0, at.z - i, at.z + i)
        p = 2 * z + at.core

        @pl.when((z >= 0) & (z < nb // 2))
        def _():
            @pl.when((second == 0) & (at.z + 1 < at.nz))
            def _():
                kv_copy(p, second, 0, right).wait_send()

            @pl.when((second == 1) & (at.z > 0))
            def _():
                kv_copy(p, second, 0, left).wait_send()

            @pl.when((i > 0) | (second == at.core))
            def _():
                kv_copy(p, second, 1, across).wait_send()

        return 0

    lax.fori_loop(0, nb, drain, 0)

    def end(z, unused):
        for k in range(1, nh):
            for move in (
                go(out_g, in_g, g_sems, z, k),
                go(out_rows, in_rows, row_sems, z, k),
                go(out_gate, in_gate, gate_sems, z, k),
            ):
                move.wait_recv()
                move.wait_send()
        keep(out_g, in_g, 0, z).wait()
        keep(out_rows, in_rows, 1, z).wait()
        return 0

    lax.fori_loop(0, at.nz, end, 0)
    deal.end()


def front(nb, nh, hl, kl, repeat, *operands):
    inputs, w_own = operands[0], operands[3]
    hidden_units = operands[9].shape[2]
    fr = hidden_units // repeat
    rows = inputs.shape[0]
    group, half = rows * nh, rows * nh // 2
    nz = nb // 2
    dl, wide = w_own.shape
    qw, kw = hl * HEAD_SIZE, kl * HEAD_SIZE
    shape = jax.ShapeDtypeStruct
    dma = pltpu.SemaphoreType.DMA
    chunk = (nz, nh, 2 * CAP, MODEL_WIDTH)
    line = (nz, nh, 1, 2 * CAP)
    relay_sems = [dma((3, nb)), dma((nb,))]
    return pl.pallas_call(
        functools.partial(front_kernel, nb, nh, hl, kl, repeat),
        out_shape=(
            shape((nh, rows, MODEL_WIDTH), BF),
            shape((nb, dl, wide), BF),
            shape((2, qw, half), BF),
            shape((nb, 2, half, 2 * kw), BF),
            shape((2, max(hl, 8), half), F32),
            shape((2, qw, half), F32),
            shape((qw, group), BF),
            shape((rows, MODEL_WIDTH), F32),
            shape((rows, MODEL_WIDTH), BF),
            shape((nz, E, 2 * rows), jnp.int32),
            shape((E, rows), F32),
            shape(line, F32),
            shape(chunk, BF),
            shape(chunk, BF),
            shape((nb, dl, fr), BF),
            shape((nb, dl, fr), BF),
            shape((nb, fr, dl), BF),
        ),
        in_specs=[VMEM] * 5 + [SMEM] + [VMEM] * 3 + [ANY] * 3,
        out_specs=[VMEM] * 12 + [ANY] * 5,
        scratch_shapes=[
            pltpu.VMEM((group, qw), BF),
            pltpu.VMEM((group, group), BF),
            pltpu.VMEM((2, max(hl, 8), half), F32),
            pltpu.VMEM((2, max(hl, 8), half), F32),
            pltpu.VMEM((nh, rows, MODEL_WIDTH), BF),
            pltpu.VMEM((nh, rows, MODEL_WIDTH), BF),
            dma((2, nh)),
            dma((3, nb)),
            dma((nb,)),
            dma((2, nb)),
            dma((nb,)),
            dma((2, nh)),
            pltpu.VMEM((nb, E, rows), jnp.int32),
            pltpu.VMEM((nb, rows, MODEL_WIDTH), BF),
            pltpu.VMEM((nb, rows, MODEL_WIDTH), BF),
            pltpu.VMEM((nz, E, 2 * rows), F32),
            pltpu.VMEM(chunk, BF),
            pltpu.VMEM(chunk, BF),
            pltpu.VMEM(line, F32),
            *relay_sems,
            *relay_sems,
            *relay_sems,
            dma((2, nz, nh)),
            dma((2, nz, nh)),
            dma((2, nz, nh)),
            dma((2, nz)),
            dma((2, 3, nb)),
            dma((3,)),
            pltpu.VMEM((2, 1, half), jnp.int32),
        ],
        compiler_params=pltpu.CompilerParams(collective_id=1, vmem_limit_bytes=60 * 2**20),
        name="front",
    )(*operands)


def slot_table(nb, nh, repeat, routes, slot_order):
    local = E // nh
    mine = (routes % local) * nh + routes // local
    match = mine.T[:, None, :] == jnp.arange(E, dtype=jnp.int32)[None, :, None]
    order = jnp.min(jnp.where(match, slot_order.T[:, None, :], 1 << 20), axis=0)
    before = jnp.sum((order[:, :, None] < order[:, None, :]).astype(jnp.int32), axis=1)
    return jnp.where(order < (1 << 20), before, -1)


def experts_kernel(
    nz,
    nh,
    x_ref,
    g_ref,
    gate_ref,
    w_gate_ref,
    w_up_ref,
    w_down_ref,
    d_rows,
    scaled,
    d_gate_row,
    grad_gate,
    grad_up,
    grad_down,
    w_down,
    sum_gate,
    sum_up,
    sum_down,
):
    step = pl.program_id(0)
    nb, dl, fr = w_gate_ref.shape

    @pl.when(step == 0)
    def _():
        w_down[...] = jnp.concatenate([w_down_ref[p] for p in range(nb)], axis=1)
        for total in (sum_gate, sum_up, sum_down):
            total[...] = jnp.zeros(total.shape, F32)

    x = x_ref[0].reshape(nh * 2 * CAP, MODEL_WIDTH)
    gate = jnp.concatenate([to_column(gate_ref[0, h]) for h in range(nh)], axis=0)
    w_gate = w_gate_ref[...].reshape(MODEL_WIDTH, fr)
    w_up = w_up_ref[...].reshape(MODEL_WIDTH, fr)
    gate_pre, up_pre = nn(x, w_gate), nn(x, w_up)
    sigma = 1.0 / (1.0 + jnp.exp(-gate_pre))
    swish = gate_pre * sigma
    activated = (swish * up_pre).astype(BF)
    out = nn(activated, w_down[...]).astype(BF).astype(F32)
    g = g_ref[0].reshape(nh * 2 * CAP, MODEL_WIDTH).astype(F32)
    d_gate = jnp.sum(out * g, axis=1, keepdims=True)
    d_out = (gate * g).astype(BF)
    scaled[0] = (gate * out).astype(BF).reshape(nh, 2 * CAP, MODEL_WIDTH)
    d_act = nt(d_out, w_down[...])
    d_gate_pre = (d_act * up_pre * sigma * (1.0 + gate_pre * (1.0 - sigma))).astype(BF)
    d_up_pre = (d_act * swish).astype(BF)
    back_rows = (nt(d_gate_pre, w_gate) + nt(d_up_pre, w_up)).astype(BF)
    d_rows[0] = back_rows.reshape(nh, 2 * CAP, MODEL_WIDTH)
    for h in range(nh):
        d_gate_row[0, h] = to_row(d_gate[h * 2 * CAP : (h + 1) * 2 * CAP])
    sum_gate[...] += tn(x, d_gate_pre)
    sum_up[...] += tn(x, d_up_pre)
    sum_down[...] += tn(activated, d_out)

    @pl.when(step == nz - 1)
    def _():
        for p in range(nb):
            own = slice(p * dl, (p + 1) * dl)
            grad_gate[p] = sum_gate[own].astype(BF)
            grad_up[p] = sum_up[own].astype(BF)
            grad_down[p] = sum_down[:, own].astype(BF)


def experts(nz, nh, x, g, gate, w_gate, w_up, w_down):
    nb, dl, fr = w_gate.shape
    shape = jax.ShapeDtypeStruct
    wide = pl.BlockSpec((1,) + x.shape[1:], lambda i: (i, 0, 0, 0))
    line = pl.BlockSpec((1,) + gate.shape[1:], lambda i: (i, 0, 0, 0))
    deep = pl.BlockSpec(w_gate.shape, lambda i: (0, 0, 0))
    flat = pl.BlockSpec(w_down.shape, lambda i: (0, 0, 0))
    return pl.pallas_call(
        functools.partial(experts_kernel, nz, nh),
        grid=(nz,),
        out_shape=(
            shape(x.shape, BF),
            shape(x.shape, BF),
            shape(gate.shape, F32),
            shape(w_gate.shape, BF),
            shape(w_up.shape, BF),
            shape(w_down.shape, BF),
        ),
        in_specs=[wide, wide, line, deep, deep, flat],
        out_specs=[wide, wide, line, deep, deep, flat],
        scratch_shapes=[
            pltpu.VMEM((fr, MODEL_WIDTH), BF),
            pltpu.VMEM((MODEL_WIDTH, fr), F32),
            pltpu.VMEM((MODEL_WIDTH, fr), F32),
            pltpu.VMEM((fr, MODEL_WIDTH), F32),
        ],
        compiler_params=pltpu.CompilerParams(vmem_limit_bytes=60 * 2**20),
        name="experts",
    )(x, g, gate, w_gate, w_up, w_down)


class Scatter:
    def __init__(self, at, bufs, sems):
        self.at, self.sems = at, sems
        self.sib_out, self.sib_in, self.z_out, self.z_in = (bufs.at[j] for j in range(4))

    def across(self, z):
        return remote(
            self.sib_out.at[z],
            self.sib_in.at[z],
            self.sems.at[0, z],
            self.sems.at[1, z],
            self.at.in_blk(self.at.sibling),
        )

    def along(self, z):
        at = self.at
        slot = jnp.where(z == at.z - 1, at.nz, z)
        ahead = jnp.clip(jnp.where(z > at.z, at.z + 1, at.z - 1), 0, at.nz - 1)
        return remote(
            self.z_out.at[z],
            self.z_in.at[slot],
            self.sems.at[2, z],
            self.sems.at[3, slot],
            at.in_blk(2 * ahead + at.core),
        )

    def arrived(self, slot):
        at = self.at
        remote(
            self.z_out.at[0],
            self.z_in.at[slot],
            self.sems.at[2, 0],
            self.sems.at[3, slot],
            at.in_blk(at.sibling),
        ).wait_recv()
        return self.z_in[slot].astype(F32)

    def give_sibling(self, z, value):
        self.sib_out[z] = value.astype(BF)
        self.across(z).start()

    def from_sibling(self, z):
        self.across(z).wait_recv()
        return self.sib_in[z].astype(F32)

    def give(self, z, value):
        at = self.at
        joins = ((z > at.z) & (at.z > 0)) | ((z < at.z) & (at.z < at.nz - 1))

        @pl.when(joins)
        def _():
            self.z_out[z] = (value + self.arrived(z)).astype(BF)

        @pl.when(jnp.logical_not(joins))
        def _():
            self.z_out[z] = value.astype(BF)

        self.along(z).start()

    def take(self, add):
        at = self.at
        pl.when(at.z > 0)(lambda: add(self.arrived(at.z), True))
        pl.when(at.z < at.nz - 1)(lambda: add(self.arrived(at.nz), False))

    def finish(self):
        at = self.at
        for z in range(at.nz):
            self.across(z).wait_send()
            pl.when(at.z != z)(lambda: self.along(z).wait_send())


class Total:
    def __init__(self, at, part, by_head, by_blk, whole, sems):
        self.at, self.part, self.by_head, self.by_blk, self.whole = at, part, by_head, by_blk, whole
        self.sems = sems

    def copy(self, stage, k):
        at = self.at
        peer = at.blk_peer(k) if stage == 1 else at.head_peer(k)
        device = at.in_blk(peer) if stage == 1 else at.in_head(peer)
        if stage == 0:
            src, dst = self.part.at[peer], self.by_head.at[at.h]
        elif stage == 1:
            src, dst = self.by_blk.at[at.b], self.by_blk.at[at.b]
        else:
            src, dst = self.whole.at[at.h], self.whole.at[at.h]
        return remote(src, dst, self.sems.at[0, stage, k], self.sems.at[1, stage, k], device)

    def peers(self, stage):
        return range(1, self.at.nb if stage == 1 else self.at.nh)

    def begin(self, stage):
        at = self.at
        if stage == 0:
            self.by_head[at.h] = self.part[at.h]
        elif stage == 1:
            self.by_blk[at.b] = sum_slots(self.by_head, at.nh)
        else:
            self.whole[at.h] = sum_slots(self.by_blk, at.nb)
        for k in self.peers(stage):
            self.copy(stage, k).start()

    def end(self, stage):
        for k in self.peers(stage):
            self.copy(stage, k).wait_recv()

    def finish(self):
        for stage in range(3):
            for k in self.peers(stage):
                self.copy(stage, k).wait_send()


def sum_slots(ref, n):
    total = ref[0]
    for s in range(1, n):
        total = total + ref[s]
    return total


def back_kernel(
    nb,
    nh,
    hl,
    kl,
    repeat,
    inputs,
    w_norm1,
    w_norm2,
    middle,
    n2,
    grad_out,
    router_t,
    slots,
    own_gates,
    d_gate_rows,
    wg,
    xg,
    ao_t,
    qt,
    kv,
    lse,
    attn_t,
    places,
    lengths,
    d_rows,
    scaled,
    gate_sum,
    up_sum,
    down_sum,
    output,
    grad_in,
    grad_q,
    grad_k,
    grad_v,
    grad_o,
    grad_n1,
    small_sum,
    gate_in,
    up_in,
    down_in,
    dbg,
    perm,
    d_rows_ref,
    do_t,
    delta,
    dq_t,
    own_kv,
    kv_bufs,
    w_part,
    w_bufs,
    out_send,
    out_recv,
    n1_head,
    n1_blk,
    s_head,
    s_blk,
    d_sems,
    kv_sems,
    w_sems,
    o_sems,
    n_sems,
    s_sems,
    small,
    back_rows,
    in_dgate,
    own_part,
    d_middle,
    dg_out,
    dg_in,
    sc_bufs,
    sc_sems,
    mix_sems,
    ret_sems,
    eout_sems,
    dgate_sems,
    dg_sems,
    local_sems,
    deal_sems,
    deal_local,
    begin,
    grad_w,
    *loaded,
):
    at = Place(nb, nh)
    nz = at.nz
    rows = inputs.shape[0]
    group = rows * nh
    half = group // 2
    qw, kw = hl * HEAD_SIZE, kl * HEAD_SIZE
    width = qw + 2 * kw
    dl = MODEL_WIDTH // nb
    scale = 1.0 / math.sqrt(HEAD_SIZE)

    pair = 2 * rows
    own_expert = (at.b // repeat) * nh
    at.meet()

    def go(buf_out, buf_in, sems, z, k, count=1):
        peer = at.head_peer(k)
        return Copy(
            buf_out.at[z, peer],
            buf_in.at[z, at.h],
            count,
            sems.at[0, z, k],
            sems.at[1, z, k],
            at.in_head(peer),
        )

    def keep(buf_out, j, z):
        return pltpu.make_async_copy(buf_out.at[z, at.h], back_rows.at[z, at.h], local_sems.at[j, z])

    def far_first(body):
        def step(t, unused):
            d, side = nz - 1 - t // 2, lax.rem(t, 2)
            z = jnp.where(side == 0, at.z - d, at.z + d)

            @pl.when((z >= 0) & (z < nz) & ((d > 0) | (side == 0)))
            def _():
                body(z)

            return 0

        lax.fori_loop(0, 2 * nz, step, 0)

    def send_back(z):
        for k in range(1, nh):
            go(d_rows, back_rows, ret_sems, z, k).start()
            go(d_gate_rows, in_dgate, dgate_sems, z, k).start()
        keep(d_rows, 0, z).start()
        in_dgate[z, at.h] = d_gate_rows[z, at.h]

    far_first(send_back)
    load_sems = loaded[-1]
    sources = (wg, xg, ao_t, qt, kv, attn_t)
    loads = [
        pltpu.make_async_copy(src, dst, load_sems.at[i])
        for i, (src, dst) in enumerate(zip(sources, loaded[:-1]))
    ]
    for c in loads:
        c.start()
    wg, xg, ao_t, qt, kv, attn_t = loaded[:-1]
    place_row = places[at.b]
    sorted_row = sorted_place(at, half, (1, group), 1)
    in_order = begin_of(sorted_row, lengths)
    begin[0] = in_order[:, :half]
    begin[1] = in_order[:, half:]
    cos, sin = rotation(sorted_row, in_order)
    place_col = column_of(place_row)
    sums_of = (gate_sum, up_sum, down_sum)
    deal = Deal(at, lambda j, p: sums_of[j].at[p], (gate_in, up_in, down_in), deal_sems, deal_local)
    deal.start(0, BACK_DEAL[0])
    n2_scatter = Scatter(at, sc_bufs, sc_sems)

    def dg_copy(p):
        return remote(
            dg_out.at[p], dg_in.at[at.b], dg_sems.at[0, p], dg_sems.at[1, at.b], at.in_blk(p)
        )

    def masks_of(z):
        return [
            hits(pick_targets(slots[z, pl.ds(own_expert + h, 1)], pair), pair) for h in range(nh)
        ]

    def spread(z, masks, scatter):
        hit_rows = jnp.concatenate([jnp.where(m, 1.0, 0.0).astype(BF) for m in masks], axis=0)
        part = tn(hit_rows, back_rows[z].reshape(nh * 2 * CAP, MODEL_WIDTH))
        own_part[0] = part[:rows]
        own_part[1] = part[rows:]
        scatter.give_sibling(z, own_part[1 - at.core])

        @pl.when(z != at.z)
        def _():
            scatter.give(z, own_part[at.core] + scatter.from_sibling(z))

    def gathered_part(scatter):
        own_part[2] = own_part[at.core] + scatter.from_sibling(at.z)

        def add(value, from_left):
            own_part[2] += value

        scatter.take(add)
        return own_part[2]

    def gather_back(z):
        for k in range(1, nh):
            go(d_rows, back_rows, ret_sems, z, k).wait_recv()
            go(d_gate_rows, in_dgate, dgate_sems, z, k).wait_recv()
        keep(d_rows, 0, z).wait()
        masks = masks_of(z)
        d_gates = jnp.concatenate(
            [
                jnp.sum(jnp.where(m, to_column(in_dgate[z, h]), 0.0), axis=0, keepdims=True)
                for h, m in enumerate(masks)
            ],
            axis=0,
        )
        dg_out[2 * z] = d_gates[:, :rows]
        dg_out[2 * z + 1] = d_gates[:, rows:]
        pl.when(z == at.z)(lambda: dg_copy(at.sibling).start())

        @pl.when(z != at.z)
        def _():
            dg_copy(2 * z).start()
            dg_copy(2 * z + 1).start()

        spread(z, masks, n2_scatter)
        deal.one(z)

    far_first(gather_back)
    dg_in[at.b] = dg_out[at.b]
    for k in range(1, nb):
        p = at.blk_peer(k)
        remote(dg_out.at[p], dg_in.at[p], dg_sems.at[0, p], dg_sems.at[1, p], at.in_blk(p)).wait_recv()
    d_gates = jnp.concatenate(
        [sum_slots(dg_in.at[pl.ds(i * repeat, repeat)], repeat) for i in range(nb // repeat)], axis=0
    )
    d_logits = own_gates[...] * (
        d_gates - jnp.sum(own_gates[...] * d_gates, axis=0, keepdims=True)
    )
    from_logits = split_product(tn, d_logits, router_t[...])
    g_router = split_product(nn, d_logits, n2[...])
    mid = middle[...]
    factor_two = lax.rsqrt(jnp.mean(mid * mid, axis=-1, keepdims=True) + eps)
    unit_two = mid * factor_two
    d_n2 = gathered_part(n2_scatter) + from_logits
    weighted_two = d_n2 * w_norm2[...]
    d_middle[...] = grad_out[...].astype(F32) + factor_two * (
        weighted_two - unit_two * jnp.mean(unit_two * weighted_two, axis=-1, keepdims=True)
    )
    dbg[at.h] = d_middle[...].astype(BF)
    d_copies = [
        remote(dbg.at[at.h], dbg.at[at.h], d_sems.at[0, k], d_sems.at[1, k], at.in_head(at.head_peer(k)))
        for k in range(1, nh)
    ]
    for c in d_copies:
        c.start()
    g_norm = jnp.sum(d_n2 * unit_two, axis=0, keepdims=True)
    slab = MODEL_WIDTH // nh
    for h in range(nh):
        cols = slice(h * slab, (h + 1) * slab)
        small[h, :E] = g_router[:, cols]
        small[h, E:] = jnp.broadcast_to(g_norm[:, cols], (8, slab))
    totals = Total(at, small, s_head, s_blk, small_sum, s_sems)
    totals.begin(0)
    perm[...] = jnp.where(
        place_row == sorted_place(at, half, (group, group), 0), 1.0, 0.0
    ).astype(BF)
    dq_t[...] = jnp.zeros(dq_t.shape, F32)
    for c in d_copies:
        c.wait_recv()

    def send_scaled(z):
        for k in range(1, nh):
            go(scaled, back_rows, eout_sems, z, k, 5).start()
        keep(scaled, 1, z).start()

    far_first(send_scaled)
    totals.end(0)
    totals.begin(1)
    deal.start(BACK_DEAL[0], BACK_DEAL[1])
    for c in loads:
        c.wait()
    d_branch = dbg[...].reshape(group, MODEL_WIDTH)
    w = wg[...].reshape(MODEL_WIDTH, width + qw)
    d_attn_t = nn(d_branch, w[:, width:]).T.astype(BF)
    d_sorted = nt(d_attn_t, perm[...])
    for second in range(2):
        piece = d_sorted[:, second * half : (second + 1) * half]
        do_t[second] = piece.astype(BF)
        product = piece * attn_t[second]
        delta[second, :hl] = jnp.concatenate(
            [
                jnp.sum(product[a * HEAD_SIZE : (a + 1) * HEAD_SIZE], axis=0, keepdims=True)
                for a in range(hl)
            ],
            axis=0,
        )

    def step_back(p, second):
        block = kv[p, second]
        lse_all, delta_all = lse[second], delta[second]
        key_place = block_base(at, p, second, half) + lax.broadcasted_iota(
            jnp.int32, (half, half), 0
        )
        own_place = block_base(at, at.b, second, half) + lax.broadcasted_iota(
            jnp.int32, (half, half), 1
        )
        allowed = (key_place <= own_place) & (key_place >= begin[second])
        d_keys, d_values = [None] * kl, [None] * kl
        for a in range(hl):
            g = a // (hl // kl)
            rows_a = slice(a * HEAD_SIZE, (a + 1) * HEAD_SIZE)
            key = block[:, g * HEAD_SIZE : (g + 1) * HEAD_SIZE]
            value = block[:, kw + g * HEAD_SIZE : kw + (g + 1) * HEAD_SIZE]
            scores = jnp.where(allowed, nn(key, qt[second, rows_a]), -1e30)
            probs = jnp.exp(scores - lse_all[a : a + 1])
            d_probs = nn(value, do_t[second, rows_a])
            d_scores = (probs * (d_probs - delta_all[a : a + 1])).astype(BF)
            d_key = nt(qt[second, rows_a], d_scores)
            d_value = nt(do_t[second, rows_a], probs.astype(BF))
            d_keys[g] = d_key if d_keys[g] is None else d_keys[g] + d_key
            d_values[g] = d_value if d_values[g] is None else d_values[g] + d_value
            dq_t[second, rows_a] += tn(key, d_scores)
        return jnp.concatenate(d_keys + d_values, axis=0)

    scatter = Scatter(at, kv_bufs, kv_sems)

    def visit(step, unused):
        i = nz - 1 - step // 4
        second = lax.rem(step // 2, 2)
        same = lax.rem(step, 2) == 1
        z = jnp.where(second == 0, at.z - i, at.z + i)
        p = 2 * z + jnp.where(same, at.core, 1 - at.core)
        exists = (z >= 0) & (z < nz) & ((i > 0) | same | (at.core != second))

        @pl.when(exists)
        def _():
            part = step_back(p, second)

            @pl.when(jnp.logical_not(same))
            def _():
                scatter.give_sibling(z, part)

            @pl.when(same & (i > 0))
            def _():
                scatter.give(z, part + scatter.from_sibling(z))

            @pl.when(same & (i == 0))
            def _():
                own_kv[second] = part

        return 0

    lax.fori_loop(0, 4 * nz, visit, 0)
    deal.start(BACK_DEAL[1], BACK_DEAL[2])
    totals.end(1)
    totals.begin(2)
    wide = 256

    def weight_part(first, left):
        for c in range(MODEL_WIDTH // wide):
            source = xg if first == 0 else dbg
            piece = nn(left, source[:, :, c * wide : (c + 1) * wide].reshape(group, wide))
            for j in range(wide // dl):
                w_part[c * (wide // dl) + j, first : first + left.shape[0]] = piece[
                    :, j * dl : (j + 1) * dl
                ]

    weight_part(width, ao_t[...])
    own_kv[at.core] += scatter.from_sibling(at.z)

    def add_kv(value, from_left):
        own_kv[1 if from_left else 0] += value

    scatter.take(add_kv)

    d_sorted_t = []
    for second in range(2):
        cols = slice(second * half, (second + 1) * half)
        both = own_kv[second]
        turned = jnp.concatenate([dq_t[second] * scale, both[:kw]], axis=0)
        turned = turn_rows(turned, cos[:, cols], -sin[:, cols])
        d_sorted_t.append(jnp.concatenate([turned, both[kw:]], axis=0).astype(BF))
    back = jnp.where(place_col == sorted_place(at, half, (group, group), 1), 1.0, 0.0).astype(BF)
    turned_back = (
        nt(back[:, :half], d_sorted_t[0]) + nt(back[:, half:], d_sorted_t[1])
    ).astype(BF)
    d_rows_ref[...] = turned_back.reshape(nh, rows, width)
    d_cols = (nn(d_sorted_t[0], perm[:half]) + nn(d_sorted_t[1], perm[half:])).astype(BF)
    o_copies = []
    for k in range(1, nh):
        peer = at.head_peer(k)
        out_send[peer] = nt(d_rows_ref[peer], w[:, :width]).astype(BF)
        c = remote(
            out_send.at[peer], out_recv.at[at.h], o_sems.at[0, k], o_sems.at[1, k], at.in_head(peer)
        )
        c.start()
        o_copies.append(c)
    own_normed = nt(d_rows_ref[at.h], w[:, :width])
    weight_part(0, d_cols)
    w_scatter = Scatter(at, w_bufs, w_sems)

    def w_pass(z):
        w_scatter.give_sibling(z, w_part[2 * z + 1 - at.core])

    def w_along(z):
        pl.when(z != at.z)(
            lambda: w_scatter.give(z, w_part[2 * z + at.core] + w_scatter.from_sibling(z))
        )

    far_first(w_pass)
    far_first(w_along)
    n2_scatter.finish()
    mix_scatter = Scatter(at, sc_bufs, mix_sems)

    def mix(z):
        for k in range(1, nh):
            go(scaled, back_rows, eout_sems, z, k).wait_recv()
        keep(scaled, 1, z).wait()
        spread(z, masks_of(z), mix_scatter)

    far_first(mix)
    deal.start(BACK_DEAL[2], 1)
    for k in range(1, nh):
        o_copies[k - 1].wait_recv()
        own_normed = own_normed + out_recv[lax.rem(at.h + nh - k, nh)].astype(F32)
    hidden = inputs[...].astype(F32)
    factor = lax.rsqrt(jnp.mean(hidden * hidden, axis=-1, keepdims=True) + eps)
    unit = hidden * factor
    n1_head[at.h] = jnp.sum(own_normed * unit, axis=0, keepdims=True)
    n1_copies = [
        remote(n1_head.at[at.h], n1_head.at[at.h], n_sems.at[0, k], n_sems.at[1, k], at.in_head(at.head_peer(k)))
        for k in range(1, nh)
    ]
    for c in n1_copies:
        c.start()
    weighted = own_normed * w_norm1[...]
    grad_in[...] = d_middle[...] + factor * (
        weighted - unit * jnp.mean(unit * weighted, axis=-1, keepdims=True)
    )
    for c in n1_copies:
        c.wait_recv()
    n1_blk[at.b] = sum_slots(n1_head, nh)
    n1_blk_copies = [
        remote(n1_blk.at[at.b], n1_blk.at[at.b], n_sems.at[0, nh + k], n_sems.at[1, nh + k], at.in_blk(at.blk_peer(k)))
        for k in range(1, nb)
    ]
    for c in n1_blk_copies:
        c.start()
    grad_w[...] = w_part[at.b] + w_scatter.from_sibling(at.z)

    def add_w(value, from_left):
        grad_w[...] += value

    w_scatter.take(add_w)
    grad_q[...] = grad_w[:qw].T
    grad_k[...] = grad_w[qw : qw + kw].T
    grad_v[...] = grad_w[qw + kw : width].T
    grad_o[...] = grad_w[width:]

    for c in n1_blk_copies:
        c.wait_recv()
    grad_n1[...] = sum_slots(n1_blk, nb)
    totals.end(2)
    output[...] = (middle[...] + gathered_part(mix_scatter)).astype(BF)
    totals.finish()
    scatter.finish()
    mix_scatter.finish()

    def drain(z):
        for k in range(1, nh):
            go(d_rows, back_rows, ret_sems, z, k).wait_send()
            go(d_gate_rows, in_dgate, dgate_sems, z, k).wait_send()
            go(scaled, back_rows, eout_sems, z, k).wait_send()

    far_first(drain)
    deal.end()
    for k in range(1, nb):
        dg_copy(at.blk_peer(k)).wait_send()
    w_scatter.finish()
    for c in d_copies + o_copies + n1_copies + n1_blk_copies:
        c.wait_send()


def back(nb, nh, hl, kl, repeat, *operands):
    rows = operands[0].shape[0]
    group, half = rows * nh, rows * nh // 2
    nz, dl = nb // 2, MODEL_WIDTH // nb
    qw, kw = hl * HEAD_SIZE, kl * HEAD_SIZE
    width = qw + 2 * kw
    shape = jax.ShapeDtypeStruct
    dma = pltpu.SemaphoreType.DMA
    chunk = (E + 8, MODEL_WIDTH // nh)
    line = (nz, nh, 1, 2 * CAP)
    return pl.pallas_call(
        functools.partial(back_kernel, nb, nh, hl, kl, repeat),
        out_shape=(
            shape((rows, MODEL_WIDTH), BF),
            shape((rows, MODEL_WIDTH), F32),
            shape((dl, qw), F32),
            shape((dl, kw), F32),
            shape((dl, kw), F32),
            shape((qw, dl), F32),
            shape((1, MODEL_WIDTH), F32),
            shape((nh,) + chunk, F32),
            *(shape(v.shape, BF) for v in operands[-3:]),
        ),
        in_specs=[VMEM] * 10 + [ANY] * 4 + [ANY, VMEM, ANY] + [VMEM, SMEM] + [ANY] * 5,
        out_specs=[VMEM] * 8 + [ANY] * 3,
        scratch_shapes=[
            pltpu.VMEM((nh, rows, MODEL_WIDTH), BF),
            pltpu.VMEM((group, group), BF),
            pltpu.VMEM((nh, rows, width), BF),
            pltpu.VMEM((2, qw, half), BF),
            pltpu.VMEM((2, max(hl, 8), half), F32),
            pltpu.VMEM((2, qw, half), F32),
            pltpu.VMEM((2, 2 * kw, half), F32),
            pltpu.VMEM((4, nz + 1, 2 * kw, half), BF),
            pltpu.VMEM((nb, width + qw, dl), F32),
            pltpu.VMEM((4, nz + 1, width + qw, dl), BF),
            pltpu.VMEM((nh, rows, MODEL_WIDTH), BF),
            pltpu.VMEM((nh, rows, MODEL_WIDTH), BF),
            pltpu.VMEM((nh, 1, MODEL_WIDTH), F32),
            pltpu.VMEM((nb, 1, MODEL_WIDTH), F32),
            pltpu.VMEM((nh,) + chunk, F32),
            pltpu.VMEM((nb,) + chunk, F32),
            dma((2, nh)),
            dma((4, nz + 1)),
            dma((4, nz + 1)),
            dma((2, nh)),
            dma((2, nh + nb)),
            dma((2, 3, max(nh, nb))),
            pltpu.VMEM((nh,) + chunk, F32),
            pltpu.VMEM((nz, nh, 2 * CAP, MODEL_WIDTH), BF),
            pltpu.VMEM(line, F32),
            pltpu.VMEM((3, rows, MODEL_WIDTH), F32),
            pltpu.VMEM((rows, MODEL_WIDTH), F32),
            pltpu.VMEM((nb, nh, rows), F32),
            pltpu.VMEM((nb, nh, rows), F32),
            pltpu.VMEM((4, nz + 1, rows, MODEL_WIDTH), BF),
            dma((4, nz + 1)),
            dma((4, nz + 1)),
            dma((2, nz, nh)),
            dma((2, nz, nh)),
            dma((2, nz, nh)),
            dma((2, nb)),
            dma((2, nz)),
            dma((2, 3, nb)),
            dma((3,)),
            pltpu.VMEM((2, 1, half), jnp.int32),
            pltpu.VMEM((width + qw, dl), F32),
            *(pltpu.VMEM(operands[i].shape, operands[i].dtype) for i in (10, 11, 12, 13, 14, 16)),
            dma((6,)),
        ],
        compiler_params=pltpu.CompilerParams(collective_id=2, vmem_limit_bytes=62 * 2**20),
        name="back",
    )(*operands)


def on_device(
    inputs,
    token_place,
    lengths,
    w_norm1,
    w_query,
    key_weight,
    value_weight,
    w_out,
    w_norm2,
    router,
    routes,
    slot_order,
    w_gate,
    w_up,
    w_down,
    grad_out,
):
    rows = inputs.shape[0]
    nb, nh = lax.axis_size("blk"), lax.axis_size("head")
    nz = nb // 2
    hl = w_query.shape[1] // HEAD_SIZE
    kl = key_weight.shape[1] // HEAD_SIZE
    local, dl, hidden_units = w_gate.shape
    repeat = nb // local
    fr = hidden_units // repeat
    qw, kw = hl * HEAD_SIZE, kl * HEAD_SIZE

    w_own = jnp.concatenate([w_query, key_weight, value_weight, w_out.T], axis=1)
    places = token_place.reshape(nb, 1, rows * nh)
    gain_one, gain_two = w_norm1.reshape(1, -1), w_norm2.reshape(1, -1)
    sizes = (nb, nh, hl, kl, repeat)
    router_t = router.T.reshape(nh, local, MODEL_WIDTH).transpose(1, 0, 2).reshape(E, MODEL_WIDTH)
    (
        gathered,
        weights,
        turned_q,
        kv,
        lse,
        attn_t,
        ao_t,
        middle,
        normed_two,
        slots,
        own_gates,
        in_gate,
        in_rows,
        in_g,
        *projections,
    ) = front(
        *sizes,
        inputs,
        gain_one,
        gain_two,
        w_own,
        places,
        lengths,
        grad_out,
        slot_table(nb, nh, repeat, routes, slot_order),
        router_t,
        w_gate,
        w_up,
        w_down,
    )
    d_rows, scaled, d_gate_rows, *sums = experts(nz, nh, in_rows, in_g, in_gate, *projections)
    output, grad_inputs, grad_q, grad_k, grad_v, grad_o, grad_norm1, small, *sums = back(
        *sizes,
        inputs,
        gain_one,
        gain_two,
        middle,
        normed_two,
        grad_out,
        router_t,
        slots,
        own_gates,
        d_gate_rows,
        weights,
        gathered,
        ao_t,
        turned_q,
        kv,
        lse,
        attn_t,
        places,
        lengths,
        d_rows,
        scaled,
        *sums,
    )

    small = small.transpose(1, 0, 2).reshape(E + 8, MODEL_WIDTH)
    grad_router = (
        small[:E].reshape(local, nh, MODEL_WIDTH).transpose(1, 0, 2).reshape(E, MODEL_WIDTH).T
    )

    def whole_part(v, axis):
        v = v.reshape((local, repeat) + v.shape[1:])
        v = v if repeat == 1 else jnp.moveaxis(v, 1, axis)
        return v.reshape((local, dl, hidden_units) if axis == 2 else (local, hidden_units, dl)).astype(F32)

    return (
        output,
        grad_inputs,
        grad_norm1.reshape(-1),
        grad_q,
        grad_k,
        grad_v,
        grad_o,
        small[E],
        grad_router,
        whole_part(sums[0], 2),
        whole_part(sums[1], 2),
        whole_part(sums[2], 1),
    )


def solution(mesh):
    rows, whole = P(("blk", "head"), None), P()
    pair, out = P("blk", "head"), P("head", "blk")
    first, last = P("head", "blk", None), P("head", None, "blk")
    return jax.shard_map(
        on_device,
        mesh=mesh,
        in_specs=(
            rows,
            whole,
            whole,
            whole,
            pair,
            pair,
            pair,
            out,
            whole,
            whole,
            rows,
            rows,
            first,
            first,
            last,
            rows,
        ),
        out_specs=(
            rows,
            rows,
            whole,
            pair,
            pair,
            pair,
            out,
            whole,
            whole,
            first,
            first,
            last,
        ),
        check_vma=False,
    )
```
